32 devices in a mesh: dp: 8 (over y, x, core), tensor: 4 (over z).
Axes of the slice: x: 2, y: 2, z: 4, core: 2. Of those that a mesh axis runs over, the one named last changes fastest.
Arguments:
- x_rows: bfloat16 [64, 128, 3072], P('dp', 'tensor'), may hold values from -6 to 6
- g_rows: bfloat16 [64, 128, 3072], P('dp', 'tensor'), may hold values from -1.5 to 1.5
- w_up: bfloat16 [3072, 12288], P(None, 'tensor'), may hold values from -0.109375 to 0.109375
- w_down_t: bfloat16 [3072, 12288], P(None, 'tensor'), may hold values from -0.0546875 to 0.0546875
- block_count: int32 [8], replicated, may hold values from 1 to 8, 32 in all
- patches: int32 [8, 8], replicated, may hold values from 64 to 128, as said below
Outputs:
- input_grad: bfloat16 [32, 128, 3072], P('dp', 'tensor')
- up_grad: bfloat16 [3072, 12288], P('dp', 'tensor')
- down_grad_t: bfloat16 [3072, 12288], P('dp', 'tensor')
The draws below stay inside these ranges and needn't reach their ends.
Inputs may be any that keep to these rules, and one draw needn't show every extreme that they name: `block_count`: the counts sum to 32; the largest is exactly 8. `patches`: in each source at least one block is full.
All inputs are finite; a program needn't handle non-finite values.
Results may differ from the reference program's by a relative error of at most 0.023.
Values may be sent and summed in bfloat16 or wider, within the bound.
No kernel may reach another device: no remote copies, remote signals or barrier semaphores. Data moves between devices by JAX's collectives and lax.ppermute only.
A program may use at most 192 MiB of HBM per device.

```python
import math
import jax
import jax.numpy as jnp
import numpy as np
from jax import lax

D = 3072
FF = 12288
BLK = 128
NB = 8
OWNB = 4
FT = 3072
SRC_BLOCKS = 64
N_DP = 8
N_TENSOR = 4


def draw_patches(key, part):
    first_key, second_key = jax.random.split(key)
    padding = jax.random.randint(first_key, (N_DP, NB), 0, BLK // 2 + 1)
    full_block = jax.random.randint(second_key, (N_DP, 1), 0, NB)
    padding = jnp.where(jnp.arange(NB)[None, :] == full_block, 0, padding)
    return (BLK - padding).astype(jnp.int32)


def level_of(own_key, shape, cuts, least, top_value):
    gain = 1.0
    for dim, blocks in cuts:
        steps = jax.random.uniform(jax.random.fold_in(jax.random.fold_in(own_key, 6), dim), (blocks,), jnp.float32, least / len(cuts), top_value / len(cuts))
        gain = gain * jnp.repeat(jnp.exp(steps), shape[dim] // blocks).reshape((-1,) + (1,) * (len(shape) - 1 - dim))
    return gain


def split_up(amount, total, reach, lean):
    weights = [(1 << 20) // math.isqrt(rank ** lean) + 1 for rank in range(2, amount + 1)]
    spare, given = total - reach - (amount - 1), [1] * (amount - 1)
    while spare > 0:
        movable = [i for i in range(amount - 1) if given[i] < reach]
        pool, left = sum([weights[i] for i in movable]), spare
        for i in movable:
            extra = min(reach - given[i], max(1, left * weights[i] // pool), spare)
            given[i] = given[i] + extra
            spare = spare - extra
    return np.array([reach] + given)


def ragged(stream_key, amount, total, limit, skew):
    if amount == 2:
        one = jax.random.randint(stream_key, (), max(1, total - limit), min(limit, total - 1) + 1)
        return jnp.stack([one, total - one])
    sizes = jnp.asarray(split_up(amount, total, limit, skew), jnp.int32)
    couples = (amount - 1) // 2
    giver, taker = sizes[1:1 + 2 * couples:2], sizes[2:2 + 2 * couples:2]
    slack = jnp.minimum(giver - 1, limit - taker)
    passed = jax.random.randint(jax.random.fold_in(stream_key, 1), (couples,), 0, 1 << 20) % (slack + 1)
    sizes = sizes.at[1:1 + 2 * couples:2].set(giver - passed).at[2:2 + 2 * couples:2].set(taker + passed)
    return sizes[jax.random.permutation(jax.random.fold_in(stream_key, 2), amount)]


def bell_draw(key, extent, spread, limit, shards=(), held_as=jnp.bfloat16):
    values = spread * jax.random.normal(key, extent, jnp.float32)
    if shards:
        values = values * level_of(key, extent, shards, -0.22, 0.18)
    return jnp.clip(values, -limit, limit).astype(held_as)


def setup_inputs(seed: int = 0) -> dict:
    key_list = jax.random.split(jax.random.key(seed), 7)
    x_rows = bell_draw(key_list[0], (SRC_BLOCKS, BLK, D), 1.0, 6.0, ((0, 8), (1, 4)))
    g_rows = bell_draw(key_list[1], (SRC_BLOCKS, BLK, D), 0.25, 1.5, ((0, 8), (1, 4)))
    w_up = bell_draw(key_list[2], (D, FF), D ** -0.5, 0.109375, ((1, 4),))
    w_down_t = bell_draw(key_list[3], (D, FF), FF ** -0.5, 0.0546875, ((1, 4),))
    block_count = ragged(key_list[4], N_DP, OWNB * N_DP, NB, 2).astype(jnp.int32)
    patches = draw_patches(jax.random.fold_in(key_list[6], 71), 0)
    return dict(x_rows=x_rows, g_rows=g_rows, w_up=w_up, w_down_t=w_down_t, block_count=block_count, patches=patches)


def gelu_pair(pre_act):
    normal_cdf = 0.5 * (1.0 + lax.erf(pre_act * 0.7071067811865476))
    density = jnp.exp(-0.5 * pre_act * pre_act) * 0.3989422804014327
    return pre_act * normal_cdf, normal_cdf + pre_act * density


def owner_order(block_count, patches):
    counts = block_count.astype(jnp.int32)
    starts = (jnp.cumsum(counts) - counts).astype(jnp.int32)
    block_ends = starts + counts
    targets = jnp.arange(N_DP * OWNB, dtype=jnp.int32)
    global_number = (targets // OWNB + N_DP * (targets % OWNB)).astype(jnp.int32)
    source = jnp.sum((block_ends[None, :] <= global_number[:, None]).astype(jnp.int32), axis=1).astype(jnp.int32)
    inner = (global_number - starts[source]).astype(jnp.int32)
    filled = patches[source, inner].astype(jnp.int32)
    row_keep = jnp.arange(BLK, dtype=jnp.int32)[None, :] < filled[:, None]
    return (source * NB + inner).astype(jnp.int32), row_keep


def reference(x_rows, g_rows, w_up, w_down_t, block_count, patches):
    block_index, row_keep = owner_order(block_count, patches)
    owner_x = jnp.where(row_keep[:, :, None], x_rows[block_index], jnp.zeros((), x_rows.dtype))
    owner_g = jnp.where(row_keep[:, :, None], g_rows[block_index], jnp.zeros((), g_rows.dtype))
    flat_x = owner_x.reshape(-1, D)
    flat_g = owner_g.reshape(-1, D)
    pre_act = jnp.dot(flat_x, w_up, preferred_element_type=jnp.float32)
    gelu_value, gelu_slope = gelu_pair(pre_act)
    activation = gelu_value.astype(jnp.bfloat16)
    act_grad = jnp.dot(flat_g, w_down_t, preferred_element_type=jnp.float32)
    pre_grad = (act_grad * gelu_slope).astype(jnp.bfloat16)
    input_sum = jnp.zeros((flat_x.shape[0], D), jnp.float32)
    for tensor_shard in range(N_TENSOR):
        hidden_cols = slice(tensor_shard * FT, (tensor_shard + 1) * FT)
        partial_value = lax.dot_general(pre_grad[:, hidden_cols], w_up[:, hidden_cols], (((1,), (1,)), ((), ())), preferred_element_type=jnp.float32)
        partial_value = lax.optimization_barrier(partial_value.astype(jnp.bfloat16))
        input_sum = input_sum + partial_value.astype(jnp.float32)
    input_grad = input_sum.astype(jnp.bfloat16).reshape(N_DP * OWNB, BLK, D)
    up_grad = lax.dot_general(flat_x, pre_grad, (((0,), (0,)), ((), ())), preferred_element_type=jnp.float32).astype(jnp.bfloat16)
    down_grad_t = lax.dot_general(flat_g, activation, (((0,), (0,)), ((), ())), preferred_element_type=jnp.float32).astype(jnp.bfloat16)
    return input_grad, up_grad, down_grad_t
```

```python
import functools

import jax
import jax.numpy as jnp
from jax import lax
from jax.experimental import pallas as pl
from jax.experimental.pallas import tpu as pltpu
from jax.sharding import PartitionSpec as P

OWNB = 4
BF16 = jnp.bfloat16
F32 = jnp.float32
VMEM_LIMIT = 60 * 1024 * 1024
SHORT = pl.CostEstimate(flops=1, bytes_accessed=1, transcendentals=0)


def chip_with(j, v, core):
    return jnp.where(core == 0, 2 * j + v, ((j >> 1) << 2) + 2 * v + (j & 1))


def pool_bit(chip, core):
    return jnp.where(core == 0, chip & 1, (chip >> 1) & 1)


def other_bits(chip, core):
    return jnp.where(core == 0, chip >> 1, ((chip >> 2) << 1) + (chip & 1))


def chip_perm(dp, flip, cross=False):
    return [(i, 2 * ((i >> 1) ^ flip(i & 1)) + ((i & 1) ^ int(cross))) for i in range(dp)]


def start_of(count, source, dp):
    total = jnp.int32(0)
    for j in range(dp):
        total = total + jnp.where(source > j, count[j], 0)
    return total


def source_of(count, number, dp):
    end, source = jnp.int32(0), jnp.int32(0)
    for j in range(dp):
        end = end + count[j]
        source = source + jnp.where(end <= number, 1, 0)
    return source


def pack_body(info, count, x, g, x_out, g_out, sems):
    dp, blocks = x_out.shape[0], x.shape[0]
    start = start_of(count, info[0], dp)
    copies = []
    for t, (rows, out) in enumerate(((x, x_out), (g, g_out))):
        for k in range(dp):
            block = jnp.minimum(lax.rem(k + OWNB * dp - start, dp), blocks - 1)
            copies.append(pltpu.make_async_copy(rows.at[block], out.at[k], sems.at[t, k]))
    for copy in copies:
        copy.start()
    for copy in copies:
        copy.wait()


def pack(x_rows, g_rows, info, count, dp):
    _, here, d = x_rows.shape
    shape = jax.ShapeDtypeStruct((dp, here, d), BF16)
    any_spec = pl.BlockSpec(memory_space=pl.ANY)
    return pl.pallas_call(
        pack_body,
        out_shape=(shape, shape),
        grid_spec=pltpu.PrefetchScalarGridSpec(
            num_scalar_prefetch=2,
            in_specs=[any_spec, any_spec],
            out_specs=(any_spec, any_spec),
            scratch_shapes=[pltpu.SemaphoreType.DMA((2, dp))],
        ),
        compiler_params=pltpu.CompilerParams(vmem_limit_bytes=VMEM_LIMIT),
        cost_estimate=SHORT,
    )(info, count, x_rows, g_rows)


def select_body(info, count, patches, rows, out, *, dp):
    number = info[0] + dp * pl.program_id(0)
    source = source_of(count, number, dp)
    filled = patches[source, number - start_of(count, source, dp)]
    here = rows.shape[1]
    row = lax.broadcasted_iota(jnp.int32, rows.shape, 1) + info[1] * here
    out[...] = jnp.where(row < filled, rows[...].astype(F32), 0.0).astype(out.dtype)


def select(arrived, info, count, patches):
    dp, here, d = arrived.shape
    return pl.pallas_call(
        functools.partial(select_body, dp=dp),
        out_shape=jax.ShapeDtypeStruct((OWNB, here, d), arrived.dtype),
        grid_spec=pltpu.PrefetchScalarGridSpec(
            num_scalar_prefetch=3,
            grid=(OWNB,),
            in_specs=[pl.BlockSpec((1, here, d), lambda m, i, n, p: (source_of(n, i[0] + dp * m, dp), 0, 0))],
            out_specs=pl.BlockSpec((1, here, d), lambda m, i, n, p: (m, 0, 0)),
        ),
        compiler_params=pltpu.CompilerParams(vmem_limit_bytes=VMEM_LIMIT),
        cost_estimate=SHORT,
    )(info, count, patches, arrived)


def block_of(size, most):
    for width in range(most, 0, -128):
        if size % width == 0:
            return width
    return size


def load_rows(own, sib, rows):
    half = own.shape[0]
    rows[:half] = own[...]
    rows[half:] = sib[...]


def put_partner_columns(info, rows, out, hidden, chips):
    core, chip = info[0] & 1, info[0] >> 1
    width = rows.shape[1] // chips
    away = 1 - pool_bit(chip, core)
    for j in range(chips // 2):
        at = pl.multiple_of(chip_with(j, away, core) * width, 128)
        out[:, hidden + j * width:hidden + (j + 1) * width] = rows[:, pl.ds(at, width)]


def up_body(info, own, sib, w, out, slope, rows, *, hidden, chips):
    n = pl.program_id(0)

    @pl.when(n == 0)
    def _():
        load_rows(own, sib, rows)
        put_partner_columns(info, rows, out, hidden, chips)

    pre_act = jnp.dot(rows[...], w[...], preferred_element_type=F32)
    cdf = 0.5 * (1.0 + lax.erf(pre_act * 0.7071067811865476))
    density = jnp.exp(-0.5 * pre_act * pre_act) * 0.3989422804014327
    width = w.shape[1]
    out[:, pl.ds(pl.multiple_of(n * width, 128), width)] = (pre_act * cdf).astype(out.dtype)
    slope[...] = (cdf + pre_act * density).astype(slope.dtype)


def down_body(info, own, sib, w, slope, out, rows, *, hidden, chips):
    n = pl.program_id(0)

    @pl.when(n == 0)
    def _():
        load_rows(own, sib, rows)
        if out.shape[1] > hidden:
            put_partner_columns(info, rows, out, hidden, chips)

    act_grad = jnp.dot(rows[...], w[...], preferred_element_type=F32)
    width = w.shape[1]
    out[:, pl.ds(pl.multiple_of(n * width, 128), width)] = (act_grad * slope[...]).astype(out.dtype)


def columns_body(info, own, sib, out, rows, *, chips):
    load_rows(own, sib, rows)
    put_partner_columns(info, rows, out, 0, chips)


def partner_columns(own, sib, info, chips):
    half, d = own.shape
    spec = pl.BlockSpec((half, d), lambda n, i: (0, 0))
    return pl.pallas_call(
        functools.partial(columns_body, chips=chips),
        out_shape=jax.ShapeDtypeStruct((2 * half, d // 2), BF16),
        grid_spec=pltpu.PrefetchScalarGridSpec(
            num_scalar_prefetch=1,
            grid=(1,),
            in_specs=[spec, spec],
            out_specs=pl.BlockSpec((2 * half, d // 2), lambda n, i: (0, 0)),
            scratch_shapes=[pltpu.VMEM((2 * half, d), BF16)],
        ),
        compiler_params=pltpu.CompilerParams(vmem_limit_bytes=VMEM_LIMIT),
        cost_estimate=SHORT,
    )(info, own, sib)


def forward(own, sib, w, info, chips, slope=None, with_columns=True):
    half, d = own.shape
    hidden = w.shape[1] // 2
    width = block_of(hidden, 768)
    steps = hidden // width
    across = hidden + (d // 2 if with_columns else 0)
    out_shape = jax.ShapeDtypeStruct((2 * half, across), BF16)
    out_spec = pl.BlockSpec((2 * half, across), lambda n, i: (0, 0))
    slope_spec = pl.BlockSpec((2 * half, width), lambda n, i: (0, n))
    rows_spec = pl.BlockSpec((half, d), lambda n, i: (0, 0))
    w_spec = pl.BlockSpec((d, width), lambda n, i: (0, (i[0] & 1) * steps + n))
    in_specs = [rows_spec, rows_spec, w_spec]
    operands = [own, sib, w]
    if slope is None:
        body = up_body
        out_shape = (out_shape, jax.ShapeDtypeStruct((2 * half, hidden), BF16))
        out_specs = (out_spec, slope_spec)
    else:
        body = down_body
        out_specs = out_spec
        in_specs.append(slope_spec)
        operands.append(slope)
    return pl.pallas_call(
        functools.partial(body, hidden=hidden, chips=chips),
        out_shape=out_shape,
        grid_spec=pltpu.PrefetchScalarGridSpec(
            num_scalar_prefetch=1,
            grid=(steps,),
            in_specs=in_specs,
            out_specs=out_specs,
            scratch_shapes=[pltpu.VMEM((2 * half, d), BF16)],
        ),
        compiler_params=pltpu.CompilerParams(vmem_limit_bytes=VMEM_LIMIT),
        cost_estimate=SHORT,
    )(info, *operands)


def input_body(info, pre, w, own, sib):
    value = lax.dot_general(pre[...], w[...], (((1,), (1,)), ((), ())), preferred_element_type=F32)
    half = own.shape[0]
    own[...] = value[:half].astype(own.dtype)
    sib[...] = value[half:].astype(sib.dtype)


def input_part(pre, w, info):
    rows = pre.shape[0]
    d, hidden = w.shape[0], w.shape[1] // 2
    width = block_of(d, 768)
    shape = jax.ShapeDtypeStruct((rows // 2, d), BF16)
    spec = pl.BlockSpec((rows // 2, width), lambda n, i: (0, n))
    return pl.pallas_call(
        input_body,
        out_shape=(shape, shape),
        grid_spec=pltpu.PrefetchScalarGridSpec(
            num_scalar_prefetch=1,
            grid=(d // width,),
            in_specs=[
                pl.BlockSpec((rows, hidden), lambda n, i: (0, 0)),
                pl.BlockSpec((width, hidden), lambda n, i: (n, i[0] & 1)),
            ],
            out_specs=(spec, spec),
        ),
        compiler_params=pltpu.CompilerParams(vmem_limit_bytes=VMEM_LIMIT),
        cost_estimate=SHORT,
    )(info, pre, w)


def weight_body(at, *refs, slots):
    ins, (straight, crossed) = refs[:5 * slots], refs[5 * slots:]
    total = None
    dims = (((0,), (0,)), ((), ()))
    for s in range(slots):
        own, sib, there, mine, theirs = ins[5 * s:5 * s + 5]
        half = own.shape[0]
        for left, right in ((own[...], mine[:half]), (sib[...], mine[half:]), (there[...], theirs[...])):
            term = lax.dot_general(left, right, dims, preferred_element_type=F32)
            total = term if total is None else total + term
    span = straight.shape[0]
    low, high = total[:span], total[span:]
    first = at[2] == 0
    straight[...] = jnp.where(first, low, high).astype(straight.dtype)
    crossed[...] = jnp.where(first, high, low).astype(crossed.dtype)


def weight_part(rows, there_rows, rights, own_at, there_at, core, width, hidden):
    slots = len(rows)
    at = jnp.stack([own_at, there_at, core]).astype(jnp.int32)
    block = block_of(hidden, 512)
    operands, specs = [], []
    for (own, sib), (there, begin), (mine, theirs) in zip(rows, there_rows, rights):
        half = own.shape[0]
        operands += [own, sib, there, mine, theirs]
        specs += [
            pl.BlockSpec((half, width), lambda n, a: (0, a[0])),
            pl.BlockSpec((half, width), lambda n, a: (0, a[0])),
            pl.BlockSpec((2 * half, width), lambda n, a, first=begin // width: (0, first + a[1])),
            pl.BlockSpec((2 * half, block), lambda n, a: (0, n)),
            pl.BlockSpec((2 * half, block), lambda n, a: (0, n)),
        ]
    total = 4 * half * slots
    shape = jax.ShapeDtypeStruct((width // 2, hidden), BF16)
    spec = pl.BlockSpec((width // 2, block), lambda n, a: (0, n))
    return pl.pallas_call(
        functools.partial(weight_body, slots=slots),
        out_shape=(shape, shape),
        grid_spec=pltpu.PrefetchScalarGridSpec(
            num_scalar_prefetch=1,
            grid=(hidden // block,),
            in_specs=specs,
            out_specs=(spec, spec),
        ),
        compiler_params=pltpu.CompilerParams(vmem_limit_bytes=VMEM_LIMIT),
        cost_estimate=SHORT,
    )(at, *operands)


def add(*values):
    return sum(v.astype(F32) for v in values).astype(BF16)


def local(x_rows, g_rows, w_up, w_down_t, block_count, patches):
    dp, tensor = lax.axis_size("dp"), lax.axis_size("tensor")
    chips = dp // 2
    me, plane = lax.axis_index("dp"), lax.axis_index("tensor")
    chip, core = me >> 1, me & 1
    info = jnp.stack([me, plane]).astype(jnp.int32)
    here, d = x_rows.shape[1:]
    hidden = w_up.shape[1] // 2
    ring = [(i, (i + 1) % tensor) for i in range(tensor)]
    to_sibling = [(i, i ^ 1) for i in range(dp)]
    to_pool = chip_perm(dp, lambda c: 1 << c)
    last = []

    def after(*values):
        out = lax.optimization_barrier((*values, *last))[:len(values)]
        return out if len(out) > 1 else out[0]

    def done(value):
        last[:] = [value]
        return value

    def exchange(rows):
        return lax.all_to_all(rows, "dp", split_axis=0, concat_axis=0, tiled=True)

    def onward(piece):
        return lax.ppermute(piece, "tensor", ring)

    def sibling(piece):
        return lax.ppermute(piece, "dp", to_sibling)

    def pooled(piece):
        return lax.ppermute(piece, "dp", to_pool)

    def chosen(arrived):
        return done(select(after(arrived), info, block_count, patches)).reshape(OWNB * here, d)

    send_x, send_g = pack(x_rows, g_rows, info, block_count, dp)
    arrived_x = done(exchange(send_x))
    arrived_g = exchange(after(send_g))
    x_own = [chosen(arrived_x)]
    x_sib, g_own, g_sib = [sibling(x_own[0])], [], []
    x_ahead = onward(x_own[0])
    act, slope, pre, shares = [], [], [], []

    def up(s):
        mine, slope_s = forward(*after(x_own[s], x_sib[s]), w_up, info, chips)
        slope.append(slope_s)
        act.append((mine, pooled(done(mine))))

    def down(s, with_columns=True):
        mine = done(forward(*after(g_own[s], g_sib[s]), w_down_t, info, chips, slope[s], with_columns))
        pre.append((mine, pooled(mine)))

    def share(s):
        own, sib = input_part(after(pre[s][0]), w_up, info)
        shares.append((own, sibling(done(sib))))

    def arrive(own, sib, ahead, further=True):
        piece = after(ahead)
        own.append(piece)
        sib.append(sibling(piece))
        return onward(piece) if further else None

    def settle(pairs, s):
        if 0 <= s < len(pairs):
            last.append(pairs[s][1])

    up(0)
    for s in range(1, tensor):
        x_ahead = arrive(x_own, x_sib, x_ahead, s + 1 < tensor)
        if s == tensor - 1:
            g_ahead = onward(after(g_own[0]))
        settle(act, s - 2)
        up(s)
        if s == 1:
            g_own.append(chosen(arrived_g))
            g_sib.append(sibling(g_own[0]))
        if s == 2:
            settle(act, 1)
            down(0)
    settle(act, tensor - 2)
    share(0)
    g_last = None
    for s in range(1, tensor):
        g_ahead = arrive(g_own, g_sib, g_ahead, s + 1 < tensor)
        if s == tensor - 1:
            running = onward(add(*after(*shares[1])))
            g_last = partner_columns(*after(g_own[s], g_sib[s]), info, chips)
            g_last = pooled(done(g_last))
        settle(pre, s - 2 if s > 2 else -1)
        down(s, s < tensor - 1)
        settle(pre if s == 1 else act, 0 if s == 1 else tensor - 1 if s == 2 else -1)
        share(s)

    span = d // dp
    near, mine_j = pool_bit(chip, core), other_bits(chip, core)
    g_there = [(theirs, hidden) for _, theirs in pre[:-1]] + [(g_last, 0)]
    x_there = [(theirs, hidden) for _, theirs in act]
    sums = {"down": (list(zip(g_own, g_sib)), g_there, act), "up": (list(zip(x_own, x_sib)), x_there, pre)}

    def part(key, r):
        j = mine_j ^ r
        at = chip_with(j, near, core)
        straight, crossed = weight_part(*sums[key], at, j, core, 2 * span, hidden)
        return [straight, crossed]

    bits = (chips // 2).bit_length() - 1
    halves = {key: {} for key in sums}
    for key in sums:
        for r in reversed(range(1, chips // 2)):
            halves[key][r] = part(key, r)
    for s in range(2, tensor):
        running = onward(add(*shares[s], running))
    input_grad = add(*shares[0], running).reshape(OWNB, here, d)
    for key in sums:
        halves[key][0] = part(key, 0)

    def finished(parts):
        for k in reversed(range(1, bits)):
            perm = chip_perm(dp, lambda c: 2 << k)
            for r in range(1 << k, 2 << k):
                for h in range(2):
                    parts[r ^ (1 << k)][h] = add(parts[r ^ (1 << k)][h], lax.ppermute(parts[r][h], "dp", perm))
        flip = lambda c: 2 >> c
        straight = lax.ppermute(parts[1][0], "dp", chip_perm(dp, flip))
        crossed = lax.ppermute(parts[1][1], "dp", chip_perm(dp, flip, True))
        mine = add(parts[0][0], straight)
        other = add(sibling(parts[0][1]), crossed)
        return jnp.where(
            core == 0, jnp.concatenate([mine, other], axis=1), jnp.concatenate([other, mine], axis=1)
        )

    down_grad = finished(halves["down"])
    up_grad = finished(halves["up"])
    return input_grad, up_grad, down_grad


def solution(mesh):
    placed = (
        P("dp", "tensor", None),
        P("dp", "tensor", None),
        P(None, "tensor"),
        P(None, "tensor"),
        P(),
        P(),
    )
    return jax.shard_map(
        local,
        mesh=mesh,
        in_specs=placed,
        out_specs=(P("dp", "tensor", None), P("dp", "tensor"), P("dp", "tensor")),
        check_vma=False,
    )
```

```python
import functools

import jax
import jax.numpy as jnp
from jax import lax
from jax.experimental import pallas as pl
from jax.experimental.pallas import tpu as pltpu
from jax.sharding import PartitionSpec as P

OWNB = 4
BF16 = jnp.bfloat16
F32 = jnp.float32
VMEM_LIMIT = 60 * 1024 * 1024
SHORT = pl.CostEstimate(flops=1, bytes_accessed=1, transcendentals=0)


def chip_with(j, v, core):
    return jnp.where(core == 0, 2 * j + v, ((j >> 1) << 2) + 2 * v + (j & 1))


def pool_bit(chip, core):
    return jnp.where(core == 0, chip & 1, (chip >> 1) & 1)


def other_bits(chip, core):
    return jnp.where(core == 0, chip >> 1, ((chip >> 2) << 1) + (chip & 1))


def chip_perm(dp, flip, cross=False):
    return [(i, 2 * ((i >> 1) ^ flip(i & 1)) + ((i & 1) ^ int(cross))) for i in range(dp)]


def start_of(count, source, dp):
    total = jnp.int32(0)
    for j in range(dp):
        total = total + jnp.where(source > j, count[j], 0)
    return total


def source_of(count, number, dp):
    end, source = jnp.int32(0), jnp.int32(0)
    for j in range(dp):
        end = end + count[j]
        source = source + jnp.where(end <= number, 1, 0)
    return source


def pack_body(info, count, rows, out, sems):
    dp, blocks = out.shape[0], rows.shape[0]
    start = start_of(count, info[0], dp)
    copies = []
    for k in range(dp):
        block = jnp.minimum(lax.rem(k + OWNB * dp - start, dp), blocks - 1)
        copies.append(pltpu.make_async_copy(rows.at[block], out.at[k], sems.at[k]))
    for copy in copies:
        copy.start()
    for copy in copies:
        copy.wait()


def pack(rows, info, count, dp):
    _, here, d = rows.shape
    return pl.pallas_call(
        pack_body,
        out_shape=jax.ShapeDtypeStruct((dp, here, d), BF16),
        grid_spec=pltpu.PrefetchScalarGridSpec(
            num_scalar_prefetch=2,
            grid=(1,),
            in_specs=[pl.BlockSpec(memory_space=pl.ANY)],
            out_specs=pl.BlockSpec((dp, here, d), lambda n, i, c: (0, 0, 0)),
            scratch_shapes=[pltpu.SemaphoreType.DMA((dp,))],
        ),
        compiler_params=pltpu.CompilerParams(vmem_limit_bytes=VMEM_LIMIT),
        cost_estimate=SHORT,
    )(info, count, rows)


def select_body(info, count, patches, rows, out, *, dp):
    number = info[0] + dp * pl.program_id(0)
    source = source_of(count, number, dp)
    filled = patches[source, number - start_of(count, source, dp)]
    here = rows.shape[1]
    row = lax.broadcasted_iota(jnp.int32, rows.shape, 1) + info[1] * here
    out[...] = jnp.where(row < filled, rows[...].astype(F32), 0.0).astype(out.dtype)


def select(arrived, info, count, patches):
    dp, here, d = arrived.shape
    return pl.pallas_call(
        functools.partial(select_body, dp=dp),
        out_shape=jax.ShapeDtypeStruct((OWNB, here, d), arrived.dtype),
        grid_spec=pltpu.PrefetchScalarGridSpec(
            num_scalar_prefetch=3,
            grid=(OWNB,),
            in_specs=[pl.BlockSpec((1, here, d), lambda m, i, n, p: (source_of(n, i[0] + dp * m, dp), 0, 0))],
            out_specs=pl.BlockSpec((1, here, d), lambda m, i, n, p: (m, 0, 0)),
        ),
        compiler_params=pltpu.CompilerParams(vmem_limit_bytes=VMEM_LIMIT),
        cost_estimate=SHORT,
    )(info, count, patches, arrived)


def block_of(size, most):
    for width in range(most, 0, -128):
        if size % width == 0:
            return width
    return size


def load_rows(own, sib, rows):
    half = own.shape[0]
    rows[:half] = own[...]
    rows[half:] = sib[...]


def put_partner_columns(info, rows, out, hidden, chips):
    core, chip = info[0] & 1, info[0] >> 1
    width = rows.shape[1] // chips
    away = 1 - pool_bit(chip, core)
    for j in range(chips // 2):
        at = pl.multiple_of(chip_with(j, away, core) * width, 128)
        out[:, hidden + j * width:hidden + (j + 1) * width] = rows[:, pl.ds(at, width)]


def up_body(info, own, sib, w, out, rows, slope, *, hidden, chips):
    n = pl.program_id(0)

    @pl.when(n == 0)
    def _():
        load_rows(own, sib, rows)
        put_partner_columns(info, rows, out, hidden, chips)

    pre_act = jnp.dot(rows[...], w[...], preferred_element_type=F32)
    cdf = 0.5 * (1.0 + lax.erf(pre_act * 0.7071067811865476))
    density = jnp.exp(-0.5 * pre_act * pre_act) * 0.3989422804014327
    width = w.shape[1]
    out[:, pl.ds(pl.multiple_of(n * width, 128), width)] = (pre_act * cdf).astype(out.dtype)
    slope[...] = (cdf + pre_act * density).astype(slope.dtype)


def down_body(info, own, sib, w, slope, out, rows, *, hidden, chips):
    n = pl.program_id(0)

    @pl.when(n == 0)
    def _():
        load_rows(own, sib, rows)
        if out.shape[1] > hidden:
            put_partner_columns(info, rows, out, hidden, chips)

    act_grad = jnp.dot(rows[...], w[...], preferred_element_type=F32)
    width = w.shape[1]
    out[:, pl.ds(pl.multiple_of(n * width, 128), width)] = (act_grad * slope[...]).astype(out.dtype)


def columns_body(info, own, sib, out, rows, *, chips):
    load_rows(own, sib, rows)
    put_partner_columns(info, rows, out, 0, chips)


def partner_columns(own, sib, info, chips):
    half, d = own.shape
    spec = pl.BlockSpec((half, d), lambda n, i: (0, 0))
    return pl.pallas_call(
        functools.partial(columns_body, chips=chips),
        out_shape=jax.ShapeDtypeStruct((2 * half, d // 2), BF16),
        grid_spec=pltpu.PrefetchScalarGridSpec(
            num_scalar_prefetch=1,
            grid=(1,),
            in_specs=[spec, spec],
            out_specs=pl.BlockSpec((2 * half, d // 2), lambda n, i: (0, 0)),
            scratch_shapes=[pltpu.VMEM((2 * half, d), BF16)],
        ),
        compiler_params=pltpu.CompilerParams(vmem_limit_bytes=VMEM_LIMIT),
        cost_estimate=SHORT,
    )(info, own, sib)


def forward(own, sib, w, info, chips, slope=None, with_columns=True):
    half, d = own.shape
    hidden = w.shape[1] // 2
    width = block_of(hidden, 768)
    steps = hidden // width
    across = hidden + (d // 2 if with_columns else 0)
    out_shape = (jax.ShapeDtypeStruct((2 * half, across), BF16), jax.ShapeDtypeStruct((2 * half, d), BF16))
    out_specs = (
        pl.BlockSpec((2 * half, across), lambda n, i: (0, 0)),
        pl.BlockSpec((2 * half, d), lambda n, i: (0, 0)),
    )
    slope_spec = pl.BlockSpec((2 * half, width), lambda n, i: (0, n))
    rows_spec = pl.BlockSpec((half, d), lambda n, i: (0, 0))
    w_spec = pl.BlockSpec((d, width), lambda n, i: (0, (i[0] & 1) * steps + n))
    in_specs = [rows_spec, rows_spec, w_spec]
    operands = [own, sib, w]
    if slope is None:
        body = up_body
        out_shape += (jax.ShapeDtypeStruct((2 * half, hidden), BF16),)
        out_specs += (slope_spec,)
    else:
        body = down_body
        in_specs.append(slope_spec)
        operands.append(slope)
    return pl.pallas_call(
        functools.partial(body, hidden=hidden, chips=chips),
        out_shape=out_shape,
        grid_spec=pltpu.PrefetchScalarGridSpec(
            num_scalar_prefetch=1,
            grid=(steps,),
            in_specs=in_specs,
            out_specs=out_specs,
        ),
        compiler_params=pltpu.CompilerParams(vmem_limit_bytes=VMEM_LIMIT),
        cost_estimate=SHORT,
    )(info, *operands)


def input_body(info, pre, w, own, sib):
    value = lax.dot_general(pre[...], w[...], (((1,), (1,)), ((), ())), preferred_element_type=F32)
    half = own.shape[0]
    own[...] = value[:half].astype(own.dtype)
    sib[...] = value[half:].astype(sib.dtype)


def input_part(pre, w, info):
    rows = pre.shape[0]
    d, hidden = w.shape[0], w.shape[1] // 2
    width = block_of(d, 768)
    shape = jax.ShapeDtypeStruct((rows // 2, d), BF16)
    spec = pl.BlockSpec((rows // 2, width), lambda n, i: (0, n))
    return pl.pallas_call(
        input_body,
        out_shape=(shape, shape),
        grid_spec=pltpu.PrefetchScalarGridSpec(
            num_scalar_prefetch=1,
            grid=(d // width,),
            in_specs=[
                pl.BlockSpec((rows, hidden), lambda n, i: (0, 0)),
                pl.BlockSpec((width, hidden), lambda n, i: (n, i[0] & 1)),
            ],
            out_specs=(spec, spec),
        ),
        compiler_params=pltpu.CompilerParams(vmem_limit_bytes=VMEM_LIMIT),
        cost_estimate=SHORT,
    )(info, pre, w)


def weight_body(at, *refs, begins, width, block):
    slots = len(begins)
    ins, (straight, crossed, left, right, left_sems, right_sems) = refs[:4 * slots], refs[4 * slots:]
    steps, size = right.shape[0], ins[0].shape[0]
    left_copies, right_copies = [], [[] for _ in range(steps)]
    for s in range(slots):
        own, there, mine, theirs = ins[4 * s:4 * s + 4]
        columns = (at[0] * width, begins[s] + at[1] * width)
        for k, (rows, hidden_side) in enumerate(((own, mine), (there, theirs))):
            to = pl.ds((2 * s + k) * size, size)
            source = rows.at[:, pl.ds(pl.multiple_of(columns[k], 128), width)]
            left_copies.append(pltpu.make_async_copy(source, left.at[to], left_sems.at[2 * s + k]))
            for n in range(steps):
                source = hidden_side.at[:, pl.ds(n * block, block)]
                right_copies[n].append(
                    pltpu.make_async_copy(source, right.at[n, to], right_sems.at[n, 2 * s + k])
                )
    for copies in (left_copies, *right_copies):
        for copy in copies:
            copy.start()
    for copy in left_copies:
        copy.wait()
    span = width // 2
    first = at[2] == 0
    for n in range(steps):
        for copy in right_copies[n]:
            copy.wait()
        total = lax.dot_general(left[...], right[n], (((0,), (0,)), ((), ())), preferred_element_type=F32)
        low, high = total[:span], total[span:]
        straight[:, n * block:(n + 1) * block] = jnp.where(first, low, high).astype(straight.dtype)
        crossed[:, n * block:(n + 1) * block] = jnp.where(first, high, low).astype(crossed.dtype)


def weight_part(rows, there_rows, rights, own_at, there_at, core, width, hidden):
    slots, size = len(rows), rows[0].shape[0]
    at = jnp.stack([own_at, there_at, core]).astype(jnp.int32)
    block = block_of(hidden, 512)
    steps = hidden // block
    operands = []
    for own, (there, _), (mine, theirs) in zip(rows, there_rows, rights):
        operands += [own, there, mine, theirs]
    shape = jax.ShapeDtypeStruct((width // 2, hidden), BF16)
    spec = pl.BlockSpec((width // 2, hidden), lambda n, a: (0, 0))
    return pl.pallas_call(
        functools.partial(weight_body, begins=[begin for _, begin in there_rows], width=width, block=block),
        out_shape=(shape, shape),
        grid_spec=pltpu.PrefetchScalarGridSpec(
            num_scalar_prefetch=1,
            grid=(1,),
            in_specs=[pl.BlockSpec(memory_space=pl.ANY)] * len(operands),
            out_specs=(spec, spec),
            scratch_shapes=[
                pltpu.VMEM((2 * slots * size, width), BF16),
                pltpu.VMEM((steps, 2 * slots * size, block), BF16),
                pltpu.SemaphoreType.DMA((2 * slots,)),
                pltpu.SemaphoreType.DMA((steps, 2 * slots)),
            ],
        ),
        compiler_params=pltpu.CompilerParams(vmem_limit_bytes=VMEM_LIMIT),
        cost_estimate=SHORT,
    )(at, *operands)


def add(*values):
    return sum(v.astype(F32) for v in values).astype(BF16)


def local(x_rows, g_rows, w_up, w_down_t, block_count, patches):
    dp, tensor = lax.axis_size("dp"), lax.axis_size("tensor")
    chips = dp // 2
    me, plane = lax.axis_index("dp"), lax.axis_index("tensor")
    chip, core = me >> 1, me & 1
    info = jnp.stack([me, plane]).astype(jnp.int32)
    here, d = x_rows.shape[1:]
    hidden = w_up.shape[1] // 2
    ring = [(i, (i + 1) % tensor) for i in range(tensor)]
    to_sibling = [(i, i ^ 1) for i in range(dp)]
    to_pool = chip_perm(dp, lambda c: 1 << c)
    last = []

    def after(*values):
        out = lax.optimization_barrier((*values, *last))[:len(values)]
        return out if len(out) > 1 else out[0]

    def done(value):
        last[:] = [value]
        return value

    def exchange(rows):
        return lax.all_to_all(rows, "dp", split_axis=0, concat_axis=0, tiled=True)

    def onward(piece):
        return lax.ppermute(piece, "tensor", ring)

    def sibling(piece):
        return lax.ppermute(piece, "dp", to_sibling)

    def pooled(piece):
        return lax.ppermute(piece, "dp", to_pool)

    def chosen(arrived):
        return done(select(after(arrived), info, block_count, patches)).reshape(OWNB * here, d)

    def arrive(own, sib, ahead, further=True):
        piece = after(ahead)
        own.append(piece)
        sib.append(sibling(piece))
        return onward(piece) if further else None

    x_own, x_sib, x_rows_of, x_there = [], [], [], []
    g_own, g_sib, g_rows_of, g_there = [], [], [], []
    act, slope, pre, shares, pools = [], [], [], [], {}

    def settle(*names):
        last.extend(pools[name] for name in names if name in pools)

    def up(s):
        mine, rows, slope_s = forward(*after(x_own[s], x_sib[s]), w_up, info, chips)
        theirs = pools["x", s] = pooled(done(mine))
        x_rows_of.append(rows)
        x_there.append((theirs, hidden))
        slope.append(slope_s)
        act.append((mine, theirs))

    def down(s, with_columns=True):
        mine, rows = forward(*after(g_own[s], g_sib[s]), w_down_t, info, chips, slope[s], with_columns)
        theirs = pools["g", s] = pooled(done(mine))
        g_rows_of.append(rows)
        if with_columns:
            g_there.append((theirs, hidden))
        pre.append((mine, theirs))

    def share(s):
        own, sib = input_part(after(pre[s][0]), w_up, info)
        pools["share", s] = sibling(done(sib))
        shares.append((own, pools["share", s]))

    send_x = done(pack(x_rows, info, block_count, dp))
    arrived_x = exchange(send_x)
    send_g = done(pack(after(g_rows), info, block_count, dp))
    arrived_g = exchange(lax.optimization_barrier((send_g, arrived_x))[0])
    x_own.append(chosen(arrived_x))
    x_sib.append(sibling(x_own[0]))
    x_ahead = onward(x_own[0])
    up(0)
    end = tensor - 1
    for s in range(1, tensor):
        x_ahead = arrive(x_own, x_sib, x_ahead, s < end)
        if s == end:
            g_ahead = onward(after(g_own[0]))
        settle(("x", s - 2))
        up(s)
        if s == 1:
            g_own.append(chosen(arrived_g))
            g_sib.append(sibling(g_own[0]))
        if s == 2:
            settle(("x", 1))
            down(0)
    settle(("x", end - 1))
    share(0)
    for s in range(1, end):
        g_ahead = arrive(g_own, g_sib, g_ahead)
        settle(("share", s - 1), ("x", end) if s > 1 else None, ("g", s - 2))
        down(s)
        settle(("g", 0))
        share(s)

    settle(("g", end - 2))
    first_share = done(add(*after(*shares[1])))
    arrive(g_own, g_sib, g_ahead, False)
    running = onward(lax.optimization_barrier((first_share, g_own[end]))[0])
    columns = done(partner_columns(*after(g_own[end], g_sib[end]), info, chips))
    pools["columns"] = pooled(columns)
    g_there.append((pools["columns"], 0))
    settle(("g", end - 1), ("share", end - 1))
    down(end, False)
    share(end)

    span = d // dp
    near, mine_j = pool_bit(chip, core), other_bits(chip, core)

    def part(r, rows, there, rights):
        j = mine_j ^ r
        rows = [after(rows[0]), *rows[1:]]
        straight, crossed = weight_part(rows, there, rights, chip_with(j, near, core), j, core, 2 * span, hidden)
        done(straight)
        return [straight, crossed]

    bits = (chips // 2).bit_length() - 1

    def pass_on(parts):
        for k in reversed(range(1, bits)):
            perm = chip_perm(dp, lambda c: 2 << k)
            for r in range(1 << k, 2 << k):
                for h in range(2):
                    sent = lax.ppermute(parts[r][h], "dp", perm)
                    kept = parts.get(r ^ (1 << k))
                    parts[r ^ (1 << k)] = kept or [None, None]
                    parts[r ^ (1 << k)][h] = add(kept[h], sent) if kept and kept[h] is not None else sent
        flip = lambda c: 2 >> c
        straight = lax.ppermute(parts[1][0], "dp", chip_perm(dp, flip))
        crossed = lax.ppermute(parts[1][1], "dp", chip_perm(dp, flip, True))
        return straight, crossed

    def finished(kept, parts, straight, crossed):
        extra = parts.get(0, [])
        mine = add(kept[0], straight, *extra[:1])
        other = add(sibling(add(kept[1], *extra[1:]) if extra else kept[1]), crossed)
        return done(jnp.where(
            core == 0, jnp.concatenate([mine, other], axis=1), jnp.concatenate([other, mine], axis=1)
        ))

    down_sum, up_sum = (g_rows_of, g_there, act), (x_rows_of, x_there, pre)
    away = list(reversed(range(1, chips // 2)))
    settle("columns")
    down_parts = {r: part(r, *down_sum) for r in away}
    down_sent = pass_on(down_parts)
    for s in range(2, end):
        running = onward(done(add(*after(*shares[s]), running)))
    settle(("g", end), ("share", end))
    up_parts = {r: part(r, *up_sum) for r in away}
    up_sent = pass_on(up_parts)
    last.extend(down_sent)
    down_kept = part(0, *down_sum)
    running = onward(done(add(*after(*shares[end]), running)))
    down_grad = finished(down_kept, down_parts, *down_sent)
    up_kept = part(0, *up_sum)
    input_grad = add(*shares[0], running).reshape(OWNB, here, d)
    up_grad = finished(up_kept, up_parts, *up_sent)
    return input_grad, up_grad, down_grad


def solution(mesh):
    placed = (
        P("dp", "tensor", None),
        P("dp", "tensor", None),
        P(None, "tensor"),
        P(None, "tensor"),
        P(),
        P(),
    )
    return jax.shard_map(
        local,
        mesh=mesh,
        in_specs=placed,
        out_specs=(P("dp", "tensor", None), P("dp", "tensor"), P("dp", "tensor")),
        check_vma=False,
    )
```

```python
import functools

import jax
import jax.numpy as jnp
from jax import lax
from jax.experimental import pallas as pl
from jax.experimental.pallas import tpu as pltpu
from jax.sharding import PartitionSpec as P

OWNB = 4
BF16 = jnp.bfloat16
F32 = jnp.float32
VMEM_LIMIT = 60 * 1024 * 1024
SHORT = pl.CostEstimate(flops=1, bytes_accessed=1, transcendentals=0)


def chip_with(j, v, core):
    return jnp.where(core == 0, 2 * j + v, ((j >> 1) << 2) + 2 * v + (j & 1))


def pool_bit(chip, core):
    return jnp.where(core == 0, chip & 1, (chip >> 1) & 1)


def other_bits(chip, core):
    return jnp.where(core == 0, chip >> 1, ((chip >> 2) << 1) + (chip & 1))


def chip_perm(dp, flip, cross=False):
    return [(i, 2 * ((i >> 1) ^ flip(i & 1)) + ((i & 1) ^ int(cross))) for i in range(dp)]


def start_of(count, source, dp):
    total = jnp.int32(0)
    for j in range(dp):
        total = total + jnp.where(source > j, count[j], 0)
    return total


def source_of(count, number, dp):
    end, source = jnp.int32(0), jnp.int32(0)
    for j in range(dp):
        end = end + count[j]
        source = source + jnp.where(end <= number, 1, 0)
    return source


def run(copies):
    for copy in copies:
        copy.start()
    for copy in copies:
        copy.wait()


def pack_body(info, count, rows, *refs):
    outs, sems = refs[:-1], refs[-1]
    dp, blocks = 2 * len(outs), rows.shape[0]
    start = start_of(count, info[0], dp)
    copies = []
    for f, out in enumerate(outs):
        for core in range(2):
            owner = 2 * ((info[0] >> 1) ^ f) + core
            block = jnp.minimum(lax.rem(owner + OWNB * dp - start, dp), blocks - 1)
            copies.append(pltpu.make_async_copy(rows.at[block], out.at[core], sems.at[2 * f + core]))
    run(copies)


def pack(rows, info, count, chips):
    _, here, d = rows.shape
    shape = jax.ShapeDtypeStruct((2, here, d), BF16)
    spec = pl.BlockSpec((2, here, d), lambda n, i, c: (0, 0, 0))
    return pl.pallas_call(
        pack_body,
        out_shape=(shape,) * chips,
        grid_spec=pltpu.PrefetchScalarGridSpec(
            num_scalar_prefetch=2,
            grid=(1,),
            in_specs=[pl.BlockSpec(memory_space=pl.ANY)],
            out_specs=(spec,) * chips,
            scratch_shapes=[pltpu.SemaphoreType.DMA((2 * chips,))],
        ),
        compiler_params=pltpu.CompilerParams(vmem_limit_bytes=VMEM_LIMIT),
        cost_estimate=SHORT,
    )(info, count, rows)


def across_body(info, *refs):
    arrived, out, sems = refs[:-2], refs[-2], refs[-1]
    away = 1 - (info[0] & 1)
    run([pltpu.make_async_copy(a.at[away], out.at[f], sems.at[f]) for f, a in enumerate(arrived)])


def across(arrived, info):
    chips = len(arrived)
    _, here, d = arrived[0].shape
    return pl.pallas_call(
        across_body,
        out_shape=jax.ShapeDtypeStruct((chips, here, d), BF16),
        grid_spec=pltpu.PrefetchScalarGridSpec(
            num_scalar_prefetch=1,
            grid=(1,),
            in_specs=[pl.BlockSpec(memory_space=pl.ANY)] * chips,
            out_specs=pl.BlockSpec((chips, here, d), lambda n, i: (0, 0, 0)),
            scratch_shapes=[pltpu.SemaphoreType.DMA((chips,))],
        ),
        compiler_params=pltpu.CompilerParams(vmem_limit_bytes=VMEM_LIMIT),
        cost_estimate=SHORT,
    )(info, *arrived)


def select_body(info, count, patches, *refs):
    arrived, (sib, out, sems) = refs[:-3], refs[-3:]
    dp, here = 2 * len(arrived), out.shape[1]
    core, chip = info[0] & 1, info[0] >> 1
    filled = []
    for m in range(OWNB):
        number = info[0] + dp * m
        source = source_of(count, number, dp)
        filled.append(patches[source, number - start_of(count, source, dp)])
        f = (source >> 1) ^ chip
        same = (source & 1) == core
        for k, a in enumerate(arrived):
            @pl.when(same & (f == k))
            def _(a=a):
                pltpu.make_async_copy(a.at[core], out.at[m], sems.at[m]).start()

        @pl.when(jnp.logical_not(same))
        def _():
            pltpu.make_async_copy(sib.at[f], out.at[m], sems.at[m]).start()

    row = lax.broadcasted_iota(jnp.int32, out.shape[1:], 0) + info[1] * here
    for m in range(OWNB):
        pltpu.make_async_copy(sib.at[0], out.at[m], sems.at[m]).wait()
        out[m] = jnp.where(row < filled[m], out[m].astype(F32), 0.0).astype(out.dtype)


def select(arrived, sib, info, count, patches):
    _, here, d = sib.shape
    return pl.pallas_call(
        select_body,
        out_shape=jax.ShapeDtypeStruct((OWNB, here, d), BF16),
        grid_spec=pltpu.PrefetchScalarGridSpec(
            num_scalar_prefetch=3,
            grid=(1,),
            in_specs=[pl.BlockSpec(memory_space=pl.ANY)] * (len(arrived) + 1),
            out_specs=pl.BlockSpec((OWNB, here, d), lambda n, i, c, p: (0, 0, 0)),
            scratch_shapes=[pltpu.SemaphoreType.DMA((OWNB,))],
        ),
        compiler_params=pltpu.CompilerParams(vmem_limit_bytes=VMEM_LIMIT),
        cost_estimate=SHORT,
    )(info, count, patches, *arrived, sib)


def block_of(size, most):
    for width in range(most, 0, -128):
        if size % width == 0:
            return width
    return size


def load_rows(own, sib, rows):
    half = own.shape[0]
    rows[:half] = own[...]
    rows[half:] = sib[...]


def put_partner_columns(info, rows, out, hidden, chips):
    core, chip = info[0] & 1, info[0] >> 1
    width = rows.shape[1] // chips
    away = 1 - pool_bit(chip, core)
    for j in range(chips // 2):
        at = pl.multiple_of(chip_with(j, away, core) * width, 128)
        out[:, hidden + j * width:hidden + (j + 1) * width] = rows[:, pl.ds(at, width)]


def up_body(info, own, sib, w, out, slope, rows, *, hidden, chips):
    n = pl.program_id(0)

    @pl.when(n == 0)
    def _():
        load_rows(own, sib, rows)
        put_partner_columns(info, rows, out, hidden, chips)

    pre_act = jnp.dot(rows[...], w[...], preferred_element_type=F32)
    cdf = 0.5 * (1.0 + lax.erf(pre_act * 0.7071067811865476))
    density = jnp.exp(-0.5 * pre_act * pre_act) * 0.3989422804014327
    width = w.shape[1]
    out[:, pl.ds(pl.multiple_of(n * width, 128), width)] = (pre_act * cdf).astype(out.dtype)
    slope[...] = (cdf + pre_act * density).astype(slope.dtype)


def down_body(info, own, sib, w, slope, out, rows, *, hidden, chips):
    n = pl.program_id(0)

    @pl.when(n == 0)
    def _():
        load_rows(own, sib, rows)
        if out.shape[1] > hidden:
            put_partner_columns(info, rows, out, hidden, chips)

    act_grad = jnp.dot(rows[...], w[...], preferred_element_type=F32)
    width = w.shape[1]
    out[:, pl.ds(pl.multiple_of(n * width, 128), width)] = (act_grad * slope[...]).astype(out.dtype)


def columns_body(info, own, sib, out, rows, *, chips):
    load_rows(own, sib, rows)
    put_partner_columns(info, rows, out, 0, chips)


def partner_columns(own, sib, info, chips):
    half, d = own.shape
    spec = pl.BlockSpec((half, d), lambda n, i: (0, 0))
    return pl.pallas_call(
        functools.partial(columns_body, chips=chips),
        out_shape=jax.ShapeDtypeStruct((2 * half, d // 2), BF16),
        grid_spec=pltpu.PrefetchScalarGridSpec(
            num_scalar_prefetch=1,
            grid=(1,),
            in_specs=[spec, spec],
            out_specs=pl.BlockSpec((2 * half, d // 2), lambda n, i: (0, 0)),
            scratch_shapes=[pltpu.VMEM((2 * half, d), BF16)],
        ),
        compiler_params=pltpu.CompilerParams(vmem_limit_bytes=VMEM_LIMIT),
        cost_estimate=SHORT,
    )(info, own, sib)


def forward(own, sib, w, info, chips, slope=None, with_columns=True):
    half, d = own.shape
    hidden = w.shape[1] // 2
    width = block_of(hidden, 768)
    steps = hidden // width
    total = hidden + (d // 2 if with_columns else 0)
    out_shape = jax.ShapeDtypeStruct((2 * half, total), BF16)
    out_specs = pl.BlockSpec((2 * half, total), lambda n, i: (0, 0))
    slope_spec = pl.BlockSpec((2 * half, width), lambda n, i: (0, n))
    rows_spec = pl.BlockSpec((half, d), lambda n, i: (0, 0))
    w_spec = pl.BlockSpec((d, width), lambda n, i: (0, (i[0] & 1) * steps + n))
    in_specs = [rows_spec, rows_spec, w_spec]
    operands = [own, sib, w]
    if slope is None:
        body = up_body
        out_shape = (out_shape, jax.ShapeDtypeStruct((2 * half, hidden), BF16))
        out_specs = (out_specs, slope_spec)
    else:
        body = down_body
        in_specs.append(slope_spec)
        operands.append(slope)
    return pl.pallas_call(
        functools.partial(body, hidden=hidden, chips=chips),
        out_shape=out_shape,
        grid_spec=pltpu.PrefetchScalarGridSpec(
            num_scalar_prefetch=1,
            grid=(steps,),
            in_specs=in_specs,
            out_specs=out_specs,
            scratch_shapes=[pltpu.VMEM((2 * half, d), BF16)],
        ),
        compiler_params=pltpu.CompilerParams(vmem_limit_bytes=VMEM_LIMIT),
        cost_estimate=SHORT,
    )(info, *operands)


def input_body(info, pre, w, own, sib):
    value = lax.dot_general(pre[...], w[...], (((1,), (1,)), ((), ())), preferred_element_type=F32)
    half = own.shape[0]
    own[...] = value[:half].astype(own.dtype)
    sib[...] = value[half:].astype(sib.dtype)


def input_part(pre, w, info):
    rows = pre.shape[0]
    d, hidden = w.shape[0], w.shape[1] // 2
    width = block_of(d, 1536)
    shape = jax.ShapeDtypeStruct((rows // 2, d), BF16)
    spec = pl.BlockSpec((rows // 2, width), lambda n, i: (0, n))
    return pl.pallas_call(
        input_body,
        out_shape=(shape, shape),
        grid_spec=pltpu.PrefetchScalarGridSpec(
            num_scalar_prefetch=1,
            grid=(d // width,),
            in_specs=[
                pl.BlockSpec((rows, hidden), lambda n, i: (0, 0)),
                pl.BlockSpec((width, hidden), lambda n, i: (n, i[0] & 1)),
            ],
            out_specs=(spec, spec),
        ),
        compiler_params=pltpu.CompilerParams(vmem_limit_bytes=VMEM_LIMIT),
        cost_estimate=SHORT,
    )(info, pre, w)


def weight_body(at, *refs, begins, width, block):
    slots = len(begins)
    ins, (straight, crossed, left, right, total, left_sems, right_sems) = refs[:5 * slots], refs[5 * slots:]
    half, hidden = ins[0].shape[0], right.shape[1]
    copies = []
    for s in range(slots):
        own, sib, there, mine, theirs = ins[5 * s:5 * s + 5]
        first = 4 * s * half
        for k, (rows, column, to, size) in enumerate((
            (own, at[0] * width, first, half),
            (sib, at[0] * width, first + half, half),
            (there, begins[s] + at[1] * width, first + 2 * half, 2 * half),
        )):
            source = rows.at[:, pl.ds(pl.multiple_of(column, 128), width)]
            copies.append(pltpu.make_async_copy(source, left.at[pl.ds(to, size)], left_sems.at[3 * s + k]))
        for k, hidden_side in enumerate((mine, theirs)):
            source = hidden_side.at[:, pl.ds(0, hidden)]
            to = right.at[pl.ds(first + 2 * k * half, 2 * half)]
            copies.append(pltpu.make_async_copy(source, to, right_sems.at[2 * s + k]))
    for copy in copies:
        copy.start()
    middle = slots // 2
    dims = (((0,), (0,)), ((), ()))
    columns = [slice(n, n + block) for n in range(0, hidden, block)]
    for copy in copies[:5 * middle]:
        copy.wait()
    early = 4 * middle * half
    for cut in columns:
        total[:, cut] = lax.dot_general(left[:early], right[:early, cut], dims, preferred_element_type=F32)
    for copy in copies[5 * middle:]:
        copy.wait()
    span = width // 2
    is_first = at[2] == 0
    for cut in columns:
        value = total[:, cut] + lax.dot_general(left[early:], right[early:, cut], dims, preferred_element_type=F32)
        low, high = value[:span], value[span:]
        straight[:, cut] = jnp.where(is_first, low, high).astype(straight.dtype)
        crossed[:, cut] = jnp.where(is_first, high, low).astype(crossed.dtype)


def weight_part(rows, there_rows, rights, own_at, there_at, core, width, hidden):
    slots, size = len(rows), 2 * rows[0][0].shape[0]
    at = jnp.stack([own_at, there_at, core]).astype(jnp.int32)
    block = block_of(hidden, 512)
    operands = []
    for (own, sib), (there, _), (mine, theirs) in zip(rows, there_rows, rights):
        operands += [own, sib, there, mine, theirs]
    shape = jax.ShapeDtypeStruct((width // 2, hidden), BF16)
    spec = pl.BlockSpec((width // 2, hidden), lambda n, a: (0, 0))
    return pl.pallas_call(
        functools.partial(weight_body, begins=[begin for _, begin in there_rows], width=width, block=block),
        out_shape=(shape, shape),
        grid_spec=pltpu.PrefetchScalarGridSpec(
            num_scalar_prefetch=1,
            grid=(1,),
            in_specs=[pl.BlockSpec(memory_space=pl.ANY)] * len(operands),
            out_specs=(spec, spec),
            scratch_shapes=[
                pltpu.VMEM((2 * slots * size, width), BF16),
                pltpu.VMEM((2 * slots * size, hidden), BF16),
                pltpu.VMEM((width, hidden), F32),
                pltpu.SemaphoreType.DMA((3 * slots,)),
                pltpu.SemaphoreType.DMA((2 * slots,)),
            ],
        ),
        compiler_params=pltpu.CompilerParams(vmem_limit_bytes=VMEM_LIMIT),
        cost_estimate=SHORT,
    )(at, *operands)


def add(*values):
    return sum(v.astype(F32) for v in values).astype(BF16)


def local(x_rows, g_rows, w_up, w_down_t, block_count, patches):
    dp, tensor = lax.axis_size("dp"), lax.axis_size("tensor")
    chips = dp // 2
    me, plane = lax.axis_index("dp"), lax.axis_index("tensor")
    chip, core = me >> 1, me & 1
    info = jnp.stack([me, plane]).astype(jnp.int32)
    here, d = x_rows.shape[1:]
    hidden = w_up.shape[1] // 2
    ring = [(i, (i + 1) % tensor) for i in range(tensor)]
    to_sibling = [(i, i ^ 1) for i in range(dp)]
    to_pool = chip_perm(dp, lambda c: 1 << c)
    last = []

    def after(*values):
        out = lax.optimization_barrier((*values, *last))[:len(values)]
        return out if len(out) > 1 else out[0]

    def done(value):
        last[:] = [value]
        return value

    def onward(piece):
        return lax.ppermute(piece, "tensor", ring)

    def sibling(piece):
        return lax.ppermute(piece, "dp", to_sibling)

    def pooled(piece):
        return lax.ppermute(piece, "dp", to_pool)

    def dispatched(packed):
        return [packed[0]] + [
            lax.ppermute(p, "dp", [(i, i ^ (2 * f)) for i in range(dp)]) for f, p in enumerate(packed) if f
        ]

    def chosen(arrived):
        arrived = list(after(*arrived))
        sib = sibling(done(across(arrived, info)))
        return done(select(arrived, sib, info, block_count, patches)).reshape(OWNB * here, d)

    def arrive(own, sib, ahead, further=True):
        piece = after(ahead)
        own.append(piece)
        sib.append(sibling(piece))
        return onward(piece) if further else None

    x_own, x_sib, x_there = [], [], []
    g_own, g_sib, g_there = [], [], []
    act, slope, pre, shares, pools = [], [], [], [], {}

    def settle(*names):
        last.extend(pools[name] for name in names if name in pools)

    def up(s):
        mine, slope_s = forward(*after(x_own[s], x_sib[s]), w_up, info, chips)
        theirs = pools["x", s] = pooled(done(mine))
        x_there.append((theirs, hidden))
        slope.append(slope_s)
        act.append((mine, theirs))

    def down(s, with_columns=True):
        mine = forward(*after(g_own[s], g_sib[s]), w_down_t, info, chips, slope[s], with_columns)
        theirs = pools["g", s] = pooled(done(mine))
        if with_columns:
            g_there.append((theirs, hidden))
        pre.append((mine, theirs))

    def share(s):
        own, sib = input_part(after(pre[s][0]), w_up, info)
        pools["share", s] = sibling(done(sib))
        shares.append((own, pools["share", s]))

    send_x = pack(x_rows, info, block_count, chips)
    done(send_x[0])
    arrived_x = dispatched(send_x)
    send_g = pack(after(g_rows), info, block_count, chips)
    done(send_g[0])
    arrived_g = dispatched(send_g)
    x_own.append(chosen(arrived_x))
    x_sib.append(sibling(x_own[0]))
    x_ahead = onward(x_own[0])
    up(0)
    g_own.append(chosen(arrived_g))
    g_sib.append(sibling(g_own[0]))
    end = tensor - 1
    for s in range(1, tensor):
        x_ahead = arrive(x_own, x_sib, x_ahead, s < end)
        if s == end:
            g_ahead = onward(after(g_own[0]))
        settle(("x", s - 2))
        up(s)
        if s == 2:
            settle(("x", 1))
            down(0)
    settle(("x", end - 1))
    share(0)
    for s in range(1, end):
        g_ahead = arrive(g_own, g_sib, g_ahead)
        settle(("share", s - 1), ("x", end) if s > 1 else None, ("g", s - 2))
        down(s)
        settle(("g", 0))
        share(s)

    settle(("g", end - 2))
    first_share = done(add(*after(*shares[1])))
    arrive(g_own, g_sib, g_ahead, False)
    running = onward(lax.optimization_barrier((first_share, g_own[end]))[0])
    columns = done(partner_columns(*after(g_own[end], g_sib[end]), info, chips))
    pools["columns"] = pooled(columns)
    g_there.append((pools["columns"], 0))
    settle(("g", end - 1), ("share", end - 1))
    down(end, False)

    span = d // dp
    near, mine_j = pool_bit(chip, core), other_bits(chip, core)

    def part(r, rows, there, rights):
        j = mine_j ^ r
        rows = [after(*rows[0]), *rows[1:]]
        straight, crossed = weight_part(rows, there, rights, chip_with(j, near, core), j, core, 2 * span, hidden)
        done(straight)
        return [straight, crossed]

    bits = (chips // 2).bit_length() - 1

    def pass_on(parts):
        for k in reversed(range(1, bits)):
            perm = chip_perm(dp, lambda c: 2 << k)
            for r in range(1 << k, 2 << k):
                for h in range(2):
                    sent = lax.ppermute(parts[r][h], "dp", perm)
                    kept = parts.get(r ^ (1 << k))
                    parts[r ^ (1 << k)] = kept or [None, None]
                    parts[r ^ (1 << k)][h] = add(kept[h], sent) if kept and kept[h] is not None else sent
        flip = lambda c: 2 >> c
        straight = lax.ppermute(parts[1][0], "dp", chip_perm(dp, flip))
        crossed = lax.ppermute(parts[1][1], "dp", chip_perm(dp, flip, True))
        return straight, crossed

    def finished(kept, parts, straight, crossed):
        extra = parts.get(0, [])
        sib = sibling(add(kept[1], *extra[1:]) if extra else kept[1])
        straight, crossed = lax.optimization_barrier((straight, crossed))
        mine = add(kept[0], straight, *extra[:1])
        mine, sib = lax.optimization_barrier((mine, sib))
        other = add(sib, crossed)
        return done(jnp.where(
            core == 0, jnp.concatenate([mine, other], axis=1), jnp.concatenate([other, mine], axis=1)
        ))

    down_sum = (list(zip(g_own, g_sib)), g_there, act)
    up_sum = (list(zip(x_own, x_sib)), x_there, pre)
    away = list(reversed(range(1, chips // 2)))
    settle("columns")
    down_parts = {r: part(r, *down_sum) for r in away}
    down_sent = pass_on(down_parts)
    for s in range(2, end):
        running = onward(done(add(*after(*shares[s]), running)))
    share(end)
    settle(("g", end))
    last.append(down_sent[0])
    up_parts = {r: part(r, *up_sum) for r in away}
    up_sent = pass_on(up_parts)
    running = onward(done(add(*after(*shares[end]), running)))
    last.append(down_sent[1])
    down_kept = part(0, *down_sum)
    last.append(up_sent[0])
    up_kept = part(0, *up_sum)
    down_grad = finished(down_kept, down_parts, *down_sent)
    input_grad = done(add(*after(*shares[0]), running)).reshape(OWNB, here, d)
    up_grad = finished(up_kept, up_parts, *up_sent)
    return input_grad, up_grad, down_grad


def solution(mesh):
    placed = (
        P("dp", "tensor", None),
        P("dp", "tensor", None),
        P(None, "tensor"),
        P(None, "tensor"),
        P(),
        P(),
    )
    return jax.shard_map(
        local,
        mesh=mesh,
        in_specs=placed,
        out_specs=(P("dp", "tensor", None), P("dp", "tensor"), P("dp", "tensor")),
        check_vma=False,
    )
```

```python
import functools

import jax
import jax.numpy as jnp
from jax import lax
from jax.experimental import pallas as pl
from jax.experimental.pallas import tpu as pltpu
from jax.sharding import PartitionSpec as P

OWNB = 4
BF16 = jnp.bfloat16
F32 = jnp.float32
VMEM_LIMIT = 60 * 1024 * 1024
SHORT = pl.CostEstimate(flops=1, bytes_accessed=1, transcendentals=0)


def chip_with(j, v, core):
    return jnp.where(core == 0, 2 * j + v, ((j >> 1) << 2) + 2 * v + (j & 1))


def pool_bit(chip, core):
    return jnp.where(core == 0, chip & 1, (chip >> 1) & 1)


def other_bits(chip, core):
    return jnp.where(core == 0, chip >> 1, ((chip >> 2) << 1) + (chip & 1))


def chip_perm(dp, flip, cross=False):
    return [(i, 2 * ((i >> 1) ^ flip(i & 1)) + ((i & 1) ^ int(cross))) for i in range(dp)]


def start_of(count, source, dp):
    total = jnp.int32(0)
    for j in range(dp):
        total = total + jnp.where(source > j, count[j], 0)
    return total


def source_of(count, number, dp):
    end, source = jnp.int32(0), jnp.int32(0)
    for j in range(dp):
        end = end + count[j]
        source = source + jnp.where(end <= number, 1, 0)
    return source


def run(copies):
    for copy in copies:
        copy.start()
    for copy in copies:
        copy.wait()


def pack_body(info, count, rows, *refs):
    outs, sems = refs[:-1], refs[-1]
    dp, blocks = 2 * len(outs), rows.shape[0]
    start = start_of(count, info[0], dp)
    copies = []
    for f, out in enumerate(outs):
        for core in range(2):
            owner = 2 * ((info[0] >> 1) ^ f) + core
            block = jnp.minimum(lax.rem(owner + OWNB * dp - start, dp), blocks - 1)
            copies.append(pltpu.make_async_copy(rows.at[block], out.at[core], sems.at[2 * f + core]))
    run(copies)


def pack(rows, info, count, chips):
    _, here, d = rows.shape
    shape = jax.ShapeDtypeStruct((2, here, d), BF16)
    spec = pl.BlockSpec((2, here, d), lambda n, i, c: (0, 0, 0))
    return pl.pallas_call(
        pack_body,
        out_shape=(shape,) * chips,
        grid_spec=pltpu.PrefetchScalarGridSpec(
            num_scalar_prefetch=2,
            grid=(1,),
            in_specs=[pl.BlockSpec(memory_space=pl.ANY)],
            out_specs=(spec,) * chips,
            scratch_shapes=[pltpu.SemaphoreType.DMA((2 * chips,))],
        ),
        compiler_params=pltpu.CompilerParams(vmem_limit_bytes=VMEM_LIMIT),
        cost_estimate=SHORT,
    )(info, count, rows)


def across_body(info, *refs):
    arrived, (here, away, sems) = refs[:-3], refs[-3:]
    core = info[0] & 1
    copies = []
    for f, a in enumerate(arrived):
        copies.append(pltpu.make_async_copy(a.at[1 - core], away.at[f], sems.at[2 * f]))
        copies.append(pltpu.make_async_copy(a.at[core], here.at[f], sems.at[2 * f + 1]))
    run(copies)


def across(arrived, info):
    chips = len(arrived)
    _, here, d = arrived[0].shape
    shape = jax.ShapeDtypeStruct((chips, here, d), BF16)
    spec = pl.BlockSpec((chips, here, d), lambda n, i: (0, 0, 0))
    return pl.pallas_call(
        across_body,
        out_shape=(shape, shape),
        grid_spec=pltpu.PrefetchScalarGridSpec(
            num_scalar_prefetch=1,
            grid=(1,),
            in_specs=[pl.BlockSpec(memory_space=pl.ANY)] * chips,
            out_specs=(spec, spec),
            scratch_shapes=[pltpu.SemaphoreType.DMA((2 * chips,))],
        ),
        compiler_params=pltpu.CompilerParams(vmem_limit_bytes=VMEM_LIMIT),
        cost_estimate=SHORT,
    )(info, *arrived)


def select_body(info, count, patches, own, sib, out, sems):
    dp, here = 2 * own.shape[0], out.shape[1]
    core, chip = info[0] & 1, info[0] >> 1
    filled = []
    for m in range(OWNB):
        number = info[0] + dp * m
        source = source_of(count, number, dp)
        filled.append(patches[source, number - start_of(count, source, dp)])
        f = (source >> 1) ^ chip
        same = (source & 1) == core

        @pl.when(same)
        def _():
            pltpu.make_async_copy(own.at[f], out.at[m], sems.at[m]).start()

        @pl.when(jnp.logical_not(same))
        def _():
            pltpu.make_async_copy(sib.at[f], out.at[m], sems.at[m]).start()

    row = lax.broadcasted_iota(jnp.int32, out.shape[1:], 0) + info[1] * here
    for m in range(OWNB):
        pltpu.make_async_copy(sib.at[0], out.at[m], sems.at[m]).wait()
        out[m] = jnp.where(row < filled[m], out[m].astype(F32), 0.0).astype(out.dtype)


def select(own, sib, info, count, patches):
    _, here, d = sib.shape
    return pl.pallas_call(
        select_body,
        out_shape=jax.ShapeDtypeStruct((OWNB, here, d), BF16),
        grid_spec=pltpu.PrefetchScalarGridSpec(
            num_scalar_prefetch=3,
            grid=(1,),
            in_specs=[pl.BlockSpec(memory_space=pl.ANY)] * 2,
            out_specs=pl.BlockSpec((OWNB, here, d), lambda n, i, c, p: (0, 0, 0)),
            scratch_shapes=[pltpu.SemaphoreType.DMA((OWNB,))],
        ),
        compiler_params=pltpu.CompilerParams(vmem_limit_bytes=VMEM_LIMIT),
        cost_estimate=SHORT,
    )(info, count, patches, own, sib)


def block_of(size, most):
    for width in range(most, 0, -128):
        if size % width == 0:
            return width
    return size


def load_rows(own, sib, rows):
    half = own.shape[0]
    rows[:half] = own[...]
    rows[half:] = sib[...]


def put_partner_columns(info, rows, out, hidden, chips):
    core, chip = info[0] & 1, info[0] >> 1
    width = rows.shape[1] // chips
    away = 1 - pool_bit(chip, core)
    for j in range(chips // 2):
        at = pl.multiple_of(chip_with(j, away, core) * width, 128)
        out[:, hidden + j * width:hidden + (j + 1) * width] = rows[:, pl.ds(at, width)]


def up_body(info, own, sib, w, out, slope, rows, *, hidden, chips):
    n = pl.program_id(0)

    @pl.when(n == 0)
    def _():
        load_rows(own, sib, rows)
        put_partner_columns(info, rows, out, hidden, chips)

    pre_act = jnp.dot(rows[...], w[...], preferred_element_type=F32)
    cdf = 0.5 * (1.0 + lax.erf(pre_act * 0.7071067811865476))
    density = jnp.exp(-0.5 * pre_act * pre_act) * 0.3989422804014327
    width = w.shape[1]
    out[:, pl.ds(pl.multiple_of(n * width, 128), width)] = (pre_act * cdf).astype(out.dtype)
    slope[...] = (cdf + pre_act * density).astype(slope.dtype)


def down_body(info, own, sib, w, slope, out, rows, *, hidden, chips):
    n = pl.program_id(0)

    @pl.when(n == 0)
    def _():
        load_rows(own, sib, rows)
        if out.shape[1] > hidden:
            put_partner_columns(info, rows, out, hidden, chips)

    act_grad = jnp.dot(rows[...], w[...], preferred_element_type=F32)
    width = w.shape[1]
    out[:, pl.ds(pl.multiple_of(n * width, 128), width)] = (act_grad * slope[...]).astype(out.dtype)


def columns_body(info, own, sib, out, rows, *, chips):
    load_rows(own, sib, rows)
    put_partner_columns(info, rows, out, 0, chips)


def partner_columns(own, sib, info, chips):
    half, d = own.shape
    spec = pl.BlockSpec((half, d), lambda n, i: (0, 0))
    return pl.pallas_call(
        functools.partial(columns_body, chips=chips),
        out_shape=jax.ShapeDtypeStruct((2 * half, d // 2), BF16),
        grid_spec=pltpu.PrefetchScalarGridSpec(
            num_scalar_prefetch=1,
            grid=(1,),
            in_specs=[spec, spec],
            out_specs=pl.BlockSpec((2 * half, d // 2), lambda n, i: (0, 0)),
            scratch_shapes=[pltpu.VMEM((2 * half, d), BF16)],
        ),
        compiler_params=pltpu.CompilerParams(vmem_limit_bytes=VMEM_LIMIT),
        cost_estimate=SHORT,
    )(info, own, sib)


def forward(own, sib, w, info, chips, slope=None, with_columns=True):
    half, d = own.shape
    hidden = w.shape[1] // 2
    width = block_of(hidden, 768)
    steps = hidden // width
    total = hidden + (d // 2 if with_columns else 0)
    out_shape = jax.ShapeDtypeStruct((2 * half, total), BF16)
    out_specs = pl.BlockSpec((2 * half, total), lambda n, i: (0, 0))
    slope_spec = pl.BlockSpec((2 * half, width), lambda n, i: (0, n))
    rows_spec = pl.BlockSpec((half, d), lambda n, i: (0, 0))
    w_spec = pl.BlockSpec((d, width), lambda n, i: (0, (i[0] & 1) * steps + n))
    in_specs = [rows_spec, rows_spec, w_spec]
    operands = [own, sib, w]
    if slope is None:
        body = up_body
        out_shape = (out_shape, jax.ShapeDtypeStruct((2 * half, hidden), BF16))
        out_specs = (out_specs, slope_spec)
    else:
        body = down_body
        in_specs.append(slope_spec)
        operands.append(slope)
    return pl.pallas_call(
        functools.partial(body, hidden=hidden, chips=chips),
        out_shape=out_shape,
        grid_spec=pltpu.PrefetchScalarGridSpec(
            num_scalar_prefetch=1,
            grid=(steps,),
            in_specs=in_specs,
            out_specs=out_specs,
            scratch_shapes=[pltpu.VMEM((2 * half, d), BF16)],
        ),
        compiler_params=pltpu.CompilerParams(vmem_limit_bytes=VMEM_LIMIT),
        cost_estimate=SHORT,
    )(info, *operands)


def input_body(info, pre, w, own, sib):
    value = lax.dot_general(pre[...], w[...], (((1,), (1,)), ((), ())), preferred_element_type=F32)
    half = own.shape[0]
    own[...] = value[:half].astype(own.dtype)
    sib[...] = value[half:].astype(sib.dtype)


def input_part(pre, w, info):
    rows = pre.shape[0]
    d, hidden = w.shape[0], w.shape[1] // 2
    width = block_of(d, 1536)
    shape = jax.ShapeDtypeStruct((rows // 2, d), BF16)
    spec = pl.BlockSpec((rows // 2, width), lambda n, i: (0, n))
    return pl.pallas_call(
        input_body,
        out_shape=(shape, shape),
        grid_spec=pltpu.PrefetchScalarGridSpec(
            num_scalar_prefetch=1,
            grid=(d // width,),
            in_specs=[
                pl.BlockSpec((rows, hidden), lambda n, i: (0, 0)),
                pl.BlockSpec((width, hidden), lambda n, i: (n, i[0] & 1)),
            ],
            out_specs=(spec, spec),
        ),
        compiler_params=pltpu.CompilerParams(vmem_limit_bytes=VMEM_LIMIT),
        cost_estimate=SHORT,
    )(info, pre, w)


def weight_body(at, *refs, begins, width, block):
    slots = len(begins)
    ins, (straight, crossed, left, right, total, left_sems, right_sems) = refs[:5 * slots], refs[5 * slots:]
    half, hidden = ins[0].shape[0], right.shape[1]
    copies = []
    for s in range(slots):
        own, sib, there, mine, theirs = ins[5 * s:5 * s + 5]
        first = 4 * s * half
        for k, (rows, column, to, size) in enumerate((
            (own, at[0] * width, first, half),
            (sib, at[0] * width, first + half, half),
            (there, begins[s] + at[1] * width, first + 2 * half, 2 * half),
        )):
            source = rows.at[:, pl.ds(pl.multiple_of(column, 128), width)]
            copies.append(pltpu.make_async_copy(source, left.at[pl.ds(to, size)], left_sems.at[3 * s + k]))
        for k, hidden_side in enumerate((mine, theirs)):
            source = hidden_side.at[:, pl.ds(0, hidden)]
            to = right.at[pl.ds(first + 2 * k * half, 2 * half)]
            copies.append(pltpu.make_async_copy(source, to, right_sems.at[2 * s + k]))
    for copy in copies:
        copy.start()
    middle = slots // 2
    dims = (((0,), (0,)), ((), ()))
    columns = [slice(n, n + block) for n in range(0, hidden, block)]
    for copy in copies[:5 * middle]:
        copy.wait()
    early = 4 * middle * half
    for cut in columns:
        total[:, cut] = lax.dot_general(left[:early], right[:early, cut], dims, preferred_element_type=F32)
    for copy in copies[5 * middle:]:
        copy.wait()
    span = width // 2
    is_first = at[2] == 0
    for cut in columns:
        value = total[:, cut] + lax.dot_general(left[early:], right[early:, cut], dims, preferred_element_type=F32)
        low, high = value[:span], value[span:]
        straight[:, cut] = jnp.where(is_first, low, high).astype(straight.dtype)
        crossed[:, cut] = jnp.where(is_first, high, low).astype(crossed.dtype)


def weight_part(rows, there_rows, rights, own_at, there_at, core, width, hidden):
    slots, size = len(rows), 2 * rows[0][0].shape[0]
    at = jnp.stack([own_at, there_at, core]).astype(jnp.int32)
    block = block_of(hidden, 512)
    operands = []
    for (own, sib), (there, _), (mine, theirs) in zip(rows, there_rows, rights):
        operands += [own, sib, there, mine, theirs]
    shape = jax.ShapeDtypeStruct((width // 2, hidden), BF16)
    spec = pl.BlockSpec((width // 2, hidden), lambda n, a: (0, 0))
    return pl.pallas_call(
        functools.partial(weight_body, begins=[begin for _, begin in there_rows], width=width, block=block),
        out_shape=(shape, shape),
        grid_spec=pltpu.PrefetchScalarGridSpec(
            num_scalar_prefetch=1,
            grid=(1,),
            in_specs=[pl.BlockSpec(memory_space=pl.ANY)] * len(operands),
            out_specs=(spec, spec),
            scratch_shapes=[
                pltpu.VMEM((2 * slots * size, width), BF16),
                pltpu.VMEM((2 * slots * size, hidden), BF16),
                pltpu.VMEM((width, hidden), F32),
                pltpu.SemaphoreType.DMA((3 * slots,)),
                pltpu.SemaphoreType.DMA((2 * slots,)),
            ],
        ),
        compiler_params=pltpu.CompilerParams(vmem_limit_bytes=VMEM_LIMIT),
        cost_estimate=SHORT,
    )(at, *operands)


def add(*values):
    return sum(v.astype(F32) for v in values).astype(BF16)


def local(x_rows, g_rows, w_up, w_down_t, block_count, patches):
    dp, tensor = lax.axis_size("dp"), lax.axis_size("tensor")
    chips = dp // 2
    me, plane = lax.axis_index("dp"), lax.axis_index("tensor")
    chip, core = me >> 1, me & 1
    info = jnp.stack([me, plane]).astype(jnp.int32)
    here, d = x_rows.shape[1:]
    hidden = w_up.shape[1] // 2
    ring = [(i, (i + 1) % tensor) for i in range(tensor)]
    to_sibling = [(i, i ^ 1) for i in range(dp)]
    to_pool = chip_perm(dp, lambda c: 1 << c)
    last = []

    def after(*values):
        out = lax.optimization_barrier((*values, *last))[:len(values)]
        return out if len(out) > 1 else out[0]

    def done(value):
        last[:] = [value]
        return value

    def onward(piece):
        return lax.ppermute(piece, "tensor", ring)

    def sibling(piece):
        return lax.ppermute(piece, "dp", to_sibling)

    def pooled(piece):
        return lax.ppermute(piece, "dp", to_pool)

    def dispatched(packed):
        return [packed[0]] + [
            lax.ppermute(p, "dp", [(i, i ^ (2 * f)) for i in range(dp)]) for f, p in enumerate(packed) if f
        ]

    def crossed_over(arrived):
        own, away = across(list(after(*arrived)), info)
        return own, sibling(done(away))

    def chosen(own, sib):
        return done(select(*after(own, sib), info, block_count, patches)).reshape(OWNB * here, d)

    def arrive(own, sib, ahead, further=True):
        piece = after(ahead)
        own.append(piece)
        sib.append(sibling(piece))
        return onward(piece) if further else None

    x_own, x_sib, x_there = [], [], []
    g_own, g_sib, g_there = [], [], []
    act, slope, pre, shares, pools = [], [], [], [], {}

    def settle(*names):
        last.extend(pools[name] for name in names if name in pools)

    def up(s):
        mine, slope_s = forward(*after(x_own[s], x_sib[s]), w_up, info, chips)
        theirs = pools["x", s] = pooled(done(mine))
        x_there.append((theirs, hidden))
        slope.append(slope_s)
        act.append((mine, theirs))

    def down(s, with_columns=True):
        mine = forward(*after(g_own[s], g_sib[s]), w_down_t, info, chips, slope[s], with_columns)
        theirs = pools["g", s] = pooled(done(mine))
        if with_columns:
            g_there.append((theirs, hidden))
        pre.append((mine, theirs))

    def share(s):
        own, sib = input_part(after(pre[s][0]), w_up, info)
        pools["share", s] = sibling(done(sib))
        shares.append((own, pools["share", s]))

    send_x = pack(x_rows, info, block_count, chips)
    done(send_x[0])
    arrived_x = dispatched(send_x)
    send_g = pack(after(g_rows), info, block_count, chips)
    done(send_g[0])
    arrived_g = dispatched(send_g)
    x_own.append(chosen(*crossed_over(arrived_x)))
    x_sib.append(sibling(x_own[0]))
    x_ahead = onward(x_own[0])
    up(0)
    halves_g = crossed_over(arrived_g)
    end = tensor - 1
    for s in range(1, tensor):
        x_ahead = arrive(x_own, x_sib, x_ahead, s < end)
        if s == end:
            g_ahead = onward(after(g_own[0]))
        settle(("x", s - 2))
        up(s)
        if s == 1:
            g_own.append(chosen(*halves_g))
            g_sib.append(sibling(g_own[0]))
        if s == 2:
            settle(("x", 1))
            down(0)
    settle(("x", end - 1))
    share(0)
    for s in range(1, end):
        g_ahead = arrive(g_own, g_sib, g_ahead)
        settle(("share", s - 1), ("x", end) if s > 1 else None, ("g", s - 2))
        down(s)
        settle(("g", 0))
        share(s)

    settle(("g", end - 2))
    first_share = done(add(*after(*shares[1])))
    arrive(g_own, g_sib, g_ahead, False)
    running = onward(lax.optimization_barrier((first_share, g_own[end]))[0])
    columns = done(partner_columns(*after(g_own[end], g_sib[end]), info, chips))
    pools["columns"] = pooled(columns)
    g_there.append((pools["columns"], 0))
    settle(("g", end - 1), ("share", end - 1))
    down(end, False)
    share(end)

    span = d // dp
    near, mine_j = pool_bit(chip, core), other_bits(chip, core)

    def part(r, rows, there, rights):
        j = mine_j ^ r
        rows = [after(*rows[0]), *rows[1:]]
        straight, crossed = weight_part(rows, there, rights, chip_with(j, near, core), j, core, 2 * span, hidden)
        done(straight)
        return [straight, crossed]

    bits = (chips // 2).bit_length() - 1

    def pass_on(parts):
        for k in reversed(range(1, bits)):
            perm = chip_perm(dp, lambda c: 2 << k)
            for r in range(1 << k, 2 << k):
                for h in range(2):
                    sent = lax.ppermute(parts[r][h], "dp", perm)
                    kept = parts.get(r ^ (1 << k))
                    parts[r ^ (1 << k)] = kept or [None, None]
                    parts[r ^ (1 << k)][h] = add(kept[h], sent) if kept and kept[h] is not None else sent
        flip = lambda c: 2 >> c
        straight = lax.ppermute(parts[1][0], "dp", chip_perm(dp, flip))
        crossed = lax.ppermute(parts[1][1], "dp", chip_perm(dp, flip, True))
        return straight, crossed

    def finished(kept, parts, straight, crossed):
        extra = parts.get(0, [])
        sib = sibling(add(kept[1], *extra[1:]) if extra else kept[1])
        mine = add(after(kept[0]), straight, *extra[:1])
        other = add(sib, crossed)
        return done(jnp.where(
            core == 0, jnp.concatenate([mine, other], axis=1), jnp.concatenate([other, mine], axis=1)
        ))

    down_sum = (list(zip(g_own, g_sib)), g_there, act)
    up_sum = (list(zip(x_own, x_sib)), x_there, pre)
    away = list(reversed(range(1, chips // 2)))
    settle("columns")
    down_parts = {r: part(r, *down_sum) for r in away}
    down_sent = pass_on(down_parts)
    for s in range(2, end):
        running = onward(done(add(*after(*shares[s]), running)))
    settle(("g", end), ("share", end))
    up_parts = {r: part(r, *up_sum) for r in away}
    up_sent = pass_on(up_parts)
    running = onward(done(add(*after(*shares[end]), running)))
    last.extend(down_sent)
    down_kept = part(0, *down_sum)
    up_kept = part(0, *up_sum)
    input_grad = done(add(*after(*shares[0]), running)).reshape(OWNB, here, d)
    down_grad = finished(down_kept, down_parts, *down_sent)
    up_grad = finished(up_kept, up_parts, *up_sent)
    return input_grad, up_grad, down_grad


def solution(mesh):
    placed = (
        P("dp", "tensor", None),
        P("dp", "tensor", None),
        P(None, "tensor"),
        P(None, "tensor"),
        P(),
        P(),
    )
    return jax.shard_map(
        local,
        mesh=mesh,
        in_specs=placed,
        out_specs=(P("dp", "tensor", None), P("dp", "tensor"), P("dp", "tensor")),
        check_vma=False,
    )
```

```python
import functools

import jax
import jax.numpy as jnp
from jax import lax
from jax.experimental import pallas as pl
from jax.experimental.pallas import tpu as pltpu
from jax.sharding import PartitionSpec as P

OWNB = 4
BF16 = jnp.bfloat16
F32 = jnp.float32
VMEM_LIMIT = 60 * 1024 * 1024
SHORT = pl.CostEstimate(flops=1, bytes_accessed=1, transcendentals=0)


def chip_with(j, v, core):
    return jnp.where(core == 0, 2 * j + v, ((j >> 1) << 2) + 2 * v + (j & 1))


def pool_bit(chip, core):
    return jnp.where(core == 0, chip & 1, (chip >> 1) & 1)


def other_bits(chip, core):
    return jnp.where(core == 0, chip >> 1, ((chip >> 2) << 1) + (chip & 1))


def chip_perm(dp, flip, cross=False):
    return [(i, 2 * ((i >> 1) ^ flip(i & 1)) + ((i & 1) ^ int(cross))) for i in range(dp)]


def start_of(count, source, dp):
    total = jnp.int32(0)
    for j in range(dp):
        total = total + jnp.where(source > j, count[j], 0)
    return total


def source_of(count, number, dp):
    end, source = jnp.int32(0), jnp.int32(0)
    for j in range(dp):
        end = end + count[j]
        source = source + jnp.where(end <= number, 1, 0)
    return source


def run(copies):
    for copy in copies:
        copy.start()
    for copy in copies:
        copy.wait()


def pack_body(info, count, rows, *refs, slots):
    outs, sems = refs[:-1], refs[-1]
    blocks = rows.shape[0]
    dp = slots * len(outs)
    start = start_of(count, info[0], dp)
    copies = []
    for k in range(dp):
        f, slot = divmod(k, slots)
        owner = k if len(outs) == 1 else 2 * ((info[0] >> 1) ^ f) + slot
        block = jnp.minimum(lax.rem(owner + OWNB * dp - start, dp), blocks - 1)
        copies.append(pltpu.make_async_copy(rows.at[block], outs[f].at[slot], sems.at[k]))
    run(copies)


def pack(rows, info, count, dp, slots):
    _, here, d = rows.shape
    shape = jax.ShapeDtypeStruct((slots, here, d), BF16)
    spec = pl.BlockSpec((slots, here, d), lambda n, i, c: (0, 0, 0))
    return pl.pallas_call(
        functools.partial(pack_body, slots=slots),
        out_shape=(shape,) * (dp // slots),
        grid_spec=pltpu.PrefetchScalarGridSpec(
            num_scalar_prefetch=2,
            grid=(1,),
            in_specs=[pl.BlockSpec(memory_space=pl.ANY)],
            out_specs=(spec,) * (dp // slots),
            scratch_shapes=[pltpu.SemaphoreType.DMA((dp,))],
        ),
        compiler_params=pltpu.CompilerParams(vmem_limit_bytes=VMEM_LIMIT),
        cost_estimate=SHORT,
    )(info, count, rows)


def across_body(info, *refs):
    arrived, (here, away, sems) = refs[:-3], refs[-3:]
    core = info[0] & 1
    copies = []
    for f, a in enumerate(arrived):
        copies.append(pltpu.make_async_copy(a.at[1 - core], away.at[f], sems.at[2 * f]))
        copies.append(pltpu.make_async_copy(a.at[core], here.at[f], sems.at[2 * f + 1]))
    run(copies)


def across(arrived, info):
    chips = len(arrived)
    _, here, d = arrived[0].shape
    shape = jax.ShapeDtypeStruct((chips, here, d), BF16)
    spec = pl.BlockSpec((chips, here, d), lambda n, i: (0, 0, 0))
    return pl.pallas_call(
        across_body,
        out_shape=(shape, shape),
        grid_spec=pltpu.PrefetchScalarGridSpec(
            num_scalar_prefetch=1,
            grid=(1,),
            in_specs=[pl.BlockSpec(memory_space=pl.ANY)] * chips,
            out_specs=(spec, spec),
            scratch_shapes=[pltpu.SemaphoreType.DMA((2 * chips,))],
        ),
        compiler_params=pltpu.CompilerParams(vmem_limit_bytes=VMEM_LIMIT),
        cost_estimate=SHORT,
    )(info, *arrived)


def select_body(info, count, patches, *refs):
    arrived, (out, sems) = refs[:-2], refs[-2:]
    dp, here = len(arrived) * arrived[0].shape[0], out.shape[1]
    core, chip = info[0] & 1, info[0] >> 1
    filled = []
    for m in range(OWNB):
        number = info[0] + dp * m
        source = source_of(count, number, dp)
        filled.append(patches[source, number - start_of(count, source, dp)])
        if len(arrived) == 1:
            pltpu.make_async_copy(arrived[0].at[source], out.at[m], sems.at[m]).start()
        else:
            own, sib = arrived
            f = (source >> 1) ^ chip
            same = (source & 1) == core

            @pl.when(same)
            def _():
                pltpu.make_async_copy(own.at[f], out.at[m], sems.at[m]).start()

            @pl.when(jnp.logical_not(same))
            def _():
                pltpu.make_async_copy(sib.at[f], out.at[m], sems.at[m]).start()

    row = lax.broadcasted_iota(jnp.int32, out.shape[1:], 0) + info[1] * here
    for m in range(OWNB):
        pltpu.make_async_copy(arrived[0].at[0], out.at[m], sems.at[m]).wait()
        out[m] = jnp.where(row < filled[m], out[m].astype(F32), 0.0).astype(out.dtype)


def select(arrived, info, count, patches):
    _, here, d = arrived[0].shape
    return pl.pallas_call(
        select_body,
        out_shape=jax.ShapeDtypeStruct((OWNB, here, d), BF16),
        grid_spec=pltpu.PrefetchScalarGridSpec(
            num_scalar_prefetch=3,
            grid=(1,),
            in_specs=[pl.BlockSpec(memory_space=pl.ANY)] * len(arrived),
            out_specs=pl.BlockSpec((OWNB, here, d), lambda n, i, c, p: (0, 0, 0)),
            scratch_shapes=[pltpu.SemaphoreType.DMA((OWNB,))],
        ),
        compiler_params=pltpu.CompilerParams(vmem_limit_bytes=VMEM_LIMIT),
        cost_estimate=SHORT,
    )(info, count, patches, *arrived)


def block_of(size, most):
    for width in range(most, 0, -128):
        if size % width == 0:
            return width
    return size


def load_rows(own, sib, rows):
    half = own.shape[0]
    rows[:half] = own[...]
    rows[half:] = sib[...]


def put_partner_columns(info, rows, out, hidden, chips):
    core, chip = info[0] & 1, info[0] >> 1
    width = rows.shape[1] // chips
    away = 1 - pool_bit(chip, core)
    for j in range(chips // 2):
        at = pl.multiple_of(chip_with(j, away, core) * width, 128)
        out[:, hidden + j * width:hidden + (j + 1) * width] = rows[:, pl.ds(at, width)]


def up_body(info, own, sib, w, out, slope, rows, *, hidden, chips):
    n = pl.program_id(0)

    @pl.when(n == 0)
    def _():
        load_rows(own, sib, rows)
        put_partner_columns(info, rows, out, hidden, chips)

    pre_act = jnp.dot(rows[...], w[...], preferred_element_type=F32)
    cdf = 0.5 * (1.0 + lax.erf(pre_act * 0.7071067811865476))
    density = jnp.exp(-0.5 * pre_act * pre_act) * 0.3989422804014327
    width = w.shape[1]
    out[:, pl.ds(pl.multiple_of(n * width, 128), width)] = (pre_act * cdf).astype(out.dtype)
    slope[...] = (cdf + pre_act * density).astype(slope.dtype)


def down_body(info, own, sib, w, slope, out, rows, *, hidden, chips):
    n = pl.program_id(0)

    @pl.when(n == 0)
    def _():
        load_rows(own, sib, rows)
        if out.shape[1] > hidden:
            put_partner_columns(info, rows, out, hidden, chips)

    act_grad = jnp.dot(rows[...], w[...], preferred_element_type=F32)
    width = w.shape[1]
    out[:, pl.ds(pl.multiple_of(n * width, 128), width)] = (act_grad * slope[...]).astype(out.dtype)


def columns_body(info, own, sib, out, rows, *, chips):
    load_rows(own, sib, rows)
    put_partner_columns(info, rows, out, 0, chips)


def partner_columns(own, sib, info, chips):
    half, d = own.shape
    spec = pl.BlockSpec((half, d), lambda n, i: (0, 0))
    return pl.pallas_call(
        functools.partial(columns_body, chips=chips),
        out_shape=jax.ShapeDtypeStruct((2 * half, d // 2), BF16),
        grid_spec=pltpu.PrefetchScalarGridSpec(
            num_scalar_prefetch=1,
            grid=(1,),
            in_specs=[spec, spec],
            out_specs=pl.BlockSpec((2 * half, d // 2), lambda n, i: (0, 0)),
            scratch_shapes=[pltpu.VMEM((2 * half, d), BF16)],
        ),
        compiler_params=pltpu.CompilerParams(vmem_limit_bytes=VMEM_LIMIT),
        cost_estimate=SHORT,
    )(info, own, sib)


def forward(own, sib, w, info, chips, slope=None, with_columns=True):
    half, d = own.shape
    hidden = w.shape[1] // 2
    width = block_of(hidden, 768)
    steps = hidden // width
    total = hidden + (d // 2 if with_columns else 0)
    out_shape = jax.ShapeDtypeStruct((2 * half, total), BF16)
    out_specs = pl.BlockSpec((2 * half, total), lambda n, i: (0, 0))
    slope_spec = pl.BlockSpec((2 * half, width), lambda n, i: (0, n))
    rows_spec = pl.BlockSpec((half, d), lambda n, i: (0, 0))
    w_spec = pl.BlockSpec((d, width), lambda n, i: (0, (i[0] & 1) * steps + n))
    in_specs = [rows_spec, rows_spec, w_spec]
    operands = [own, sib, w]
    if slope is None:
        body = up_body
        out_shape = (out_shape, jax.ShapeDtypeStruct((2 * half, hidden), BF16))
        out_specs = (out_specs, slope_spec)
    else:
        body = down_body
        in_specs.append(slope_spec)
        operands.append(slope)
    return pl.pallas_call(
        functools.partial(body, hidden=hidden, chips=chips),
        out_shape=out_shape,
        grid_spec=pltpu.PrefetchScalarGridSpec(
            num_scalar_prefetch=1,
            grid=(steps,),
            in_specs=in_specs,
            out_specs=out_specs,
            scratch_shapes=[pltpu.VMEM((2 * half, d), BF16)],
        ),
        compiler_params=pltpu.CompilerParams(vmem_limit_bytes=VMEM_LIMIT),
        cost_estimate=SHORT,
    )(info, *operands)


def input_body(info, pre, w, own, sib):
    value = lax.dot_general(pre[...], w[...], (((1,), (1,)), ((), ())), preferred_element_type=F32)
    half = own.shape[0]
    own[...] = value[:half].astype(own.dtype)
    sib[...] = value[half:].astype(sib.dtype)


def input_part(pre, w, info):
    rows = pre.shape[0]
    d, hidden = w.shape[0], w.shape[1] // 2
    width = block_of(d, 1536)
    shape = jax.ShapeDtypeStruct((rows // 2, d), BF16)
    spec = pl.BlockSpec((rows // 2, width), lambda n, i: (0, n))
    return pl.pallas_call(
        input_body,
        out_shape=(shape, shape),
        grid_spec=pltpu.PrefetchScalarGridSpec(
            num_scalar_prefetch=1,
            grid=(d // width,),
            in_specs=[
                pl.BlockSpec((rows, hidden), lambda n, i: (0, 0)),
                pl.BlockSpec((width, hidden), lambda n, i: (n, i[0] & 1)),
            ],
            out_specs=(spec, spec),
        ),
        compiler_params=pltpu.CompilerParams(vmem_limit_bytes=VMEM_LIMIT),
        cost_estimate=SHORT,
    )(info, pre, w)


def weight_body(at, *refs, begins, width, block):
    slots = len(begins)
    ins, outs, (left, right, total, left_sems, right_sems) = refs[:5 * slots], refs[5 * slots:-5], refs[-5:]
    half, hidden = ins[0].shape[0], right.shape[1]
    copies = []
    for s in range(slots):
        own, sib, there, mine, theirs = ins[5 * s:5 * s + 5]
        first = 4 * s * half
        for k, (rows, column, to, size) in enumerate((
            (own, at[0] * width, first, half),
            (sib, at[0] * width, first + half, half),
            (there, begins[s] + at[1] * width, first + 2 * half, 2 * half),
        )):
            source = rows.at[:, pl.ds(pl.multiple_of(column, 128), width)]
            copies.append(pltpu.make_async_copy(source, left.at[pl.ds(to, size)], left_sems.at[3 * s + k]))
        for k, hidden_side in enumerate((mine, theirs)):
            source = hidden_side.at[:, pl.ds(0, hidden)]
            to = right.at[pl.ds(first + 2 * k * half, 2 * half)]
            copies.append(pltpu.make_async_copy(source, to, right_sems.at[2 * s + k]))
    for copy in copies:
        copy.start()
    middle = slots // 2
    dims = (((0,), (0,)), ((), ()))
    columns = [slice(n, n + block) for n in range(0, hidden, block)]
    for copy in copies[:5 * middle]:
        copy.wait()
    early = 4 * middle * half
    for cut in columns:
        total[:, cut] = lax.dot_general(left[:early], right[:early, cut], dims, preferred_element_type=F32)
    for copy in copies[5 * middle:]:
        copy.wait()
    span = width // 2
    is_first = at[2] == 0
    for cut in columns:
        value = total[:, cut] + lax.dot_general(left[early:], right[early:, cut], dims, preferred_element_type=F32)
        if len(outs) == 1:
            outs[0][:, cut] = value.astype(outs[0].dtype)
        else:
            low, high = value[:span], value[span:]
            outs[0][:, cut] = jnp.where(is_first, low, high).astype(outs[0].dtype)
            outs[1][:, cut] = jnp.where(is_first, high, low).astype(outs[1].dtype)


def weight_part(rows, there_rows, rights, own_at, there_at, core, width, hidden, split):
    slots, size = len(rows), 2 * rows[0][0].shape[0]
    at = jnp.stack([own_at, there_at, core]).astype(jnp.int32)
    block = block_of(hidden, 512)
    operands = []
    for (own, sib), (there, _), (mine, theirs) in zip(rows, there_rows, rights):
        operands += [own, sib, there, mine, theirs]
    pieces = 2 if split else 1
    shape = jax.ShapeDtypeStruct((width // pieces, hidden), BF16)
    spec = pl.BlockSpec((width // pieces, hidden), lambda n, a: (0, 0))
    return pl.pallas_call(
        functools.partial(weight_body, begins=[begin for _, begin in there_rows], width=width, block=block),
        out_shape=(shape,) * pieces,
        grid_spec=pltpu.PrefetchScalarGridSpec(
            num_scalar_prefetch=1,
            grid=(1,),
            in_specs=[pl.BlockSpec(memory_space=pl.ANY)] * len(operands),
            out_specs=(spec,) * pieces,
            scratch_shapes=[
                pltpu.VMEM((2 * slots * size, width), BF16),
                pltpu.VMEM((2 * slots * size, hidden), BF16),
                pltpu.VMEM((width, hidden), F32),
                pltpu.SemaphoreType.DMA((3 * slots,)),
                pltpu.SemaphoreType.DMA((2 * slots,)),
            ],
        ),
        compiler_params=pltpu.CompilerParams(vmem_limit_bytes=VMEM_LIMIT),
        cost_estimate=SHORT,
    )(at, *operands)


def add(*values):
    return sum(v.astype(F32) for v in values).astype(BF16)


def local(x_rows, g_rows, w_up, w_down_t, block_count, patches):
    dp, tensor = lax.axis_size("dp"), lax.axis_size("tensor")
    chips = dp // 2
    me, plane = lax.axis_index("dp"), lax.axis_index("tensor")
    chip, core = me >> 1, me & 1
    info = jnp.stack([me, plane]).astype(jnp.int32)
    here, d = x_rows.shape[1:]
    hidden = w_up.shape[1] // 2
    ring = [(i, (i + 1) % tensor) for i in range(tensor)]
    to_sibling = [(i, i ^ 1) for i in range(dp)]
    to_pool = chip_perm(dp, lambda c: 1 << c)
    last = []

    def after(*values):
        out = lax.optimization_barrier((*values, *last))[:len(values)]
        return out if len(out) > 1 else out[0]

    def done(value):
        last[:] = [value]
        return value

    def onward(piece):
        return lax.ppermute(piece, "tensor", ring)

    def sibling(piece):
        return lax.ppermute(piece, "dp", to_sibling)

    def pooled(piece):
        return lax.ppermute(piece, "dp", to_pool)

    def dispatched(packed):
        return [packed[0]] + [
            lax.ppermute(p, "dp", [(i, i ^ (2 * f)) for i in range(dp)]) for f, p in enumerate(packed) if f
        ]

    def crossed_over(arrived):
        own, away = across(list(after(*arrived)), info)
        return own, sibling(done(away))

    def chosen(*arrived):
        arrived = after(*arrived) if len(arrived) > 1 else [after(*arrived)]
        return done(select(arrived, info, block_count, patches)).reshape(OWNB * here, d)

    def arrive(own, sib, ahead, further=True):
        piece = after(ahead)
        own.append(piece)
        sib.append(sibling(piece))
        return onward(piece) if further else None

    x_own, x_sib, x_there = [], [], []
    g_own, g_sib, g_there = [], [], []
    act, slope, pre, shares, pools = [], [], [], [], {}

    def settle(*names):
        last.extend(pools[name] for name in names if name in pools)

    def up(s):
        mine, slope_s = forward(*after(x_own[s], x_sib[s]), w_up, info, chips)
        theirs = pools["x", s] = pooled(done(mine))
        x_there.append((theirs, hidden))
        slope.append(slope_s)
        act.append((mine, theirs))

    def down(s, with_columns=True):
        mine = forward(*after(g_own[s], g_sib[s]), w_down_t, info, chips, slope[s], with_columns)
        theirs = pools["g", s] = pooled(done(mine))
        if with_columns:
            g_there.append((theirs, hidden))
        pre.append((mine, theirs))

    def share(s):
        own, sib = input_part(after(pre[s][0]), w_up, info)
        pools["share", s] = sibling(done(sib))
        shares.append((own, pools["share", s]))

    (send_x,) = pack(x_rows, info, block_count, dp, dp)
    done(send_x)
    arrived_x = lax.all_to_all(send_x, "dp", split_axis=0, concat_axis=0, tiled=True)
    send_g = pack(after(g_rows), info, block_count, dp, 2)
    done(send_g[0])
    x_own.append(chosen(arrived_x))
    arrived_g = dispatched(after(*send_g))
    x_sib.append(sibling(x_own[0]))
    x_ahead = onward(x_own[0])
    up(0)
    halves_g = crossed_over(arrived_g)
    end = tensor - 1
    for s in range(1, tensor):
        x_ahead = arrive(x_own, x_sib, x_ahead, s < end)
        if s == end:
            g_ahead = onward(after(g_own[0]))
        settle(("x", s - 2))
        up(s)
        if s == 1:
            g_own.append(chosen(*halves_g))
            g_sib.append(sibling(g_own[0]))
        if s == 2:
            settle(("x", 1))
            down(0)
    settle(("x", end - 1))
    share(0)
    for s in range(1, end):
        g_ahead = arrive(g_own, g_sib, g_ahead)
        settle(("share", s - 1), ("x", end) if s > 1 else None, ("g", s - 2))
        down(s)
        settle(("g", 0))
        share(s)

    settle(("g", end - 2))
    first_share = done(add(*after(*shares[1])))
    arrive(g_own, g_sib, g_ahead, False)
    running = onward(lax.optimization_barrier((first_share, g_own[end]))[0])
    columns = done(partner_columns(*after(g_own[end], g_sib[end]), info, chips))
    pools["columns"] = pooled(columns)
    g_there.append((pools["columns"], 0))
    settle(("share", end - 1), ("g", end - 1))
    down(end, False)

    span = d // dp
    near, mine_j = pool_bit(chip, core), other_bits(chip, core)

    def part(r, rows, there, rights, split):
        j = mine_j ^ r
        rows = [after(*rows[0]), *rows[1:]]
        parts = weight_part(
            rows, there, rights, chip_with(j, near, core), j, core, 2 * span, hidden, split
        )
        done(parts[0])
        return list(parts)

    bits = (chips // 2).bit_length() - 1

    def pass_on(parts):
        for k in reversed(range(1, bits)):
            perm = chip_perm(dp, lambda c: 2 << k)
            for r in range(1 << k, 2 << k):
                sent = [lax.ppermute(p, "dp", perm) for p in parts[r]]
                kept = parts.get(r ^ (1 << k))
                parts[r ^ (1 << k)] = [add(*both) for both in zip(kept, sent)] if kept else sent
        flip = lambda c: 2 >> c
        return [lax.ppermute(p, "dp", chip_perm(dp, flip, h == 1)) for h, p in enumerate(parts[1])]

    def core_rows(value, which):
        return lax.dynamic_slice_in_dim(value, which * span, span, 0)

    def finished(kept, parts, sent):
        if 0 in parts:
            kept = [add(*both) for both in zip(kept, parts[0])]
        if len(kept) == 2:
            mine = add(after(kept[0]), sent[0])
            other = add(sibling(kept[1]), sent[1])
        else:
            other = sibling(add(core_rows(kept[0], 1 - core), core_rows(sent[0], 1 - core)))
            mine = add(core_rows(after(kept[0]), core), core_rows(sent[0], core))
        return done(jnp.where(
            core == 0, jnp.concatenate([mine, other], axis=1), jnp.concatenate([other, mine], axis=1)
        ))

    down_sum = (list(zip(g_own, g_sib)), g_there, act, True)
    up_sum = (list(zip(x_own, x_sib)), x_there, pre, True)
    away = list(reversed(range(1, chips // 2)))
    settle("columns")
    down_parts = {r: part(r, *down_sum) for r in away}
    down_sent = pass_on(down_parts)
    settle(("g", end))
    for s in range(2, end):
        running = onward(done(add(*after(*shares[s]), running)))
    share(end)
    last.append(down_sent[0])
    up_parts = {r: part(r, *up_sum) for r in away}
    up_sent = pass_on(up_parts)
    running = onward(done(add(*after(*shares[end]), running)))
    last.extend(down_sent)
    down_kept = part(0, *down_sum)
    up_kept = part(0, *up_sum)
    input_grad = done(add(*after(*shares[0]), running)).reshape(OWNB, here, d)
    down_grad = finished(down_kept, down_parts, down_sent)
    up_grad = finished(up_kept, up_parts, up_sent)
    return input_grad, up_grad, down_grad


def solution(mesh):
    placed = (
        P("dp", "tensor", None),
        P("dp", "tensor", None),
        P(None, "tensor"),
        P(None, "tensor"),
        P(),
        P(),
    )
    return jax.shard_map(
        local,
        mesh=mesh,
        in_specs=placed,
        out_specs=(P("dp", "tensor", None), P("dp", "tensor"), P("dp", "tensor")),
        check_vma=False,
    )
```

```python
import functools

import jax
import jax.numpy as jnp
from jax import lax
from jax.experimental import pallas as pl
from jax.experimental.pallas import tpu as pltpu
from jax.sharding import PartitionSpec as P

OWNB = 4
BF16 = jnp.bfloat16
F32 = jnp.float32
VMEM_LIMIT = 60 * 1024 * 1024
SHORT = pl.CostEstimate(flops=1, bytes_accessed=1, transcendentals=0)


def chip_with(j, v, core):
    return jnp.where(core == 0, 2 * j + v, ((j >> 1) << 2) + 2 * v + (j & 1))


def pool_bit(chip, core):
    return jnp.where(core == 0, chip & 1, (chip >> 1) & 1)


def other_bits(chip, core):
    return jnp.where(core == 0, chip >> 1, ((chip >> 2) << 1) + (chip & 1))


def chip_perm(dp, flip, cross=False):
    return [(i, 2 * ((i >> 1) ^ flip(i & 1)) + ((i & 1) ^ int(cross))) for i in range(dp)]


def start_of(count, source, dp):
    total = jnp.int32(0)
    for j in range(dp):
        total = total + jnp.where(source > j, count[j], 0)
    return total


def source_of(count, number, dp):
    end, source = jnp.int32(0), jnp.int32(0)
    for j in range(dp):
        end = end + count[j]
        source = source + jnp.where(end <= number, 1, 0)
    return source


def run(copies):
    for copy in copies:
        copy.start()
    for copy in copies:
        copy.wait()


def pack_body(info, count, rows, *refs, slots):
    outs, sems = refs[:-1], refs[-1]
    blocks = rows.shape[0]
    dp = slots * len(outs)
    start = start_of(count, info[0], dp)
    copies = []
    for k in range(dp):
        f, slot = divmod(k, slots)
        owner = k if len(outs) == 1 else 2 * ((info[0] >> 1) ^ f) + slot
        block = jnp.minimum(lax.rem(owner + OWNB * dp - start, dp), blocks - 1)
        copies.append(pltpu.make_async_copy(rows.at[block], outs[f].at[slot], sems.at[k]))
    run(copies)


def pack(rows, info, count, dp, slots):
    _, here, d = rows.shape
    shape = jax.ShapeDtypeStruct((slots, here, d), BF16)
    spec = pl.BlockSpec((slots, here, d), lambda n, i, c: (0, 0, 0))
    return pl.pallas_call(
        functools.partial(pack_body, slots=slots),
        out_shape=(shape,) * (dp // slots),
        grid_spec=pltpu.PrefetchScalarGridSpec(
            num_scalar_prefetch=2,
            grid=(1,),
            in_specs=[pl.BlockSpec(memory_space=pl.ANY)],
            out_specs=(spec,) * (dp // slots),
            scratch_shapes=[pltpu.SemaphoreType.DMA((dp,))],
        ),
        compiler_params=pltpu.CompilerParams(vmem_limit_bytes=VMEM_LIMIT),
        cost_estimate=SHORT,
    )(info, count, rows)


def across_body(info, *refs):
    arrived, (here, away, sems) = refs[:-3], refs[-3:]
    core = info[0] & 1
    copies = []
    for f, a in enumerate(arrived):
        copies.append(pltpu.make_async_copy(a.at[1 - core], away.at[f], sems.at[2 * f]))
        copies.append(pltpu.make_async_copy(a.at[core], here.at[f], sems.at[2 * f + 1]))
    run(copies)


def across(arrived, info):
    chips = len(arrived)
    _, here, d = arrived[0].shape
    shape = jax.ShapeDtypeStruct((chips, here, d), BF16)
    spec = pl.BlockSpec((chips, here, d), lambda n, i: (0, 0, 0))
    return pl.pallas_call(
        across_body,
        out_shape=(shape, shape),
        grid_spec=pltpu.PrefetchScalarGridSpec(
            num_scalar_prefetch=1,
            grid=(1,),
            in_specs=[pl.BlockSpec(memory_space=pl.ANY)] * chips,
            out_specs=(spec, spec),
            scratch_shapes=[pltpu.SemaphoreType.DMA((2 * chips,))],
        ),
        compiler_params=pltpu.CompilerParams(vmem_limit_bytes=VMEM_LIMIT),
        cost_estimate=SHORT,
    )(info, *arrived)


def select_body(info, count, patches, *refs):
    arrived, (out, sems) = refs[:-2], refs[-2:]
    dp, here = len(arrived) * arrived[0].shape[0], out.shape[1]
    core, chip = info[0] & 1, info[0] >> 1
    filled = []
    for m in range(OWNB):
        number = info[0] + dp * m
        source = source_of(count, number, dp)
        filled.append(patches[source, number - start_of(count, source, dp)])
        if len(arrived) == 1:
            pltpu.make_async_copy(arrived[0].at[source], out.at[m], sems.at[m]).start()
        else:
            own, sib = arrived
            f = (source >> 1) ^ chip
            same = (source & 1) == core

            @pl.when(same)
            def _():
                pltpu.make_async_copy(own.at[f], out.at[m], sems.at[m]).start()

            @pl.when(jnp.logical_not(same))
            def _():
                pltpu.make_async_copy(sib.at[f], out.at[m], sems.at[m]).start()

    row = lax.broadcasted_iota(jnp.int32, out.shape[1:], 0) + info[1] * here
    for m in range(OWNB):
        pltpu.make_async_copy(arrived[0].at[0], out.at[m], sems.at[m]).wait()
        out[m] = jnp.where(row < filled[m], out[m].astype(F32), 0.0).astype(out.dtype)


def select(arrived, info, count, patches):
    _, here, d = arrived[0].shape
    return pl.pallas_call(
        select_body,
        out_shape=jax.ShapeDtypeStruct((OWNB, here, d), BF16),
        grid_spec=pltpu.PrefetchScalarGridSpec(
            num_scalar_prefetch=3,
            grid=(1,),
            in_specs=[pl.BlockSpec(memory_space=pl.ANY)] * len(arrived),
            out_specs=pl.BlockSpec((OWNB, here, d), lambda n, i, c, p: (0, 0, 0)),
            scratch_shapes=[pltpu.SemaphoreType.DMA((OWNB,))],
        ),
        compiler_params=pltpu.CompilerParams(vmem_limit_bytes=VMEM_LIMIT),
        cost_estimate=SHORT,
    )(info, count, patches, *arrived)


def block_of(size, most):
    for width in range(most, 0, -128):
        if size % width == 0:
            return width
    return size


def load_rows(own, sib, rows):
    half = own.shape[0]
    rows[:half] = own[...]
    rows[half:] = sib[...]


def put_partner_columns(info, rows, out, hidden, chips):
    core, chip = info[0] & 1, info[0] >> 1
    width = rows.shape[1] // chips
    away = 1 - pool_bit(chip, core)
    for j in range(chips // 2):
        at = pl.multiple_of(chip_with(j, away, core) * width, 128)
        out[:, hidden + j * width:hidden + (j + 1) * width] = rows[:, pl.ds(at, width)]


def up_body(info, own, sib, w, out, slope, rows, *, hidden, chips):
    n = pl.program_id(0)

    @pl.when(n == 0)
    def _():
        load_rows(own, sib, rows)
        put_partner_columns(info, rows, out, hidden, chips)

    pre_act = jnp.dot(rows[...], w[...], preferred_element_type=F32)
    cdf = 0.5 * (1.0 + lax.erf(pre_act * 0.7071067811865476))
    density = jnp.exp(-0.5 * pre_act * pre_act) * 0.3989422804014327
    width = w.shape[1]
    out[:, pl.ds(pl.multiple_of(n * width, 128), width)] = (pre_act * cdf).astype(out.dtype)
    slope[...] = (cdf + pre_act * density).astype(slope.dtype)


def down_body(info, own, sib, w, slope, out, rows, *, hidden, chips):
    n = pl.program_id(0)

    @pl.when(n == 0)
    def _():
        load_rows(own, sib, rows)
        if out.shape[1] > hidden:
            put_partner_columns(info, rows, out, hidden, chips)

    act_grad = jnp.dot(rows[...], w[...], preferred_element_type=F32)
    width = w.shape[1]
    out[:, pl.ds(pl.multiple_of(n * width, 128), width)] = (act_grad * slope[...]).astype(out.dtype)


def columns_body(info, own, sib, out, rows, *, chips):
    load_rows(own, sib, rows)
    put_partner_columns(info, rows, out, 0, chips)


def partner_columns(own, sib, info, chips):
    half, d = own.shape
    spec = pl.BlockSpec((half, d), lambda n, i: (0, 0))
    return pl.pallas_call(
        functools.partial(columns_body, chips=chips),
        out_shape=jax.ShapeDtypeStruct((2 * half, d // 2), BF16),
        grid_spec=pltpu.PrefetchScalarGridSpec(
            num_scalar_prefetch=1,
            grid=(1,),
            in_specs=[spec, spec],
            out_specs=pl.BlockSpec((2 * half, d // 2), lambda n, i: (0, 0)),
            scratch_shapes=[pltpu.VMEM((2 * half, d), BF16)],
        ),
        compiler_params=pltpu.CompilerParams(vmem_limit_bytes=VMEM_LIMIT),
        cost_estimate=SHORT,
    )(info, own, sib)


def forward(own, sib, w, info, chips, slope=None, with_columns=True):
    half, d = own.shape
    hidden = w.shape[1] // 2
    width = block_of(hidden, 768)
    steps = hidden // width
    total = hidden + (d // 2 if with_columns else 0)
    out_shape = jax.ShapeDtypeStruct((2 * half, total), BF16)
    out_specs = pl.BlockSpec((2 * half, total), lambda n, i: (0, 0))
    slope_spec = pl.BlockSpec((2 * half, width), lambda n, i: (0, n))
    rows_spec = pl.BlockSpec((half, d), lambda n, i: (0, 0))
    w_spec = pl.BlockSpec((d, width), lambda n, i: (0, (i[0] & 1) * steps + n))
    in_specs = [rows_spec, rows_spec, w_spec]
    operands = [own, sib, w]
    if slope is None:
        body = up_body
        out_shape = (out_shape, jax.ShapeDtypeStruct((2 * half, hidden), BF16))
        out_specs = (out_specs, slope_spec)
    else:
        body = down_body
        in_specs.append(slope_spec)
        operands.append(slope)
    return pl.pallas_call(
        functools.partial(body, hidden=hidden, chips=chips),
        out_shape=out_shape,
        grid_spec=pltpu.PrefetchScalarGridSpec(
            num_scalar_prefetch=1,
            grid=(steps,),
            in_specs=in_specs,
            out_specs=out_specs,
            scratch_shapes=[pltpu.VMEM((2 * half, d), BF16)],
        ),
        compiler_params=pltpu.CompilerParams(vmem_limit_bytes=VMEM_LIMIT),
        cost_estimate=SHORT,
    )(info, *operands)


def input_body(info, pre, w, own, sib):
    value = lax.dot_general(pre[...], w[...], (((1,), (1,)), ((), ())), preferred_element_type=F32)
    half = own.shape[0]
    own[...] = value[:half].astype(own.dtype)
    sib[...] = value[half:].astype(sib.dtype)


def input_part(pre, w, info):
    rows = pre.shape[0]
    d, hidden = w.shape[0], w.shape[1] // 2
    width = block_of(d, 1536)
    shape = jax.ShapeDtypeStruct((rows // 2, d), BF16)
    spec = pl.BlockSpec((rows // 2, width), lambda n, i: (0, n))
    return pl.pallas_call(
        input_body,
        out_shape=(shape, shape),
        grid_spec=pltpu.PrefetchScalarGridSpec(
            num_scalar_prefetch=1,
            grid=(d // width,),
            in_specs=[
                pl.BlockSpec((rows, hidden), lambda n, i: (0, 0)),
                pl.BlockSpec((width, hidden), lambda n, i: (n, i[0] & 1)),
            ],
            out_specs=(spec, spec),
        ),
        compiler_params=pltpu.CompilerParams(vmem_limit_bytes=VMEM_LIMIT),
        cost_estimate=SHORT,
    )(info, pre, w)


def weight_body(at, *refs, begins, width, block):
    slots = len(begins)
    ins, outs, (left, right, total, left_sems, right_sems) = refs[:5 * slots], refs[5 * slots:-5], refs[-5:]
    half, hidden = ins[0].shape[0], right.shape[1]
    copies = []
    for s in range(slots):
        own, sib, there, mine, theirs = ins[5 * s:5 * s + 5]
        first = 4 * s * half
        for k, (rows, column, to, size) in enumerate((
            (own, at[0] * width, first, half),
            (sib, at[0] * width, first + half, half),
            (there, begins[s] + at[1] * width, first + 2 * half, 2 * half),
        )):
            source = rows.at[:, pl.ds(pl.multiple_of(column, 128), width)]
            copies.append(pltpu.make_async_copy(source, left.at[pl.ds(to, size)], left_sems.at[3 * s + k]))
        for k, hidden_side in enumerate((mine, theirs)):
            source = hidden_side.at[:, pl.ds(0, hidden)]
            to = right.at[pl.ds(first + 2 * k * half, 2 * half)]
            copies.append(pltpu.make_async_copy(source, to, right_sems.at[2 * s + k]))
    for copy in copies:
        copy.start()
    middle = slots // 2
    dims = (((0,), (0,)), ((), ()))
    columns = [slice(n, n + block) for n in range(0, hidden, block)]
    for copy in copies[:5 * middle]:
        copy.wait()
    early = 4 * middle * half
    for cut in columns:
        total[:, cut] = lax.dot_general(left[:early], right[:early, cut], dims, preferred_element_type=F32)
    for copy in copies[5 * middle:]:
        copy.wait()
    span = width // 2
    is_first = at[2] == 0
    for cut in columns:
        value = total[:, cut] + lax.dot_general(left[early:], right[early:, cut], dims, preferred_element_type=F32)
        if len(outs) == 1:
            outs[0][:, cut] = value.astype(outs[0].dtype)
        else:
            low, high = value[:span], value[span:]
            outs[0][:, cut] = jnp.where(is_first, low, high).astype(outs[0].dtype)
            outs[1][:, cut] = jnp.where(is_first, high, low).astype(outs[1].dtype)


def weight_part(rows, there_rows, rights, own_at, there_at, core, width, hidden, split):
    slots, size = len(rows), 2 * rows[0][0].shape[0]
    at = jnp.stack([own_at, there_at, core]).astype(jnp.int32)
    block = block_of(hidden, 512)
    operands = []
    for (own, sib), (there, _), (mine, theirs) in zip(rows, there_rows, rights):
        operands += [own, sib, there, mine, theirs]
    pieces = 2 if split else 1
    shape = jax.ShapeDtypeStruct((width // pieces, hidden), BF16)
    spec = pl.BlockSpec((width // pieces, hidden), lambda n, a: (0, 0))
    return pl.pallas_call(
        functools.partial(weight_body, begins=[begin for _, begin in there_rows], width=width, block=block),
        out_shape=(shape,) * pieces,
        grid_spec=pltpu.PrefetchScalarGridSpec(
            num_scalar_prefetch=1,
            grid=(1,),
            in_specs=[pl.BlockSpec(memory_space=pl.ANY)] * len(operands),
            out_specs=(spec,) * pieces,
            scratch_shapes=[
                pltpu.VMEM((2 * slots * size, width), BF16),
                pltpu.VMEM((2 * slots * size, hidden), BF16),
                pltpu.VMEM((width, hidden), F32),
                pltpu.SemaphoreType.DMA((3 * slots,)),
                pltpu.SemaphoreType.DMA((2 * slots,)),
            ],
        ),
        compiler_params=pltpu.CompilerParams(vmem_limit_bytes=VMEM_LIMIT),
        cost_estimate=SHORT,
    )(at, *operands)


def add(*values):
    return sum(v.astype(F32) for v in values).astype(BF16)


def local(x_rows, g_rows, w_up, w_down_t, block_count, patches):
    dp, tensor = lax.axis_size("dp"), lax.axis_size("tensor")
    chips = dp // 2
    me, plane = lax.axis_index("dp"), lax.axis_index("tensor")
    chip, core = me >> 1, me & 1
    info = jnp.stack([me, plane]).astype(jnp.int32)
    here, d = x_rows.shape[1:]
    hidden = w_up.shape[1] // 2
    ring = [(i, (i + 1) % tensor) for i in range(tensor)]
    to_sibling = [(i, i ^ 1) for i in range(dp)]
    to_pool = chip_perm(dp, lambda c: 1 << c)
    last = []

    def after(*values):
        out = lax.optimization_barrier((*values, *last))[:len(values)]
        return out if len(out) > 1 else out[0]

    def done(value):
        last[:] = [value]
        return value

    def onward(piece):
        return lax.ppermute(piece, "tensor", ring)

    def sibling(piece):
        return lax.ppermute(piece, "dp", to_sibling)

    def pooled(piece):
        return lax.ppermute(piece, "dp", to_pool)

    def dispatched(packed):
        return [packed[0]] + [
            lax.ppermute(p, "dp", [(i, i ^ (2 * f)) for i in range(dp)]) for f, p in enumerate(packed) if f
        ]

    def crossed_over(arrived):
        own, away = across(list(after(*arrived)), info)
        return own, sibling(done(away))

    def chosen(*arrived):
        arrived = after(*arrived) if len(arrived) > 1 else [after(*arrived)]
        return done(select(arrived, info, block_count, patches)).reshape(OWNB * here, d)

    def arrive(own, sib, ahead, further=True):
        piece = after(ahead)
        own.append(piece)
        sib.append(sibling(piece))
        return onward(piece) if further else None

    x_own, x_sib, x_there = [], [], []
    g_own, g_sib, g_there = [], [], []
    act, slope, pre, shares, pools = [], [], [], [], {}

    def settle(*names):
        last.extend(pools[name] for name in names if name in pools)

    def up(s):
        mine, slope_s = forward(*after(x_own[s], x_sib[s]), w_up, info, chips)
        theirs = pools["x", s] = pooled(done(mine))
        x_there.append((theirs, hidden))
        slope.append(slope_s)
        act.append((mine, theirs))

    def down(s, with_columns=True):
        mine = forward(*after(g_own[s], g_sib[s]), w_down_t, info, chips, slope[s], with_columns)
        theirs = pools["g", s] = pooled(done(mine))
        if with_columns:
            g_there.append((theirs, hidden))
        pre.append((mine, theirs))

    def share(s):
        own, sib = input_part(after(pre[s][0]), w_up, info)
        pools["share", s] = sibling(done(sib))
        shares.append((own, pools["share", s]))

    (send_x,) = pack(x_rows, info, block_count, dp, dp)
    done(send_x)
    arrived_x = lax.all_to_all(send_x, "dp", split_axis=0, concat_axis=0, tiled=True)
    send_g = pack(after(g_rows), info, block_count, dp, 2)
    done(send_g[0])
    x_own.append(chosen(arrived_x))
    arrived_g = dispatched(after(*send_g))
    x_sib.append(sibling(x_own[0]))
    x_ahead = onward(x_own[0])
    up(0)
    halves_g = crossed_over(arrived_g)
    end = tensor - 1
    for s in range(1, tensor):
        x_ahead = arrive(x_own, x_sib, x_ahead, s < end)
        if s == end:
            g_ahead = onward(after(g_own[0]))
        settle(("x", s - 2))
        up(s)
        if s == 1:
            g_own.append(chosen(*halves_g))
            g_sib.append(sibling(g_own[0]))
        if s == 2:
            settle(("x", 1))
            down(0)
    settle(("x", end - 1))
    share(0)
    for s in range(1, end):
        g_ahead = arrive(g_own, g_sib, g_ahead)
        settle(("share", s - 1), ("x", end) if s > 1 else None, ("g", s - 2))
        down(s)
        settle(("g", 0))
        share(s)

    settle(("g", end - 2))
    first_share = done(add(*after(*shares[1])))
    arrive(g_own, g_sib, g_ahead, False)
    running = onward(lax.optimization_barrier((first_share, g_own[end]))[0])
    columns = done(partner_columns(*after(g_own[end], g_sib[end]), info, chips))
    pools["columns"] = pooled(columns)
    g_there.append((pools["columns"], 0))
    settle(("share", end - 1), ("g", end - 1))
    down(end, False)

    span = d // dp
    near, mine_j = pool_bit(chip, core), other_bits(chip, core)

    def part(r, rows, there, rights, split):
        j = mine_j ^ r
        rows = [after(*rows[0]), *rows[1:]]
        parts = weight_part(
            rows, there, rights, chip_with(j, near, core), j, core, 2 * span, hidden, split
        )
        done(parts[0])
        return list(parts)

    bits = (chips // 2).bit_length() - 1

    def pass_on(parts):
        for k in reversed(range(1, bits)):
            perm = chip_perm(dp, lambda c: 2 << k)
            for r in range(1 << k, 2 << k):
                sent = [lax.ppermute(p, "dp", perm) for p in parts[r]]
                kept = parts.get(r ^ (1 << k))
                parts[r ^ (1 << k)] = [add(*both) for both in zip(kept, sent)] if kept else sent
        flip = lambda c: 2 >> c
        return [lax.ppermute(p, "dp", chip_perm(dp, flip, h == 1)) for h, p in enumerate(parts[1])]

    def core_rows(value, which):
        return lax.dynamic_slice_in_dim(value, which * span, span, 0)

    def finished(kept, parts, sent):
        if 0 in parts:
            kept = [add(*both) for both in zip(kept, parts[0])]
        if len(kept) == 2:
            mine = add(after(kept[0]), sent[0])
            other = add(sibling(kept[1]), sent[1])
        else:
            other = sibling(add(core_rows(kept[0], 1 - core), core_rows(sent[0], 1 - core)))
            mine = add(core_rows(after(kept[0]), core), core_rows(sent[0], core))
        return done(jnp.where(
            core == 0, jnp.concatenate([mine, other], axis=1), jnp.concatenate([other, mine], axis=1)
        ))

    down_sum = (list(zip(g_own, g_sib)), g_there, act, True)
    up_sum = (list(zip(x_own, x_sib)), x_there, pre, True)
    away = list(reversed(range(1, chips // 2)))
    settle("columns")
    last.append(running)
    down_parts = {r: part(r, *down_sum) for r in away}
    down_sent = pass_on(down_parts)
    settle(("g", end))
    for s in range(2, end):
        running = onward(done(add(*after(*shares[s]), running)))
    share(end)
    last.append(down_sent[0])
    up_parts = {r: part(r, *up_sum) for r in away}
    up_sent = pass_on(up_parts)
    down_kept = part(0, *down_sum)
    last.append(down_sent[1])
    running = onward(done(add(*after(*shares[end]), running)))
    last.append(up_sent[0])
    up_kept = part(0, *up_sum)
    last.append(up_sent[1])
    down_grad = finished(down_kept, down_parts, down_sent)
    up_grad = finished(up_kept, up_parts, up_sent)
    input_grad = add(*after(*shares[0]), running).reshape(OWNB, here, d)
    return input_grad, up_grad, down_grad


def solution(mesh):
    placed = (
        P("dp", "tensor", None),
        P("dp", "tensor", None),
        P(None, "tensor"),
        P(None, "tensor"),
        P(),
        P(),
    )
    return jax.shard_map(
        local,
        mesh=mesh,
        in_specs=placed,
        out_specs=(P("dp", "tensor", None), P("dp", "tensor"), P("dp", "tensor")),
        check_vma=False,
    )
```

```python
import functools

import jax
import jax.numpy as jnp
from jax import lax
from jax.experimental import pallas as pl
from jax.experimental.pallas import tpu as pltpu
from jax.sharding import PartitionSpec as P

OWNB = 4
BF16 = jnp.bfloat16
F32 = jnp.float32
VMEM_LIMIT = 64 * 1024 * 1024
SHORT = pl.CostEstimate(flops=1, bytes_accessed=1, transcendentals=0)


def chip_with(j, v, core):
    return jnp.where(core == 0, 2 * j + v, ((j >> 1) << 2) + 2 * v + (j & 1))


def pool_bit(chip, core):
    return jnp.where(core == 0, chip & 1, (chip >> 1) & 1)


def other_bits(chip, core):
    return jnp.where(core == 0, chip >> 1, ((chip >> 2) << 1) + (chip & 1))


def chip_perm(dp, flip, cross=False):
    return [(i, 2 * ((i >> 1) ^ flip(i & 1)) + ((i & 1) ^ int(cross))) for i in range(dp)]


def start_of(count, source, dp):
    total = jnp.int32(0)
    for j in range(dp):
        total = total + jnp.where(source > j, count[j], 0)
    return total


def source_of(count, number, dp):
    end, source = jnp.int32(0), jnp.int32(0)
    for j in range(dp):
        end = end + count[j]
        source = source + jnp.where(end <= number, 1, 0)
    return source


def run(copies):
    for copy in copies:
        copy.start()
    for copy in copies:
        copy.wait()


def pack_body(info, count, rows, *refs, slots):
    outs, sems = refs[:-1], refs[-1]
    blocks = rows.shape[0]
    dp = slots * len(outs)
    start = start_of(count, info[0], dp)
    copies = []
    for k in range(dp):
        f, slot = divmod(k, slots)
        owner = k if len(outs) == 1 else 2 * ((info[0] >> 1) ^ f) + slot
        block = jnp.minimum(lax.rem(owner + OWNB * dp - start, dp), blocks - 1)
        copies.append(pltpu.make_async_copy(rows.at[block], outs[f].at[slot], sems.at[k]))
    run(copies)


def pack(rows, info, count, dp, slots):
    _, here, d = rows.shape
    shape = jax.ShapeDtypeStruct((slots, here, d), BF16)
    spec = pl.BlockSpec((slots, here, d), lambda n, i, c: (0, 0, 0))
    return pl.pallas_call(
        functools.partial(pack_body, slots=slots),
        out_shape=(shape,) * (dp // slots),
        grid_spec=pltpu.PrefetchScalarGridSpec(
            num_scalar_prefetch=2,
            grid=(1,),
            in_specs=[pl.BlockSpec(memory_space=pl.ANY)],
            out_specs=(spec,) * (dp // slots),
            scratch_shapes=[pltpu.SemaphoreType.DMA((dp,))],
        ),
        compiler_params=pltpu.CompilerParams(vmem_limit_bytes=VMEM_LIMIT),
        cost_estimate=SHORT,
    )(info, count, rows)


def across_body(info, *refs):
    arrived, (here, away, sems) = refs[:-3], refs[-3:]
    core = info[0] & 1
    copies = []
    for f, a in enumerate(arrived):
        copies.append(pltpu.make_async_copy(a.at[1 - core], away.at[f], sems.at[2 * f]))
        copies.append(pltpu.make_async_copy(a.at[core], here.at[f], sems.at[2 * f + 1]))
    run(copies)


def across(arrived, info):
    chips = len(arrived)
    _, here, d = arrived[0].shape
    shape = jax.ShapeDtypeStruct((chips, here, d), BF16)
    spec = pl.BlockSpec((chips, here, d), lambda n, i: (0, 0, 0))
    return pl.pallas_call(
        across_body,
        out_shape=(shape, shape),
        grid_spec=pltpu.PrefetchScalarGridSpec(
            num_scalar_prefetch=1,
            grid=(1,),
            in_specs=[pl.BlockSpec(memory_space=pl.ANY)] * chips,
            out_specs=(spec, spec),
            scratch_shapes=[pltpu.SemaphoreType.DMA((2 * chips,))],
        ),
        compiler_params=pltpu.CompilerParams(vmem_limit_bytes=VMEM_LIMIT),
        cost_estimate=SHORT,
    )(info, *arrived)


def select_body(info, count, patches, *refs):
    arrived, (out, sems) = refs[:-2], refs[-2:]
    dp, here = len(arrived) * arrived[0].shape[0], out.shape[1]
    core, chip = info[0] & 1, info[0] >> 1
    filled = []
    for m in range(OWNB):
        number = info[0] + dp * m
        source = source_of(count, number, dp)
        filled.append(patches[source, number - start_of(count, source, dp)])
        if len(arrived) == 1:
            pltpu.make_async_copy(arrived[0].at[source], out.at[m], sems.at[m]).start()
        else:
            own, sib = arrived
            f = (source >> 1) ^ chip
            same = (source & 1) == core

            @pl.when(same)
            def _():
                pltpu.make_async_copy(own.at[f], out.at[m], sems.at[m]).start()

            @pl.when(jnp.logical_not(same))
            def _():
                pltpu.make_async_copy(sib.at[f], out.at[m], sems.at[m]).start()

    row = lax.broadcasted_iota(jnp.int32, out.shape[1:], 0) + info[1] * here
    for m in range(OWNB):
        pltpu.make_async_copy(arrived[0].at[0], out.at[m], sems.at[m]).wait()
        out[m] = jnp.where(row < filled[m], out[m].astype(F32), 0.0).astype(out.dtype)


def select(arrived, info, count, patches):
    _, here, d = arrived[0].shape
    return pl.pallas_call(
        select_body,
        out_shape=jax.ShapeDtypeStruct((OWNB, here, d), BF16),
        grid_spec=pltpu.PrefetchScalarGridSpec(
            num_scalar_prefetch=3,
            grid=(1,),
            in_specs=[pl.BlockSpec(memory_space=pl.ANY)] * len(arrived),
            out_specs=pl.BlockSpec((OWNB, here, d), lambda n, i, c, p: (0, 0, 0)),
            scratch_shapes=[pltpu.SemaphoreType.DMA((OWNB,))],
        ),
        compiler_params=pltpu.CompilerParams(vmem_limit_bytes=VMEM_LIMIT),
        cost_estimate=SHORT,
    )(info, count, patches, *arrived)


def block_of(size, most):
    for width in range(most, 0, -128):
        if size % width == 0:
            return width
    return size


def load_rows(own, sib, rows):
    half = own.shape[0]
    rows[:half] = own[...]
    rows[half:] = sib[...]


def put_partner_columns(info, rows, out, hidden, chips):
    core, chip = info[0] & 1, info[0] >> 1
    width = rows.shape[1] // chips
    away = 1 - pool_bit(chip, core)
    for j in range(chips // 2):
        at = pl.multiple_of(chip_with(j, away, core) * width, 128)
        out[:, hidden + j * width:hidden + (j + 1) * width] = rows[:, pl.ds(at, width)]


def up_body(info, own, sib, w, out, slope, rows, *, hidden, chips):
    n = pl.program_id(0)

    @pl.when(n == 0)
    def _():
        load_rows(own, sib, rows)
        put_partner_columns(info, rows, out, hidden, chips)

    pre_act = jnp.dot(rows[...], w[...], preferred_element_type=F32)
    cdf = 0.5 * (1.0 + lax.erf(pre_act * 0.7071067811865476))
    density = jnp.exp(-0.5 * pre_act * pre_act) * 0.3989422804014327
    width = w.shape[1]
    out[:, pl.ds(pl.multiple_of(n * width, 128), width)] = (pre_act * cdf).astype(out.dtype)
    slope[...] = (cdf + pre_act * density).astype(slope.dtype)


def down_body(info, own, sib, w, slope, out, rows, *, hidden, chips):
    n = pl.program_id(0)

    @pl.when(n == 0)
    def _():
        load_rows(own, sib, rows)
        if out.shape[1] > hidden:
            put_partner_columns(info, rows, out, hidden, chips)

    act_grad = jnp.dot(rows[...], w[...], preferred_element_type=F32)
    width = w.shape[1]
    out[:, pl.ds(pl.multiple_of(n * width, 128), width)] = (act_grad * slope[...]).astype(out.dtype)


def columns_body(info, own, sib, out, rows, *, chips):
    load_rows(own, sib, rows)
    put_partner_columns(info, rows, out, 0, chips)


def partner_columns(own, sib, info, chips):
    half, d = own.shape
    spec = pl.BlockSpec((half, d), lambda n, i: (0, 0))
    return pl.pallas_call(
        functools.partial(columns_body, chips=chips),
        out_shape=jax.ShapeDtypeStruct((2 * half, d // 2), BF16),
        grid_spec=pltpu.PrefetchScalarGridSpec(
            num_scalar_prefetch=1,
            grid=(1,),
            in_specs=[spec, spec],
            out_specs=pl.BlockSpec((2 * half, d // 2), lambda n, i: (0, 0)),
            scratch_shapes=[pltpu.VMEM((2 * half, d), BF16)],
        ),
        compiler_params=pltpu.CompilerParams(vmem_limit_bytes=VMEM_LIMIT),
        cost_estimate=SHORT,
    )(info, own, sib)


def forward(own, sib, w, info, chips, slope=None, with_columns=True):
    half, d = own.shape
    hidden = w.shape[1] // 2
    width = block_of(hidden, 768)
    steps = hidden // width
    total = hidden + (d // 2 if with_columns else 0)
    out_shape = jax.ShapeDtypeStruct((2 * half, total), BF16)
    out_specs = pl.BlockSpec((2 * half, total), lambda n, i: (0, 0))
    slope_spec = pl.BlockSpec((2 * half, width), lambda n, i: (0, n))
    rows_spec = pl.BlockSpec((half, d), lambda n, i: (0, 0))
    w_spec = pl.BlockSpec((d, width), lambda n, i: (0, (i[0] & 1) * steps + n))
    in_specs = [rows_spec, rows_spec, w_spec]
    operands = [own, sib, w]
    if slope is None:
        body = up_body
        out_shape = (out_shape, jax.ShapeDtypeStruct((2 * half, hidden), BF16))
        out_specs = (out_specs, slope_spec)
    else:
        body = down_body
        in_specs.append(slope_spec)
        operands.append(slope)
    return pl.pallas_call(
        functools.partial(body, hidden=hidden, chips=chips),
        out_shape=out_shape,
        grid_spec=pltpu.PrefetchScalarGridSpec(
            num_scalar_prefetch=1,
            grid=(steps,),
            in_specs=in_specs,
            out_specs=out_specs,
            scratch_shapes=[pltpu.VMEM((2 * half, d), BF16)],
        ),
        compiler_params=pltpu.CompilerParams(vmem_limit_bytes=VMEM_LIMIT),
        cost_estimate=SHORT,
    )(info, *operands)


def input_body(info, pre, w, own, sib):
    value = lax.dot_general(pre[...], w[...], (((1,), (1,)), ((), ())), preferred_element_type=F32)
    half = own.shape[0]
    own[...] = value[:half].astype(own.dtype)
    sib[...] = value[half:].astype(sib.dtype)


def input_part(pre, w, info):
    rows = pre.shape[0]
    d, hidden = w.shape[0], w.shape[1] // 2
    width = block_of(d, 1536)
    shape = jax.ShapeDtypeStruct((rows // 2, d), BF16)
    spec = pl.BlockSpec((rows // 2, width), lambda n, i: (0, n))
    return pl.pallas_call(
        input_body,
        out_shape=(shape, shape),
        grid_spec=pltpu.PrefetchScalarGridSpec(
            num_scalar_prefetch=1,
            grid=(d // width,),
            in_specs=[
                pl.BlockSpec((rows, hidden), lambda n, i: (0, 0)),
                pl.BlockSpec((width, hidden), lambda n, i: (n, i[0] & 1)),
            ],
            out_specs=(spec, spec),
        ),
        compiler_params=pltpu.CompilerParams(vmem_limit_bytes=VMEM_LIMIT),
        cost_estimate=SHORT,
    )(info, pre, w)


def weight_body(at, *refs, begins, width, block):
    slots = len(begins)
    ins, outs, (left, right, total, left_sems, right_sems) = refs[:5 * slots], refs[5 * slots:-5], refs[-5:]
    half, hidden = ins[0].shape[0], right.shape[1]
    copies = []
    for s in range(slots):
        own, sib, there, mine, theirs = ins[5 * s:5 * s + 5]
        first = 4 * s * half
        for k, (rows, column, to, size) in enumerate((
            (own, at[0] * width, first, half),
            (sib, at[0] * width, first + half, half),
            (there, begins[s] + at[1] * width, first + 2 * half, 2 * half),
        )):
            source = rows.at[:, pl.ds(pl.multiple_of(column, 128), width)]
            copies.append(pltpu.make_async_copy(source, left.at[pl.ds(to, size)], left_sems.at[3 * s + k]))
        for k, hidden_side in enumerate((mine, theirs)):
            source = hidden_side.at[:, pl.ds(0, hidden)]
            to = right.at[pl.ds(first + 2 * k * half, 2 * half)]
            copies.append(pltpu.make_async_copy(source, to, right_sems.at[2 * s + k]))
    for copy in copies:
        copy.start()
    middle = slots // 2
    dims = (((0,), (0,)), ((), ()))
    columns = [slice(n, n + block) for n in range(0, hidden, block)]
    for copy in copies[:5 * middle]:
        copy.wait()
    early = 4 * middle * half
    for cut in columns:
        total[:, cut] = lax.dot_general(left[:early], right[:early, cut], dims, preferred_element_type=F32)
    for copy in copies[5 * middle:]:
        copy.wait()
    span = width // 2
    is_first = at[2] == 0
    for cut in columns:
        value = total[:, cut] + lax.dot_general(left[early:], right[early:, cut], dims, preferred_element_type=F32)
        if len(outs) == 1:
            outs[0][:, cut] = value.astype(outs[0].dtype)
        else:
            low, high = value[:span], value[span:]
            outs[0][:, cut] = jnp.where(is_first, low, high).astype(outs[0].dtype)
            outs[1][:, cut] = jnp.where(is_first, high, low).astype(outs[1].dtype)


def weight_part(rows, there_rows, rights, own_at, there_at, core, width, hidden, split):
    slots, size = len(rows), 2 * rows[0][0].shape[0]
    at = jnp.stack([own_at, there_at, core]).astype(jnp.int32)
    block = block_of(hidden, 512)
    operands = []
    for (own, sib), (there, _), (mine, theirs) in zip(rows, there_rows, rights):
        operands += [own, sib, there, mine, theirs]
    pieces = 2 if split else 1
    shape = jax.ShapeDtypeStruct((width // pieces, hidden), BF16)
    spec = pl.BlockSpec((width // pieces, hidden), lambda n, a: (0, 0))
    return pl.pallas_call(
        functools.partial(weight_body, begins=[begin for _, begin in there_rows], width=width, block=block),
        out_shape=(shape,) * pieces,
        grid_spec=pltpu.PrefetchScalarGridSpec(
            num_scalar_prefetch=1,
            grid=(1,),
            in_specs=[pl.BlockSpec(memory_space=pl.ANY)] * len(operands),
            out_specs=(spec,) * pieces,
            scratch_shapes=[
                pltpu.VMEM((2 * slots * size, width), BF16),
                pltpu.VMEM((2 * slots * size, hidden), BF16),
                pltpu.VMEM((width, hidden), F32),
                pltpu.SemaphoreType.DMA((3 * slots,)),
                pltpu.SemaphoreType.DMA((2 * slots,)),
            ],
        ),
        compiler_params=pltpu.CompilerParams(vmem_limit_bytes=VMEM_LIMIT),
        cost_estimate=SHORT,
    )(at, *operands)


def add(*values):
    return sum(v.astype(F32) for v in values).astype(BF16)


def local(x_rows, g_rows, w_up, w_down_t, block_count, patches):
    dp, tensor = lax.axis_size("dp"), lax.axis_size("tensor")
    chips = dp // 2
    me, plane = lax.axis_index("dp"), lax.axis_index("tensor")
    chip, core = me >> 1, me & 1
    info = jnp.stack([me, plane]).astype(jnp.int32)
    here, d = x_rows.shape[1:]
    hidden = w_up.shape[1] // 2
    ring = [(i, (i + 1) % tensor) for i in range(tensor)]
    to_sibling = [(i, i ^ 1) for i in range(dp)]
    to_pool = chip_perm(dp, lambda c: 1 << c)
    last = []

    def after(*values):
        out = lax.optimization_barrier((*values, *last))[:len(values)]
        return out if len(out) > 1 else out[0]

    def done(value):
        last[:] = [value]
        return value

    def onward(piece):
        return lax.ppermute(piece, "tensor", ring)

    def sibling(piece):
        return lax.ppermute(piece, "dp", to_sibling)

    def pooled(piece):
        return lax.ppermute(piece, "dp", to_pool)

    def dispatched(packed):
        return [packed[0]] + [
            lax.ppermute(p, "dp", [(i, i ^ (2 * f)) for i in range(dp)]) for f, p in enumerate(packed) if f
        ]

    def crossed_over(arrived):
        own, away = across(list(after(*arrived)), info)
        return own, sibling(done(away))

    def chosen(*arrived):
        arrived = after(*arrived) if len(arrived) > 1 else [after(*arrived)]
        return done(select(arrived, info, block_count, patches)).reshape(OWNB * here, d)

    def arrive(own, sib, ahead, further=True):
        piece = after(ahead)
        own.append(piece)
        sib.append(sibling(piece))
        return onward(piece) if further else None

    x_own, x_sib, x_there = [], [], []
    g_own, g_sib, g_there = [], [], []
    act, slope, pre, shares, pools = [], [], [], [], {}

    def settle(*names):
        last.extend(pools[name] for name in names if name in pools)

    def up(s):
        mine, slope_s = forward(*after(x_own[s], x_sib[s]), w_up, info, chips)
        theirs = pools["x", s] = pooled(done(mine))
        x_there.append((theirs, hidden))
        slope.append(slope_s)
        act.append((mine, theirs))

    def down(s, with_columns=True):
        mine = forward(*after(g_own[s], g_sib[s]), w_down_t, info, chips, slope[s], with_columns)
        theirs = pools["g", s] = pooled(done(mine))
        if with_columns:
            g_there.append((theirs, hidden))
        pre.append((mine, theirs))

    def share(s):
        own, sib = input_part(after(pre[s][0]), w_up, info)
        pools["share", s] = sibling(done(sib))
        shares.append((own, pools["share", s]))

    (send_x,) = pack(x_rows, info, block_count, dp, dp)
    done(send_x)
    arrived_x = lax.all_to_all(send_x, "dp", split_axis=0, concat_axis=0, tiled=True)
    send_g = pack(after(g_rows), info, block_count, dp, 2)
    done(send_g[0])
    x_own.append(chosen(arrived_x))
    arrived_g = dispatched(after(*send_g))
    x_sib.append(sibling(x_own[0]))
    x_ahead = onward(x_own[0])
    up(0)
    halves_g = crossed_over(arrived_g)
    end = tensor - 1
    for s in range(1, tensor):
        x_ahead = arrive(x_own, x_sib, x_ahead, s < end)
        if s == end:
            g_ahead = onward(after(g_own[0]))
        settle(("x", s - 2))
        up(s)
        if s == 1:
            g_own.append(chosen(*halves_g))
            g_sib.append(sibling(g_own[0]))
        if s == 2:
            settle(("x", 1))
            down(0)
    settle(("x", end - 1))
    share(0)
    for s in range(1, end):
        g_ahead = arrive(g_own, g_sib, g_ahead)
        settle(("share", s - 1), ("x", end) if s > 1 else None, ("g", s - 2))
        down(s)
        settle(("g", 0))
        share(s)

    settle(("g", end - 2))
    first_share = done(add(*after(*shares[1])))
    arrive(g_own, g_sib, g_ahead, False)
    running = onward(lax.optimization_barrier((first_share, g_own[end]))[0])
    columns = done(partner_columns(*after(g_own[end], g_sib[end]), info, chips))
    pools["columns"] = pooled(columns)
    g_there.append((pools["columns"], 0))
    settle(("share", end - 1), ("g", end - 1))
    down(end, False)

    span = d // dp
    near, mine_j = pool_bit(chip, core), other_bits(chip, core)

    def part(r, rows, there, rights, split):
        j = mine_j ^ r
        rows = [after(*rows[0]), *rows[1:]]
        parts = weight_part(
            rows, there, rights, chip_with(j, near, core), j, core, 2 * span, hidden, split
        )
        done(parts[0])
        return list(parts)

    bits = (chips // 2).bit_length() - 1

    def pass_on(parts):
        for k in reversed(range(1, bits)):
            perm = chip_perm(dp, lambda c: 2 << k)
            for r in range(1 << k, 2 << k):
                sent = [lax.ppermute(p, "dp", perm) for p in parts[r]]
                kept = parts.get(r ^ (1 << k))
                parts[r ^ (1 << k)] = [add(*both) for both in zip(kept, sent)] if kept else sent
        flip = lambda c: 2 >> c
        return [lax.ppermute(p, "dp", chip_perm(dp, flip, h == 1)) for h, p in enumerate(parts[1])]

    def core_rows(value, which):
        return lax.dynamic_slice_in_dim(value, which * span, span, 0)

    def finished(kept, parts, sent):
        if 0 in parts:
            kept = [add(*both) for both in zip(kept, parts[0])]
        if len(kept) == 2:
            mine = add(after(kept[0]), sent[0])
            other = add(sibling(kept[1]), sent[1])
        else:
            other = sibling(add(core_rows(kept[0], 1 - core), core_rows(sent[0], 1 - core)))
            mine = add(core_rows(after(kept[0]), core), core_rows(sent[0], core))
        return done(jnp.where(
            core == 0, jnp.concatenate([mine, other], axis=1), jnp.concatenate([other, mine], axis=1)
        ))

    down_sum = (list(zip(g_own, g_sib)), g_there, act, True)
    up_sum = (list(zip(x_own, x_sib)), x_there, pre, True)
    away = list(reversed(range(1, chips // 2)))
    settle("columns")
    last.append(running)
    down_parts = {r: part(r, *down_sum) for r in away}
    down_sent = pass_on(down_parts)
    settle(("g", end))
    for s in range(2, end):
        running = onward(done(add(*after(*shares[s]), running)))
    share(end)
    last.append(down_sent[0])
    up_parts = {r: part(r, *up_sum) for r in away}
    up_sent = pass_on(up_parts)
    down_kept = part(0, *down_sum)
    last.append(down_sent[1])
    running = onward(done(add(*after(*shares[end]), running)))
    last.append(up_sent[0])
    up_kept = part(0, *up_sum)
    last.append(up_sent[1])
    down_grad = finished(down_kept, down_parts, down_sent)
    up_grad = finished(up_kept, up_parts, up_sent)
    input_grad = add(*after(*shares[0]), running).reshape(OWNB, here, d)
    return input_grad, up_grad, down_grad


def solution(mesh):
    placed = (
        P("dp", "tensor", None),
        P("dp", "tensor", None),
        P(None, "tensor"),
        P(None, "tensor"),
        P(),
        P(),
    )
    return jax.shard_map(
        local,
        mesh=mesh,
        in_specs=placed,
        out_specs=(P("dp", "tensor", None), P("dp", "tensor"), P("dp", "tensor")),
        check_vma=False,
    )
```

```python
import functools

import jax
import jax.numpy as jnp
from jax import lax
from jax.experimental import pallas as pl
from jax.experimental.pallas import tpu as pltpu
from jax.sharding import PartitionSpec as P

OWNB = 4
BF16 = jnp.bfloat16
F32 = jnp.float32
VMEM_LIMIT = 64 * 1024 * 1024
SHORT = pl.CostEstimate(flops=1, bytes_accessed=1, transcendentals=0)


def chip_with(j, v, core):
    return jnp.where(core == 0, 2 * j + v, ((j >> 1) << 2) + 2 * v + (j & 1))


def pool_bit(chip, core):
    return jnp.where(core == 0, chip & 1, (chip >> 1) & 1)


def other_bits(chip, core):
    return jnp.where(core == 0, chip >> 1, ((chip >> 2) << 1) + (chip & 1))


def chip_perm(dp, flip, cross=False):
    return [(i, 2 * ((i >> 1) ^ flip(i & 1)) + ((i & 1) ^ int(cross))) for i in range(dp)]


def start_of(count, source, dp):
    total = jnp.int32(0)
    for j in range(dp):
        total = total + jnp.where(source > j, count[j], 0)
    return total


def source_of(count, number, dp):
    end, source = jnp.int32(0), jnp.int32(0)
    for j in range(dp):
        end = end + count[j]
        source = source + jnp.where(end <= number, 1, 0)
    return source


def run(copies):
    for copy in copies:
        copy.start()
    for copy in copies:
        copy.wait()


def pack_body(info, count, rows, out, sems):
    dp, blocks = out.shape[0], rows.shape[0]
    start = start_of(count, info[0], dp)
    copies = []
    for k in range(dp):
        block = jnp.minimum(lax.rem(k + OWNB * dp - start, dp), blocks - 1)
        copies.append(pltpu.make_async_copy(rows.at[block], out.at[k], sems.at[k]))
    run(copies)


def pack(rows, info, count, dp):
    _, here, d = rows.shape
    return pl.pallas_call(
        pack_body,
        out_shape=jax.ShapeDtypeStruct((dp, here, d), BF16),
        grid_spec=pltpu.PrefetchScalarGridSpec(
            num_scalar_prefetch=2,
            grid=(1,),
            in_specs=[pl.BlockSpec(memory_space=pl.ANY)],
            out_specs=pl.BlockSpec((dp, here, d), lambda n, i, c: (0, 0, 0)),
            scratch_shapes=[pltpu.SemaphoreType.DMA((dp,))],
        ),
        compiler_params=pltpu.CompilerParams(vmem_limit_bytes=VMEM_LIMIT),
        cost_estimate=SHORT,
    )(info, count, rows)


def select_body(info, count, patches, arrived, out, sems):
    dp, here = arrived.shape[0], out.shape[1]
    copies, filled = [], []
    for m in range(OWNB):
        number = info[0] + dp * m
        source = source_of(count, number, dp)
        filled.append(patches[source, number - start_of(count, source, dp)])
        copies.append(pltpu.make_async_copy(arrived.at[source], out.at[m], sems.at[m]))
    run(copies)
    row = lax.broadcasted_iota(jnp.int32, out.shape[1:], 0) + info[1] * here
    for m in range(OWNB):
        out[m] = jnp.where(row < filled[m], out[m].astype(F32), 0.0).astype(out.dtype)


def select(arrived, info, count, patches):
    _, here, d = arrived.shape
    return pl.pallas_call(
        select_body,
        out_shape=jax.ShapeDtypeStruct((OWNB, here, d), BF16),
        grid_spec=pltpu.PrefetchScalarGridSpec(
            num_scalar_prefetch=3,
            grid=(1,),
            in_specs=[pl.BlockSpec(memory_space=pl.ANY)],
            out_specs=pl.BlockSpec((OWNB, here, d), lambda n, i, c, p: (0, 0, 0)),
            scratch_shapes=[pltpu.SemaphoreType.DMA((OWNB,))],
        ),
        compiler_params=pltpu.CompilerParams(vmem_limit_bytes=VMEM_LIMIT),
        cost_estimate=SHORT,
    )(info, count, patches, arrived)


def block_of(size, most):
    for width in range(most, 0, -128):
        if size % width == 0:
            return width
    return size


def load_rows(own, sib, rows):
    half = own.shape[0]
    rows[:half] = own[...]
    rows[half:] = sib[...]


def put_partner_columns(info, rows, out, hidden, chips):
    core, chip = info[0] & 1, info[0] >> 1
    width = rows.shape[1] // chips
    away = 1 - pool_bit(chip, core)
    for j in range(chips // 2):
        at = pl.multiple_of(chip_with(j, away, core) * width, 128)
        out[:, hidden + j * width:hidden + (j + 1) * width] = rows[:, pl.ds(at, width)]


def up_body(info, own, sib, w, out, slope, rows, *, hidden, chips):
    n = pl.program_id(0)

    @pl.when(n == 0)
    def _():
        load_rows(own, sib, rows)
        put_partner_columns(info, rows, out, hidden, chips)

    pre_act = jnp.dot(rows[...], w[...], preferred_element_type=F32)
    cdf = 0.5 * (1.0 + lax.erf(pre_act * 0.7071067811865476))
    density = jnp.exp(-0.5 * pre_act * pre_act) * 0.3989422804014327
    width = w.shape[1]
    out[:, pl.ds(pl.multiple_of(n * width, 128), width)] = (pre_act * cdf).astype(out.dtype)
    slope[...] = (cdf + pre_act * density).astype(slope.dtype)


def down_body(info, own, sib, w, slope, out, rows, *, hidden, chips):
    n = pl.program_id(0)

    @pl.when(n == 0)
    def _():
        load_rows(own, sib, rows)
        if out.shape[1] > hidden:
            put_partner_columns(info, rows, out, hidden, chips)

    act_grad = jnp.dot(rows[...], w[...], preferred_element_type=F32)
    width = w.shape[1]
    out[:, pl.ds(pl.multiple_of(n * width, 128), width)] = (act_grad * slope[...]).astype(out.dtype)


def columns_body(info, own, sib, out, rows, *, chips):
    load_rows(own, sib, rows)
    put_partner_columns(info, rows, out, 0, chips)


def partner_columns(own, sib, info, chips):
    half, d = own.shape
    spec = pl.BlockSpec((half, d), lambda n, i: (0, 0))
    return pl.pallas_call(
        functools.partial(columns_body, chips=chips),
        out_shape=jax.ShapeDtypeStruct((2 * half, d // 2), BF16),
        grid_spec=pltpu.PrefetchScalarGridSpec(
            num_scalar_prefetch=1,
            grid=(1,),
            in_specs=[spec, spec],
            out_specs=pl.BlockSpec((2 * half, d // 2), lambda n, i: (0, 0)),
            scratch_shapes=[pltpu.VMEM((2 * half, d), BF16)],
        ),
        compiler_params=pltpu.CompilerParams(vmem_limit_bytes=VMEM_LIMIT),
        cost_estimate=SHORT,
    )(info, own, sib)


def forward(own, sib, w, info, chips, slope=None, with_columns=True):
    half, d = own.shape
    hidden = w.shape[1] // 2
    width = block_of(hidden, 768)
    steps = hidden // width
    total = hidden + (d // 2 if with_columns else 0)
    out_shape = jax.ShapeDtypeStruct((2 * half, total), BF16)
    out_specs = pl.BlockSpec((2 * half, total), lambda n, i: (0, 0))
    slope_spec = pl.BlockSpec((2 * half, width), lambda n, i: (0, n))
    rows_spec = pl.BlockSpec((half, d), lambda n, i: (0, 0))
    w_spec = pl.BlockSpec((d, width), lambda n, i: (0, (i[0] & 1) * steps + n))
    in_specs = [rows_spec, rows_spec, w_spec]
    operands = [own, sib, w]
    if slope is None:
        body = up_body
        out_shape = (out_shape, jax.ShapeDtypeStruct((2 * half, hidden), BF16))
        out_specs = (out_specs, slope_spec)
    else:
        body = down_body
        in_specs.append(slope_spec)
        operands.append(slope)
    return pl.pallas_call(
        functools.partial(body, hidden=hidden, chips=chips),
        out_shape=out_shape,
        grid_spec=pltpu.PrefetchScalarGridSpec(
            num_scalar_prefetch=1,
            grid=(steps,),
            in_specs=in_specs,
            out_specs=out_specs,
            scratch_shapes=[pltpu.VMEM((2 * half, d), BF16)],
        ),
        compiler_params=pltpu.CompilerParams(vmem_limit_bytes=VMEM_LIMIT),
        cost_estimate=SHORT,
    )(info, *operands)


def input_body(info, pre, w, own, sib):
    value = lax.dot_general(pre[...], w[...], (((1,), (1,)), ((), ())), preferred_element_type=F32)
    half = own.shape[0]
    own[...] = value[:half].astype(own.dtype)
    sib[...] = value[half:].astype(sib.dtype)


def input_part(pre, w, info):
    rows = pre.shape[0]
    d, hidden = w.shape[0], w.shape[1] // 2
    width = block_of(d, 1536)
    shape = jax.ShapeDtypeStruct((rows // 2, d), BF16)
    spec = pl.BlockSpec((rows // 2, width), lambda n, i: (0, n))
    return pl.pallas_call(
        input_body,
        out_shape=(shape, shape),
        grid_spec=pltpu.PrefetchScalarGridSpec(
            num_scalar_prefetch=1,
            grid=(d // width,),
            in_specs=[
                pl.BlockSpec((rows, hidden), lambda n, i: (0, 0)),
                pl.BlockSpec((width, hidden), lambda n, i: (n, i[0] & 1)),
            ],
            out_specs=(spec, spec),
        ),
        compiler_params=pltpu.CompilerParams(vmem_limit_bytes=VMEM_LIMIT),
        cost_estimate=SHORT,
    )(info, pre, w)


def weight_body(at, *refs, begins, width, block):
    slots = len(begins)
    ins, outs, (left, right, total, left_sems, right_sems) = refs[:5 * slots], refs[5 * slots:-5], refs[-5:]
    half, hidden = ins[0].shape[0], right.shape[1]
    copies = []
    for s in range(slots):
        own, sib, there, mine, theirs = ins[5 * s:5 * s + 5]
        first = 4 * s * half
        for k, (rows, column, to, size) in enumerate((
            (own, at[0] * width, first, half),
            (sib, at[0] * width, first + half, half),
            (there, begins[s] + at[1] * width, first + 2 * half, 2 * half),
        )):
            source = rows.at[:, pl.ds(pl.multiple_of(column, 128), width)]
            copies.append(pltpu.make_async_copy(source, left.at[pl.ds(to, size)], left_sems.at[3 * s + k]))
        for k, hidden_side in enumerate((mine, theirs)):
            source = hidden_side.at[:, pl.ds(0, hidden)]
            to = right.at[pl.ds(first + 2 * k * half, 2 * half)]
            copies.append(pltpu.make_async_copy(source, to, right_sems.at[2 * s + k]))
    for copy in copies:
        copy.start()
    middle = slots // 2
    dims = (((0,), (0,)), ((), ()))
    columns = [slice(n, n + block) for n in range(0, hidden, block)]
    for copy in copies[:5 * middle]:
        copy.wait()
    early = 4 * middle * half
    for cut in columns:
        total[:, cut] = lax.dot_general(left[:early], right[:early, cut], dims, preferred_element_type=F32)
    for copy in copies[5 * middle:]:
        copy.wait()
    span = width // 2
    is_first = at[2] == 0
    for cut in columns:
        value = total[:, cut] + lax.dot_general(left[early:], right[early:, cut], dims, preferred_element_type=F32)
        if len(outs) == 1:
            outs[0][:, cut] = value.astype(outs[0].dtype)
        else:
            low, high = value[:span], value[span:]
            outs[0][:, cut] = jnp.where(is_first, low, high).astype(outs[0].dtype)
            outs[1][:, cut] = jnp.where(is_first, high, low).astype(outs[1].dtype)


def weight_part(rows, there_rows, rights, own_at, there_at, core, width, hidden, split):
    slots, size = len(rows), 2 * rows[0][0].shape[0]
    at = jnp.stack([own_at, there_at, core]).astype(jnp.int32)
    block = block_of(hidden, 512)
    operands = []
    for (own, sib), (there, _), (mine, theirs) in zip(rows, there_rows, rights):
        operands += [own, sib, there, mine, theirs]
    pieces = 2 if split else 1
    shape = jax.ShapeDtypeStruct((width // pieces, hidden), BF16)
    spec = pl.BlockSpec((width // pieces, hidden), lambda n, a: (0, 0))
    return pl.pallas_call(
        functools.partial(weight_body, begins=[begin for _, begin in there_rows], width=width, block=block),
        out_shape=(shape,) * pieces,
        grid_spec=pltpu.PrefetchScalarGridSpec(
            num_scalar_prefetch=1,
            grid=(1,),
            in_specs=[pl.BlockSpec(memory_space=pl.ANY)] * len(operands),
            out_specs=(spec,) * pieces,
            scratch_shapes=[
                pltpu.VMEM((2 * slots * size, width), BF16),
                pltpu.VMEM((2 * slots * size, hidden), BF16),
                pltpu.VMEM((width, hidden), F32),
                pltpu.SemaphoreType.DMA((3 * slots,)),
                pltpu.SemaphoreType.DMA((2 * slots,)),
            ],
        ),
        compiler_params=pltpu.CompilerParams(vmem_limit_bytes=VMEM_LIMIT),
        cost_estimate=SHORT,
    )(at, *operands)


def add(*values):
    return sum(v.astype(F32) for v in values).astype(BF16)


def local(x_rows, g_rows, w_up, w_down_t, block_count, patches):
    dp, tensor = lax.axis_size("dp"), lax.axis_size("tensor")
    chips = dp // 2
    me, plane = lax.axis_index("dp"), lax.axis_index("tensor")
    chip, core = me >> 1, me & 1
    info = jnp.stack([me, plane]).astype(jnp.int32)
    here, d = x_rows.shape[1:]
    hidden = w_up.shape[1] // 2
    ring = [(i, (i + 1) % tensor) for i in range(tensor)]
    to_sibling = [(i, i ^ 1) for i in range(dp)]
    to_pool = chip_perm(dp, lambda c: 1 << c)
    last = []

    def after(*values):
        out = lax.optimization_barrier((*values, *last))[:len(values)]
        return out if len(out) > 1 else out[0]

    def done(value):
        last[:] = [value]
        return value

    def onward(piece):
        return lax.ppermute(piece, "tensor", ring)

    def sibling(piece):
        return lax.ppermute(piece, "dp", to_sibling)

    def pooled(piece):
        return lax.ppermute(piece, "dp", to_pool)

    def exchange(rows):
        return lax.all_to_all(rows, "dp", split_axis=0, concat_axis=0, tiled=True)

    def chosen(arrived):
        return done(select(after(arrived), info, block_count, patches)).reshape(OWNB * here, d)

    def arrive(own, sib, ahead, further=True):
        piece = after(ahead)
        own.append(piece)
        sib.append(sibling(piece))
        return onward(piece) if further else None

    x_own, x_sib, x_there = [], [], []
    g_own, g_sib, g_there = [], [], []
    act, slope, pre, shares, pools = [], [], [], [], {}

    def settle(*names):
        last.extend(pools[name] for name in names if name in pools)

    def up(s):
        mine, slope_s = forward(*after(x_own[s], x_sib[s]), w_up, info, chips)
        theirs = pools["x", s] = pooled(done(mine))
        x_there.append((theirs, hidden))
        slope.append(slope_s)
        act.append((mine, theirs))

    def down(s, with_columns=True):
        mine = forward(*after(g_own[s], g_sib[s]), w_down_t, info, chips, slope[s], with_columns)
        theirs = pools["g", s] = pooled(done(mine))
        if with_columns:
            g_there.append((theirs, hidden))
        pre.append((mine, theirs))

    def share(s):
        own, sib = input_part(after(pre[s][0]), w_up, info)
        pools["share", s] = sibling(done(sib))
        shares.append((own, pools["share", s]))

    send_x = done(pack(x_rows, info, block_count, dp))
    arrived_x = exchange(send_x)
    send_g = done(pack(after(g_rows), info, block_count, dp))
    arrived_g = exchange(lax.optimization_barrier((send_g, arrived_x))[0])
    x_own.append(chosen(arrived_x))
    x_sib.append(sibling(x_own[0]))
    x_ahead = onward(x_own[0])
    up(0)
    end = tensor - 1
    for s in range(1, tensor):
        x_ahead = arrive(x_own, x_sib, x_ahead, s < end)
        if s == end:
            g_ahead = onward(after(g_own[0]))
        settle(("x", s - 2))
        up(s)
        if s == 1:
            g_own.append(chosen(arrived_g))
            g_sib.append(sibling(g_own[0]))
        if s == 2:
            settle(("x", 1))
            down(0)
    settle(("x", end - 1))
    share(0)
    for s in range(1, end):
        g_ahead = arrive(g_own, g_sib, g_ahead)
        settle(("share", s - 1), ("x", end) if s > 1 else None, ("g", s - 2))
        down(s)
        settle(("g", 0))
        share(s)

    settle(("g", end - 2))
    first_share = done(add(*after(*shares[1])))
    arrive(g_own, g_sib, g_ahead, False)
    running = onward(lax.optimization_barrier((first_share, g_own[end]))[0])
    columns = done(partner_columns(*after(g_own[end], g_sib[end]), info, chips))
    pools["columns"] = pooled(columns)
    g_there.append((pools["columns"], 0))
    settle(("share", end - 1), ("g", end - 1))
    down(end, False)

    span = d // dp
    near, mine_j = pool_bit(chip, core), other_bits(chip, core)

    def part(r, rows, there, rights, split):
        j = mine_j ^ r
        rows = [after(*rows[0]), *rows[1:]]
        parts = weight_part(
            rows, there, rights, chip_with(j, near, core), j, core, 2 * span, hidden, split
        )
        done(parts[0])
        return list(parts)

    bits = (chips // 2).bit_length() - 1

    def pass_on(parts):
        for k in reversed(range(1, bits)):
            perm = chip_perm(dp, lambda c: 2 << k)
            for r in range(1 << k, 2 << k):
                sent = [lax.ppermute(p, "dp", perm) for p in parts[r]]
                kept = parts.get(r ^ (1 << k))
                parts[r ^ (1 << k)] = [add(*both) for both in zip(kept, sent)] if kept else sent
        flip = lambda c: 2 >> c
        return [lax.ppermute(p, "dp", chip_perm(dp, flip, h == 1)) for h, p in enumerate(parts[1])]

    def core_rows(value, which):
        return lax.dynamic_slice_in_dim(value, which * span, span, 0)

    def finished(kept, parts, sent):
        if 0 in parts:
            kept = [add(*both) for both in zip(kept, parts[0])]
        if len(kept) == 2:
            mine = add(after(kept[0]), sent[0])
            other = add(sibling(kept[1]), sent[1])
        else:
            other = sibling(add(core_rows(kept[0], 1 - core), core_rows(sent[0], 1 - core)))
            mine = add(core_rows(after(kept[0]), core), core_rows(sent[0], core))
        return done(jnp.where(
            core == 0, jnp.concatenate([mine, other], axis=1), jnp.concatenate([other, mine], axis=1)
        ))

    down_sum = (list(zip(g_own, g_sib)), g_there, act, True)
    up_sum = (list(zip(x_own, x_sib)), x_there, pre, True)
    away = list(reversed(range(1, chips // 2)))
    settle("columns")
    last.append(running)
    down_parts = {r: part(r, *down_sum) for r in away}
    down_sent = pass_on(down_parts)
    settle(("g", end))
    for s in range(2, end):
        running = onward(done(add(*after(*shares[s]), running)))
    share(end)
    last.append(down_sent[0])
    up_parts = {r: part(r, *up_sum) for r in away}
    up_sent = pass_on(up_parts)
    down_kept = part(0, *down_sum)
    last.append(down_sent[1])
    running = onward(done(add(*after(*shares[end]), running)))
    last.append(up_sent[0])
    up_kept = part(0, *up_sum)
    last.append(up_sent[1])
    down_grad = finished(down_kept, down_parts, down_sent)
    up_grad = finished(up_kept, up_parts, up_sent)
    input_grad = add(*after(*shares[0]), running).reshape(OWNB, here, d)
    return input_grad, up_grad, down_grad


def solution(mesh):
    placed = (
        P("dp", "tensor", None),
        P("dp", "tensor", None),
        P(None, "tensor"),
        P(None, "tensor"),
        P(),
        P(),
    )
    return jax.shard_map(
        local,
        mesh=mesh,
        in_specs=placed,
        out_specs=(P("dp", "tensor", None), P("dp", "tensor"), P("dp", "tensor")),
        check_vma=False,
    )
```

```python
import functools

import jax
import jax.numpy as jnp
from jax import lax
from jax.experimental import pallas as pl
from jax.experimental.pallas import tpu as pltpu
from jax.sharding import PartitionSpec as P

OWNB = 4
BF16 = jnp.bfloat16
F32 = jnp.float32
VMEM_LIMIT = 64 * 1024 * 1024
SHORT = pl.CostEstimate(flops=1, bytes_accessed=1, transcendentals=0)


def chip_with(j, v, core):
    return jnp.where(core == 0, 2 * j + v, ((j >> 1) << 2) + 2 * v + (j & 1))


def pool_bit(chip, core):
    return jnp.where(core == 0, chip & 1, (chip >> 1) & 1)


def other_bits(chip, core):
    return jnp.where(core == 0, chip >> 1, ((chip >> 2) << 1) + (chip & 1))


def chip_perm(dp, flip, cross=False):
    return [(i, 2 * ((i >> 1) ^ flip(i & 1)) + ((i & 1) ^ int(cross))) for i in range(dp)]


def start_of(count, source, dp):
    total = jnp.int32(0)
    for j in range(dp):
        total = total + jnp.where(source > j, count[j], 0)
    return total


def source_of(count, number, dp):
    end, source = jnp.int32(0), jnp.int32(0)
    for j in range(dp):
        end = end + count[j]
        source = source + jnp.where(end <= number, 1, 0)
    return source


def run(copies):
    for copy in copies:
        copy.start()
    for copy in copies:
        copy.wait()


def pack_body(info, count, rows, out, sems):
    dp, blocks = out.shape[0], rows.shape[0]
    start = start_of(count, info[0], dp)
    copies = []
    for k in range(dp):
        block = jnp.minimum(lax.rem(k + OWNB * dp - start, dp), blocks - 1)
        copies.append(pltpu.make_async_copy(rows.at[block], out.at[k], sems.at[k]))
    run(copies)


def pack(rows, info, count, dp):
    _, here, d = rows.shape
    return pl.pallas_call(
        pack_body,
        out_shape=jax.ShapeDtypeStruct((dp, here, d), BF16),
        grid_spec=pltpu.PrefetchScalarGridSpec(
            num_scalar_prefetch=2,
            grid=(1,),
            in_specs=[pl.BlockSpec(memory_space=pl.ANY)],
            out_specs=pl.BlockSpec((dp, here, d), lambda n, i, c: (0, 0, 0)),
            scratch_shapes=[pltpu.SemaphoreType.DMA((dp,))],
        ),
        compiler_params=pltpu.CompilerParams(vmem_limit_bytes=VMEM_LIMIT),
        cost_estimate=SHORT,
    )(info, count, rows)


def select_body(info, count, patches, arrived, out, sems):
    dp, here = arrived.shape[0], out.shape[1]
    copies, filled = [], []
    for m in range(OWNB):
        number = info[0] + dp * m
        source = source_of(count, number, dp)
        filled.append(patches[source, number - start_of(count, source, dp)])
        copies.append(pltpu.make_async_copy(arrived.at[source], out.at[m], sems.at[m]))
    run(copies)
    row = lax.broadcasted_iota(jnp.int32, out.shape[1:], 0) + info[1] * here
    for m in range(OWNB):
        out[m] = jnp.where(row < filled[m], out[m].astype(F32), 0.0).astype(out.dtype)


def select(arrived, info, count, patches):
    _, here, d = arrived.shape
    return pl.pallas_call(
        select_body,
        out_shape=jax.ShapeDtypeStruct((OWNB, here, d), BF16),
        grid_spec=pltpu.PrefetchScalarGridSpec(
            num_scalar_prefetch=3,
            grid=(1,),
            in_specs=[pl.BlockSpec(memory_space=pl.ANY)],
            out_specs=pl.BlockSpec((OWNB, here, d), lambda n, i, c, p: (0, 0, 0)),
            scratch_shapes=[pltpu.SemaphoreType.DMA((OWNB,))],
        ),
        compiler_params=pltpu.CompilerParams(vmem_limit_bytes=VMEM_LIMIT),
        cost_estimate=SHORT,
    )(info, count, patches, arrived)


def block_of(size, most):
    for width in range(most, 0, -128):
        if size % width == 0:
            return width
    return size


def load_rows(own, sib, rows):
    half = own.shape[0]
    rows[:half] = own[...]
    rows[half:] = sib[...]


def put_partner_columns(info, rows, out, hidden, chips):
    core, chip = info[0] & 1, info[0] >> 1
    width = rows.shape[1] // chips
    away = 1 - pool_bit(chip, core)
    for j in range(chips // 2):
        at = pl.multiple_of(chip_with(j, away, core) * width, 128)
        out[:, hidden + j * width:hidden + (j + 1) * width] = rows[:, pl.ds(at, width)]


def up_body(info, own, sib, w, out, slope, rows, *, hidden, chips):
    n = pl.program_id(0)

    @pl.when(n == 0)
    def _():
        load_rows(own, sib, rows)
        put_partner_columns(info, rows, out, hidden, chips)

    pre_act = jnp.dot(rows[...], w[...], preferred_element_type=F32)
    cdf = 0.5 * (1.0 + lax.erf(pre_act * 0.7071067811865476))
    density = jnp.exp(-0.5 * pre_act * pre_act) * 0.3989422804014327
    width = w.shape[1]
    out[:, pl.ds(pl.multiple_of(n * width, 128), width)] = (pre_act * cdf).astype(out.dtype)
    slope[...] = (cdf + pre_act * density).astype(slope.dtype)


def down_body(info, own, sib, w, slope, out, rows, *, hidden, chips):
    n = pl.program_id(0)

    @pl.when(n == 0)
    def _():
        load_rows(own, sib, rows)
        if out.shape[1] > hidden:
            put_partner_columns(info, rows, out, hidden, chips)

    act_grad = jnp.dot(rows[...], w[...], preferred_element_type=F32)
    width = w.shape[1]
    out[:, pl.ds(pl.multiple_of(n * width, 128), width)] = (act_grad * slope[...]).astype(out.dtype)


def columns_body(info, own, sib, out, rows, *, chips):
    load_rows(own, sib, rows)
    put_partner_columns(info, rows, out, 0, chips)


def partner_columns(own, sib, info, chips):
    half, d = own.shape
    spec = pl.BlockSpec((half, d), lambda n, i: (0, 0))
    return pl.pallas_call(
        functools.partial(columns_body, chips=chips),
        out_shape=jax.ShapeDtypeStruct((2 * half, d // 2), BF16),
        grid_spec=pltpu.PrefetchScalarGridSpec(
            num_scalar_prefetch=1,
            grid=(1,),
            in_specs=[spec, spec],
            out_specs=pl.BlockSpec((2 * half, d // 2), lambda n, i: (0, 0)),
            scratch_shapes=[pltpu.VMEM((2 * half, d), BF16)],
        ),
        compiler_params=pltpu.CompilerParams(vmem_limit_bytes=VMEM_LIMIT),
        cost_estimate=SHORT,
    )(info, own, sib)


def forward(own, sib, w, info, chips, slope=None, with_columns=True):
    half, d = own.shape
    hidden = w.shape[1] // 2
    width = block_of(hidden, 768)
    steps = hidden // width
    total = hidden + (d // 2 if with_columns else 0)
    out_shape = jax.ShapeDtypeStruct((2 * half, total), BF16)
    out_specs = pl.BlockSpec((2 * half, total), lambda n, i: (0, 0))
    slope_spec = pl.BlockSpec((2 * half, width), lambda n, i: (0, n))
    rows_spec = pl.BlockSpec((half, d), lambda n, i: (0, 0))
    w_spec = pl.BlockSpec((d, width), lambda n, i: (0, (i[0] & 1) * steps + n))
    in_specs = [rows_spec, rows_spec, w_spec]
    operands = [own, sib, w]
    if slope is None:
        body = up_body
        out_shape = (out_shape, jax.ShapeDtypeStruct((2 * half, hidden), BF16))
        out_specs = (out_specs, slope_spec)
    else:
        body = down_body
        in_specs.append(slope_spec)
        operands.append(slope)
    return pl.pallas_call(
        functools.partial(body, hidden=hidden, chips=chips),
        out_shape=out_shape,
        grid_spec=pltpu.PrefetchScalarGridSpec(
            num_scalar_prefetch=1,
            grid=(steps,),
            in_specs=in_specs,
            out_specs=out_specs,
            scratch_shapes=[pltpu.VMEM((2 * half, d), BF16)],
        ),
        compiler_params=pltpu.CompilerParams(vmem_limit_bytes=VMEM_LIMIT),
        cost_estimate=SHORT,
    )(info, *operands)


def input_body(info, pre, w, own, sib):
    value = lax.dot_general(pre[...], w[...], (((1,), (1,)), ((), ())), preferred_element_type=F32)
    half = own.shape[0]
    own[...] = value[:half].astype(own.dtype)
    sib[...] = value[half:].astype(sib.dtype)


def input_part(pre, w, info):
    rows = pre.shape[0]
    d, hidden = w.shape[0], w.shape[1] // 2
    width = block_of(d, 1536)
    shape = jax.ShapeDtypeStruct((rows // 2, d), BF16)
    spec = pl.BlockSpec((rows // 2, width), lambda n, i: (0, n))
    return pl.pallas_call(
        input_body,
        out_shape=(shape, shape),
        grid_spec=pltpu.PrefetchScalarGridSpec(
            num_scalar_prefetch=1,
            grid=(d // width,),
            in_specs=[
                pl.BlockSpec((rows, hidden), lambda n, i: (0, 0)),
                pl.BlockSpec((width, hidden), lambda n, i: (n, i[0] & 1)),
            ],
            out_specs=(spec, spec),
        ),
        compiler_params=pltpu.CompilerParams(vmem_limit_bytes=VMEM_LIMIT),
        cost_estimate=SHORT,
    )(info, pre, w)


def weight_body(at, *refs, begins, width, block):
    slots = len(begins)
    ins, outs, (left, right, total, left_sems, right_sems) = refs[:5 * slots], refs[5 * slots:-5], refs[-5:]
    half, hidden = ins[0].shape[0], right.shape[1]
    copies = []
    for s in range(slots):
        own, sib, there, mine, theirs = ins[5 * s:5 * s + 5]
        first = 4 * s * half
        for k, (rows, column, to, size) in enumerate((
            (own, at[0] * width, first, half),
            (sib, at[0] * width, first + half, half),
            (there, begins[s] + at[1] * width, first + 2 * half, 2 * half),
        )):
            source = rows.at[:, pl.ds(pl.multiple_of(column, 128), width)]
            copies.append(pltpu.make_async_copy(source, left.at[pl.ds(to, size)], left_sems.at[3 * s + k]))
        for k, hidden_side in enumerate((mine, theirs)):
            source = hidden_side.at[:, pl.ds(0, hidden)]
            to = right.at[pl.ds(first + 2 * k * half, 2 * half)]
            copies.append(pltpu.make_async_copy(source, to, right_sems.at[2 * s + k]))
    for copy in copies:
        copy.start()
    middle = slots // 2
    dims = (((0,), (0,)), ((), ()))
    early = 4 * middle * half
    span = width // 2
    is_first = at[2] == 0

    def by_columns(body):
        def step(n, carry):
            body(pl.ds(pl.multiple_of(n * block, 128), block))
            return carry

        lax.fori_loop(0, hidden // block, step, 0)

    def first_rows(cut):
        total[:, cut] = lax.dot_general(left[:early], right[:early, cut], dims, preferred_element_type=F32)

    def last_rows(cut):
        value = total[:, cut] + lax.dot_general(left[early:], right[early:, cut], dims, preferred_element_type=F32)
        if len(outs) == 1:
            outs[0][:, cut] = value.astype(outs[0].dtype)
        else:
            low, high = value[:span], value[span:]
            outs[0][:, cut] = jnp.where(is_first, low, high).astype(outs[0].dtype)
            outs[1][:, cut] = jnp.where(is_first, high, low).astype(outs[1].dtype)

    for copy in copies[:5 * middle]:
        copy.wait()
    by_columns(first_rows)
    for copy in copies[5 * middle:]:
        copy.wait()
    by_columns(last_rows)


def weight_part(rows, there_rows, rights, own_at, there_at, core, width, hidden, split):
    slots, size = len(rows), 2 * rows[0][0].shape[0]
    at = jnp.stack([own_at, there_at, core]).astype(jnp.int32)
    block = block_of(hidden, 512)
    operands = []
    for (own, sib), (there, _), (mine, theirs) in zip(rows, there_rows, rights):
        operands += [own, sib, there, mine, theirs]
    pieces = 2 if split else 1
    shape = jax.ShapeDtypeStruct((width // pieces, hidden), BF16)
    spec = pl.BlockSpec((width // pieces, hidden), lambda n, a: (0, 0))
    return pl.pallas_call(
        functools.partial(weight_body, begins=[begin for _, begin in there_rows], width=width, block=block),
        out_shape=(shape,) * pieces,
        grid_spec=pltpu.PrefetchScalarGridSpec(
            num_scalar_prefetch=1,
            grid=(1,),
            in_specs=[pl.BlockSpec(memory_space=pl.ANY)] * len(operands),
            out_specs=(spec,) * pieces,
            scratch_shapes=[
                pltpu.VMEM((2 * slots * size, width), BF16),
                pltpu.VMEM((2 * slots * size, hidden), BF16),
                pltpu.VMEM((width, hidden), F32),
                pltpu.SemaphoreType.DMA((3 * slots,)),
                pltpu.SemaphoreType.DMA((2 * slots,)),
            ],
        ),
        compiler_params=pltpu.CompilerParams(vmem_limit_bytes=VMEM_LIMIT),
        cost_estimate=SHORT,
    )(at, *operands)


def add(*values):
    return sum(v.astype(F32) for v in values).astype(BF16)


def local(x_rows, g_rows, w_up, w_down_t, block_count, patches):
    dp, tensor = lax.axis_size("dp"), lax.axis_size("tensor")
    chips = dp // 2
    me, plane = lax.axis_index("dp"), lax.axis_index("tensor")
    chip, core = me >> 1, me & 1
    info = jnp.stack([me, plane]).astype(jnp.int32)
    here, d = x_rows.shape[1:]
    hidden = w_up.shape[1] // 2
    ring = [(i, (i + 1) % tensor) for i in range(tensor)]
    to_sibling = [(i, i ^ 1) for i in range(dp)]
    to_pool = chip_perm(dp, lambda c: 1 << c)
    last = []

    def after(*values):
        out = lax.optimization_barrier((*values, *last))[:len(values)]
        return out if len(out) > 1 else out[0]

    def done(value):
        last[:] = [value]
        return value

    def onward(piece):
        return lax.ppermute(piece, "tensor", ring)

    def sibling(piece):
        return lax.ppermute(piece, "dp", to_sibling)

    def pooled(piece):
        return lax.ppermute(piece, "dp", to_pool)

    def exchange(rows):
        return lax.all_to_all(rows, "dp", split_axis=0, concat_axis=0, tiled=True)

    def chosen(arrived):
        return done(select(after(arrived), info, block_count, patches)).reshape(OWNB * here, d)

    def arrive(own, sib, ahead, further=True):
        piece = after(ahead)
        own.append(piece)
        sib.append(sibling(piece))
        return onward(piece) if further else None

    x_own, x_sib, x_there = [], [], []
    g_own, g_sib, g_there = [], [], []
    act, slope, pre, shares, pools = [], [], [], [], {}

    def settle(*names):
        last.extend(pools[name] for name in names if name in pools)

    def up(s):
        mine, slope_s = forward(*after(x_own[s], x_sib[s]), w_up, info, chips)
        theirs = pools["x", s] = pooled(done(mine))
        x_there.append((theirs, hidden))
        slope.append(slope_s)
        act.append((mine, theirs))

    def down(s, with_columns=True):
        mine = forward(*after(g_own[s], g_sib[s]), w_down_t, info, chips, slope[s], with_columns)
        theirs = pools["g", s] = pooled(done(mine))
        if with_columns:
            g_there.append((theirs, hidden))
        pre.append((mine, theirs))

    def share(s):
        own, sib = input_part(after(pre[s][0]), w_up, info)
        pools["share", s] = sibling(done(sib))
        shares.append((own, pools["share", s]))

    send_x = done(pack(x_rows, info, block_count, dp))
    arrived_x = exchange(send_x)
    send_g = done(pack(after(g_rows), info, block_count, dp))
    arrived_g = exchange(lax.optimization_barrier((send_g, arrived_x))[0])
    x_own.append(chosen(arrived_x))
    x_sib.append(sibling(x_own[0]))
    x_ahead = onward(x_own[0])
    up(0)
    end = tensor - 1
    for s in range(1, tensor):
        x_ahead = arrive(x_own, x_sib, x_ahead, s < end)
        if s == end:
            g_ahead = onward(after(g_own[0]))
        settle(("x", s - 2))
        up(s)
        if s == 1:
            g_own.append(chosen(arrived_g))
            g_sib.append(sibling(g_own[0]))
        if s == 2:
            settle(("x", 1))
            down(0)
    settle(("x", end - 1))
    share(0)
    for s in range(1, end):
        g_ahead = arrive(g_own, g_sib, g_ahead)
        settle(("share", s - 1), ("x", end) if s > 1 else None, ("g", s - 2))
        down(s)
        settle(("g", 0))
        share(s)

    settle(("g", end - 2))
    first_share = done(add(*after(*shares[1])))
    arrive(g_own, g_sib, g_ahead, False)
    running = onward(lax.optimization_barrier((first_share, g_own[end]))[0])
    columns = done(partner_columns(*after(g_own[end], g_sib[end]), info, chips))
    pools["columns"] = pooled(columns)
    g_there.append((pools["columns"], 0))
    settle(("share", end - 1), ("g", end - 1))
    down(end, False)

    span = d // dp
    near, mine_j = pool_bit(chip, core), other_bits(chip, core)

    def part(r, rows, there, rights, split):
        j = mine_j ^ r
        rows = [after(*rows[0]), *rows[1:]]
        parts = weight_part(
            rows, there, rights, chip_with(j, near, core), j, core, 2 * span, hidden, split
        )
        done(parts[0])
        return list(parts)

    bits = (chips // 2).bit_length() - 1

    def pass_on(parts):
        for k in reversed(range(1, bits)):
            perm = chip_perm(dp, lambda c: 2 << k)
            for r in range(1 << k, 2 << k):
                sent = [lax.ppermute(p, "dp", perm) for p in parts[r]]
                kept = parts.get(r ^ (1 << k))
                parts[r ^ (1 << k)] = [add(*both) for both in zip(kept, sent)] if kept else sent
        flip = lambda c: 2 >> c
        return [lax.ppermute(p, "dp", chip_perm(dp, flip, h == 1)) for h, p in enumerate(parts[1])]

    def core_rows(value, which):
        return lax.dynamic_slice_in_dim(value, which * span, span, 0)

    def finished(kept, parts, sent):
        if 0 in parts:
            kept = [add(*both) for both in zip(kept, parts[0])]
        if len(kept) == 2:
            mine = add(after(kept[0]), sent[0])
            other = add(sibling(kept[1]), sent[1])
        else:
            other = sibling(add(core_rows(kept[0], 1 - core), core_rows(sent[0], 1 - core)))
            mine = add(core_rows(after(kept[0]), core), core_rows(sent[0], core))
        return done(jnp.where(
            core == 0, jnp.concatenate([mine, other], axis=1), jnp.concatenate([other, mine], axis=1)
        ))

    down_sum = (list(zip(g_own, g_sib)), g_there, act, True)
    up_sum = (list(zip(x_own, x_sib)), x_there, pre, True)
    away = list(reversed(range(1, chips // 2)))
    settle("columns")
    last.append(running)
    down_parts = {r: part(r, *down_sum) for r in away}
    down_sent = pass_on(down_parts)
    settle(("g", end))
    for s in range(2, end):
        running = onward(done(add(*after(*shares[s]), running)))
    share(end)
    last.append(down_sent[0])
    up_parts = {r: part(r, *up_sum) for r in away}
    up_sent = pass_on(up_parts)
    down_kept = part(0, *down_sum)
    last.append(down_sent[1])
    running = onward(done(add(*after(*shares[end]), running)))
    last.append(up_sent[0])
    up_kept = part(0, *up_sum)
    last.append(up_sent[1])
    down_grad = finished(down_kept, down_parts, down_sent)
    up_grad = finished(up_kept, up_parts, up_sent)
    input_grad = add(*after(*shares[0]), running).reshape(OWNB, here, d)
    return input_grad, up_grad, down_grad


def solution(mesh):
    placed = (
        P("dp", "tensor", None),
        P("dp", "tensor", None),
        P(None, "tensor"),
        P(None, "tensor"),
        P(),
        P(),
    )
    return jax.shard_map(
        local,
        mesh=mesh,
        in_specs=placed,
        out_specs=(P("dp", "tensor", None), P("dp", "tensor"), P("dp", "tensor")),
        check_vma=False,
    )
```

```python
import functools

import jax
import jax.numpy as jnp
from jax import lax
from jax.experimental import pallas as pl
from jax.experimental.pallas import tpu as pltpu
from jax.sharding import PartitionSpec as P

OWNB = 4
BF16 = jnp.bfloat16
F32 = jnp.float32
VMEM_LIMIT = 64 * 1024 * 1024
SHORT = pl.CostEstimate(flops=1, bytes_accessed=1, transcendentals=0)


def chip_with(j, v, core):
    return jnp.where(core == 0, 2 * j + v, ((j >> 1) << 2) + 2 * v + (j & 1))


def pool_bit(chip, core):
    return jnp.where(core == 0, chip & 1, (chip >> 1) & 1)


def other_bits(chip, core):
    return jnp.where(core == 0, chip >> 1, ((chip >> 2) << 1) + (chip & 1))


def chip_perm(dp, flip, cross=False):
    return [(i, 2 * ((i >> 1) ^ flip(i & 1)) + ((i & 1) ^ int(cross))) for i in range(dp)]


def start_of(count, source, dp):
    total = jnp.int32(0)
    for j in range(dp):
        total = total + jnp.where(source > j, count[j], 0)
    return total


def source_of(count, number, dp):
    end, source = jnp.int32(0), jnp.int32(0)
    for j in range(dp):
        end = end + count[j]
        source = source + jnp.where(end <= number, 1, 0)
    return source


def run(copies):
    for copy in copies:
        copy.start()
    for copy in copies:
        copy.wait()


def pack_body(info, count, rows, out, sems):
    dp, blocks = out.shape[0], rows.shape[0]
    start = start_of(count, info[0], dp)
    copies = []
    for k in range(dp):
        block = jnp.minimum(lax.rem(k + OWNB * dp - start, dp), blocks - 1)
        copies.append(pltpu.make_async_copy(rows.at[block], out.at[k], sems.at[k]))
    run(copies)


def pack(rows, info, count, dp):
    _, here, d = rows.shape
    return pl.pallas_call(
        pack_body,
        out_shape=jax.ShapeDtypeStruct((dp, here, d), BF16),
        grid_spec=pltpu.PrefetchScalarGridSpec(
            num_scalar_prefetch=2,
            grid=(1,),
            in_specs=[pl.BlockSpec(memory_space=pl.ANY)],
            out_specs=pl.BlockSpec((dp, here, d), lambda n, i, c: (0, 0, 0)),
            scratch_shapes=[pltpu.SemaphoreType.DMA((dp,))],
        ),
        compiler_params=pltpu.CompilerParams(vmem_limit_bytes=VMEM_LIMIT),
        cost_estimate=SHORT,
    )(info, count, rows)


def select_body(info, count, patches, arrived, out, sems):
    dp, here = arrived.shape[0], out.shape[1]
    copies, filled = [], []
    for m in range(OWNB):
        number = info[0] + dp * m
        source = source_of(count, number, dp)
        filled.append(patches[source, number - start_of(count, source, dp)])
        copies.append(pltpu.make_async_copy(arrived.at[source], out.at[m], sems.at[m]))
    run(copies)
    row = lax.broadcasted_iota(jnp.int32, out.shape[1:], 0) + info[1] * here
    for m in range(OWNB):
        out[m] = jnp.where(row < filled[m], out[m].astype(F32), 0.0).astype(out.dtype)


def select(arrived, info, count, patches):
    _, here, d = arrived.shape
    return pl.pallas_call(
        select_body,
        out_shape=jax.ShapeDtypeStruct((OWNB, here, d), BF16),
        grid_spec=pltpu.PrefetchScalarGridSpec(
            num_scalar_prefetch=3,
            grid=(1,),
            in_specs=[pl.BlockSpec(memory_space=pl.ANY)],
            out_specs=pl.BlockSpec((OWNB, here, d), lambda n, i, c, p: (0, 0, 0)),
            scratch_shapes=[pltpu.SemaphoreType.DMA((OWNB,))],
        ),
        compiler_params=pltpu.CompilerParams(vmem_limit_bytes=VMEM_LIMIT),
        cost_estimate=SHORT,
    )(info, count, patches, arrived)


def block_of(size, most):
    for width in range(most, 0, -128):
        if size % width == 0:
            return width
    return size


def load_rows(own, sib, rows):
    half = own.shape[0]
    rows[:half] = own[...]
    rows[half:] = sib[...]


def put_partner_columns(info, rows, out, hidden, chips):
    core, chip = info[0] & 1, info[0] >> 1
    width = rows.shape[1] // chips
    away = 1 - pool_bit(chip, core)
    for j in range(chips // 2):
        at = pl.multiple_of(chip_with(j, away, core) * width, 128)
        out[:, hidden + j * width:hidden + (j + 1) * width] = rows[:, pl.ds(at, width)]


def up_body(info, own, sib, w, out, slope, rows, *, hidden, chips):
    n = pl.program_id(0)

    @pl.when(n == 0)
    def _():
        load_rows(own, sib, rows)
        put_partner_columns(info, rows, out, hidden, chips)

    pre_act = jnp.dot(rows[...], w[...], preferred_element_type=F32)
    cdf = 0.5 * (1.0 + lax.erf(pre_act * 0.7071067811865476))
    density = jnp.exp(-0.5 * pre_act * pre_act) * 0.3989422804014327
    width = w.shape[1]
    out[:, pl.ds(pl.multiple_of(n * width, 128), width)] = (pre_act * cdf).astype(out.dtype)
    slope[...] = (cdf + pre_act * density).astype(slope.dtype)


def down_body(info, own, sib, w, slope, out, rows, *, hidden, chips):
    n = pl.program_id(0)

    @pl.when(n == 0)
    def _():
        load_rows(own, sib, rows)
        if out.shape[1] > hidden:
            put_partner_columns(info, rows, out, hidden, chips)

    act_grad = jnp.dot(rows[...], w[...], preferred_element_type=F32)
    width = w.shape[1]
    out[:, pl.ds(pl.multiple_of(n * width, 128), width)] = (act_grad * slope[...]).astype(out.dtype)


def columns_body(info, own, sib, out, rows, *, chips):
    load_rows(own, sib, rows)
    put_partner_columns(info, rows, out, 0, chips)


def partner_columns(own, sib, info, chips):
    half, d = own.shape
    spec = pl.BlockSpec((half, d), lambda n, i: (0, 0))
    return pl.pallas_call(
        functools.partial(columns_body, chips=chips),
        out_shape=jax.ShapeDtypeStruct((2 * half, d // 2), BF16),
        grid_spec=pltpu.PrefetchScalarGridSpec(
            num_scalar_prefetch=1,
            grid=(1,),
            in_specs=[spec, spec],
            out_specs=pl.BlockSpec((2 * half, d // 2), lambda n, i: (0, 0)),
            scratch_shapes=[pltpu.VMEM((2 * half, d), BF16)],
        ),
        compiler_params=pltpu.CompilerParams(vmem_limit_bytes=VMEM_LIMIT),
        cost_estimate=SHORT,
    )(info, own, sib)


def forward(own, sib, w, info, chips, slope=None, with_columns=True):
    half, d = own.shape
    hidden = w.shape[1] // 2
    width = block_of(hidden, 768)
    steps = hidden // width
    total = hidden + (d // 2 if with_columns else 0)
    out_shape = jax.ShapeDtypeStruct((2 * half, total), BF16)
    out_specs = pl.BlockSpec((2 * half, total), lambda n, i: (0, 0))
    slope_spec = pl.BlockSpec((2 * half, width), lambda n, i: (0, n))
    rows_spec = pl.BlockSpec((half, d), lambda n, i: (0, 0))
    w_spec = pl.BlockSpec((d, width), lambda n, i: (0, (i[0] & 1) * steps + n))
    in_specs = [rows_spec, rows_spec, w_spec]
    operands = [own, sib, w]
    if slope is None:
        body = up_body
        out_shape = (out_shape, jax.ShapeDtypeStruct((2 * half, hidden), BF16))
        out_specs = (out_specs, slope_spec)
    else:
        body = down_body
        in_specs.append(slope_spec)
        operands.append(slope)
    return pl.pallas_call(
        functools.partial(body, hidden=hidden, chips=chips),
        out_shape=out_shape,
        grid_spec=pltpu.PrefetchScalarGridSpec(
            num_scalar_prefetch=1,
            grid=(steps,),
            in_specs=in_specs,
            out_specs=out_specs,
            scratch_shapes=[pltpu.VMEM((2 * half, d), BF16)],
        ),
        compiler_params=pltpu.CompilerParams(vmem_limit_bytes=VMEM_LIMIT),
        cost_estimate=SHORT,
    )(info, *operands)


def input_body(info, pre, w, own, sib):
    value = lax.dot_general(pre[...], w[...], (((1,), (1,)), ((), ())), preferred_element_type=F32)
    half = own.shape[0]
    own[...] = value[:half].astype(own.dtype)
    sib[...] = value[half:].astype(sib.dtype)


def input_part(pre, w, info):
    rows = pre.shape[0]
    d, hidden = w.shape[0], w.shape[1] // 2
    width = block_of(d, 1536)
    shape = jax.ShapeDtypeStruct((rows // 2, d), BF16)
    spec = pl.BlockSpec((rows // 2, width), lambda n, i: (0, n))
    return pl.pallas_call(
        input_body,
        out_shape=(shape, shape),
        grid_spec=pltpu.PrefetchScalarGridSpec(
            num_scalar_prefetch=1,
            grid=(d // width,),
            in_specs=[
                pl.BlockSpec((rows, hidden), lambda n, i: (0, 0)),
                pl.BlockSpec((width, hidden), lambda n, i: (n, i[0] & 1)),
            ],
            out_specs=(spec, spec),
        ),
        compiler_params=pltpu.CompilerParams(vmem_limit_bytes=VMEM_LIMIT),
        cost_estimate=SHORT,
    )(info, pre, w)


def weight_body(at, *refs, begins, width, block):
    slots = len(begins)
    ins, outs, (left, right, total, left_sems, right_sems) = refs[:5 * slots], refs[5 * slots:-5], refs[-5:]
    half, hidden = ins[0].shape[0], right.shape[1]
    copies = []
    for s in range(slots):
        own, sib, there, mine, theirs = ins[5 * s:5 * s + 5]
        first = 4 * s * half
        for k, (rows, column, to, size) in enumerate((
            (own, at[0] * width, first, half),
            (sib, at[0] * width, first + half, half),
            (there, begins[s] + at[1] * width, first + 2 * half, 2 * half),
        )):
            source = rows.at[:, pl.ds(pl.multiple_of(column, 128), width)]
            copies.append(pltpu.make_async_copy(source, left.at[pl.ds(to, size)], left_sems.at[3 * s + k]))
        for k, hidden_side in enumerate((mine, theirs)):
            source = hidden_side.at[:, pl.ds(0, hidden)]
            to = right.at[pl.ds(first + 2 * k * half, 2 * half)]
            copies.append(pltpu.make_async_copy(source, to, right_sems.at[2 * s + k]))
    for copy in copies:
        copy.start()
    middle = slots // 2
    dims = (((0,), (0,)), ((), ()))
    early = 4 * middle * half
    span = width // 2
    is_first = at[2] == 0

    def by_columns(body):
        def step(n, carry):
            body(pl.ds(pl.multiple_of(n * block, 128), block))
            return carry

        lax.fori_loop(0, hidden // block, step, 0)

    def first_rows(cut):
        total[:, cut] = lax.dot_general(left[:early], right[:early, cut], dims, preferred_element_type=F32)

    def last_rows(cut):
        value = total[:, cut] + lax.dot_general(left[early:], right[early:, cut], dims, preferred_element_type=F32)
        if len(outs) == 1:
            outs[0][:, cut] = value.astype(outs[0].dtype)
        else:
            low, high = value[:span], value[span:]
            outs[0][:, cut] = jnp.where(is_first, low, high).astype(outs[0].dtype)
            outs[1][:, cut] = jnp.where(is_first, high, low).astype(outs[1].dtype)

    for copy in copies[:5 * middle]:
        copy.wait()
    by_columns(first_rows)
    for copy in copies[5 * middle:]:
        copy.wait()
    by_columns(last_rows)


def weight_part(rows, there_rows, rights, own_at, there_at, core, width, hidden, split):
    slots, size = len(rows), 2 * rows[0][0].shape[0]
    at = jnp.stack([own_at, there_at, core]).astype(jnp.int32)
    block = block_of(hidden, 512)
    operands = []
    for (own, sib), (there, _), (mine, theirs) in zip(rows, there_rows, rights):
        operands += [own, sib, there, mine, theirs]
    pieces = 2 if split else 1
    shape = jax.ShapeDtypeStruct((width // pieces, hidden), BF16)
    spec = pl.BlockSpec((width // pieces, hidden), lambda n, a: (0, 0))
    return pl.pallas_call(
        functools.partial(weight_body, begins=[begin for _, begin in there_rows], width=width, block=block),
        out_shape=(shape,) * pieces,
        grid_spec=pltpu.PrefetchScalarGridSpec(
            num_scalar_prefetch=1,
            grid=(1,),
            in_specs=[pl.BlockSpec(memory_space=pl.ANY)] * len(operands),
            out_specs=(spec,) * pieces,
            scratch_shapes=[
                pltpu.VMEM((2 * slots * size, width), BF16),
                pltpu.VMEM((2 * slots * size, hidden), BF16),
                pltpu.VMEM((width, hidden), F32),
                pltpu.SemaphoreType.DMA((3 * slots,)),
                pltpu.SemaphoreType.DMA((2 * slots,)),
            ],
        ),
        compiler_params=pltpu.CompilerParams(vmem_limit_bytes=VMEM_LIMIT),
        cost_estimate=SHORT,
    )(at, *operands)


def add(*values):
    return sum(v.astype(F32) for v in values).astype(BF16)


def local(x_rows, g_rows, w_up, w_down_t, block_count, patches):
    dp, tensor = lax.axis_size("dp"), lax.axis_size("tensor")
    chips = dp // 2
    me, plane = lax.axis_index("dp"), lax.axis_index("tensor")
    chip, core = me >> 1, me & 1
    info = jnp.stack([me, plane]).astype(jnp.int32)
    here, d = x_rows.shape[1:]
    hidden = w_up.shape[1] // 2
    ring = [(i, (i + 1) % tensor) for i in range(tensor)]
    to_sibling = [(i, i ^ 1) for i in range(dp)]
    to_pool = chip_perm(dp, lambda c: 1 << c)
    last = []

    def after(*values):
        out = lax.optimization_barrier((*values, *last))[:len(values)]
        return out if len(out) > 1 else out[0]

    def done(value):
        last[:] = [value]
        return value

    def onward(piece):
        return lax.ppermute(piece, "tensor", ring)

    def sibling(piece):
        return lax.ppermute(piece, "dp", to_sibling)

    def pooled(piece):
        return lax.ppermute(piece, "dp", to_pool)

    def exchange(rows):
        return lax.all_to_all(rows, "dp", split_axis=0, concat_axis=0, tiled=True)

    def chosen(arrived):
        return done(select(after(arrived), info, block_count, patches)).reshape(OWNB * here, d)

    def arrive(own, sib, ahead, further=True):
        piece = after(ahead)
        own.append(piece)
        sib.append(sibling(piece))
        return onward(piece) if further else None

    x_own, x_sib, x_there = [], [], []
    g_own, g_sib, g_there = [], [], []
    act, slope, pre, shares, pools = [], [], [], [], {}

    def settle(*names):
        last.extend(pools[name] for name in names if name in pools)

    def up(s):
        mine, slope_s = forward(*after(x_own[s], x_sib[s]), w_up, info, chips)
        theirs = pools["x", s] = pooled(done(mine))
        x_there.append((theirs, hidden))
        slope.append(slope_s)
        act.append((mine, theirs))

    def down(s, with_columns=True):
        mine = forward(*after(g_own[s], g_sib[s]), w_down_t, info, chips, slope[s], with_columns)
        theirs = pools["g", s] = pooled(done(mine))
        if with_columns:
            g_there.append((theirs, hidden))
        pre.append((mine, theirs))

    def share(s):
        own, sib = input_part(after(pre[s][0]), w_up, info)
        pools["share", s] = sibling(done(sib))
        shares.append((own, pools["share", s]))

    send_x = done(pack(x_rows, info, block_count, dp))
    arrived_x = exchange(send_x)
    send_g = done(pack(after(g_rows), info, block_count, dp))
    arrived_g = exchange(lax.optimization_barrier((send_g, arrived_x))[0])
    x_own.append(chosen(arrived_x))
    x_sib.append(sibling(x_own[0]))
    x_ahead = onward(x_own[0])
    up(0)
    end = tensor - 1
    for s in range(1, tensor):
        x_ahead = arrive(x_own, x_sib, x_ahead, s < end)
        if s == end:
            g_ahead = onward(after(g_own[0]))
        settle(("x", s - 2))
        up(s)
        if s == 1:
            g_own.append(chosen(arrived_g))
            g_sib.append(sibling(g_own[0]))
        if s == 2:
            settle(("x", 1))
            down(0)
    settle(("x", end - 1))
    share(0)
    for s in range(1, end):
        g_ahead = arrive(g_own, g_sib, g_ahead)
        settle(("share", s - 1), ("x", end) if s > 1 else None, ("g", s - 2))
        down(s)
        settle(("g", 0))
        share(s)

    settle(("g", end - 2))
    first_share = done(add(*after(*shares[1])))
    arrive(g_own, g_sib, g_ahead, False)
    running = onward(lax.optimization_barrier((first_share, g_own[end]))[0])
    columns = done(partner_columns(*after(g_own[end], g_sib[end]), info, chips))
    pools["columns"] = pooled(columns)
    g_there.append((pools["columns"], 0))
    settle(("share", end - 1))
    down(end, False)
    settle(("g", end - 1))
    share(end)

    span = d // dp
    near, mine_j = pool_bit(chip, core), other_bits(chip, core)

    def part(r, rows, there, rights, split):
        j = mine_j ^ r
        rows = [after(*rows[0]), *rows[1:]]
        parts = weight_part(
            rows, there, rights, chip_with(j, near, core), j, core, 2 * span, hidden, split
        )
        done(parts[0])
        return list(parts)

    bits = (chips // 2).bit_length() - 1

    def pass_on(parts):
        for k in reversed(range(1, bits)):
            perm = chip_perm(dp, lambda c: 2 << k)
            for r in range(1 << k, 2 << k):
                sent = [lax.ppermute(p, "dp", perm) for p in parts[r]]
                kept = parts.get(r ^ (1 << k))
                parts[r ^ (1 << k)] = [add(*both) for both in zip(kept, sent)] if kept else sent
        flip = lambda c: 2 >> c
        return [lax.ppermute(p, "dp", chip_perm(dp, flip, h == 1)) for h, p in enumerate(parts[1])]

    def core_rows(value, which):
        return lax.dynamic_slice_in_dim(value, which * span, span, 0)

    def finished(kept, parts, sent):
        if 0 in parts:
            kept = [add(*both) for both in zip(kept, parts[0])]
        if len(kept) == 2:
            mine = add(after(kept[0]), sent[0])
            other = add(sibling(kept[1]), sent[1])
        else:
            other = sibling(add(core_rows(kept[0], 1 - core), core_rows(sent[0], 1 - core)))
            mine = add(core_rows(after(kept[0]), core), core_rows(sent[0], core))
        return done(jnp.where(
            core == 0, jnp.concatenate([mine, other], axis=1), jnp.concatenate([other, mine], axis=1)
        ))

    down_sum = (list(zip(g_own, g_sib)), g_there, act, True)
    up_sum = (list(zip(x_own, x_sib)), x_there, pre, True)
    away = list(reversed(range(1, chips // 2)))
    settle("columns")
    last.append(running)
    down_parts = {r: part(r, *down_sum) for r in away}
    down_sent = pass_on(down_parts)
    for s in range(2, end):
        running = onward(done(add(*after(*shares[s]), running)))
    settle(("g", end))
    up_parts = {r: part(r, *up_sum) for r in away}
    up_sent = pass_on(up_parts)
    down_kept = part(0, *down_sum)
    running = onward(done(add(*after(*shares[end]), running)))
    last.extend(down_sent)
    up_kept = part(0, *up_sum)
    down_grad = finished(down_kept, down_parts, down_sent)
    input_grad = done(add(*after(*shares[0]), running)).reshape(OWNB, here, d)
    up_grad = finished(up_kept, up_parts, up_sent)
    return input_grad, up_grad, down_grad


def solution(mesh):
    placed = (
        P("dp", "tensor", None),
        P("dp", "tensor", None),
        P(None, "tensor"),
        P(None, "tensor"),
        P(),
        P(),
    )
    return jax.shard_map(
        local,
        mesh=mesh,
        in_specs=placed,
        out_specs=(P("dp", "tensor", None), P("dp", "tensor"), P("dp", "tensor")),
        check_vma=False,
    )
```

```python
import functools

import jax
import jax.numpy as jnp
from jax import lax
from jax.experimental import pallas as pl
from jax.experimental.pallas import tpu as pltpu
from jax.sharding import PartitionSpec as P

OWNB = 4
BF16 = jnp.bfloat16
F32 = jnp.float32
VMEM_LIMIT = 64 * 1024 * 1024
SHORT = pl.CostEstimate(flops=1, bytes_accessed=1, transcendentals=0)


def chip_with(j, v, core):
    return jnp.where(core == 0, 2 * j + v, ((j >> 1) << 2) + 2 * v + (j & 1))


def pool_bit(chip, core):
    return jnp.where(core == 0, chip & 1, (chip >> 1) & 1)


def other_bits(chip, core):
    return jnp.where(core == 0, chip >> 1, ((chip >> 2) << 1) + (chip & 1))


def chip_perm(dp, flip, cross=False):
    return [(i, 2 * ((i >> 1) ^ flip(i & 1)) + ((i & 1) ^ int(cross))) for i in range(dp)]


def start_of(count, source, dp):
    total = jnp.int32(0)
    for j in range(dp):
        total = total + jnp.where(source > j, count[j], 0)
    return total


def source_of(count, number, dp):
    end, source = jnp.int32(0), jnp.int32(0)
    for j in range(dp):
        end = end + count[j]
        source = source + jnp.where(end <= number, 1, 0)
    return source


def run(copies):
    for copy in copies:
        copy.start()
    for copy in copies:
        copy.wait()


def pack_body(info, count, rows, out, sems):
    dp, blocks = out.shape[0], rows.shape[0]
    start = start_of(count, info[0], dp)
    copies = []
    for k in range(dp):
        block = jnp.minimum(lax.rem(k + OWNB * dp - start, dp), blocks - 1)
        copies.append(pltpu.make_async_copy(rows.at[block], out.at[k], sems.at[k]))
    run(copies)


def pack(rows, info, count, dp):
    _, here, d = rows.shape
    return pl.pallas_call(
        pack_body,
        out_shape=jax.ShapeDtypeStruct((dp, here, d), BF16),
        grid_spec=pltpu.PrefetchScalarGridSpec(
            num_scalar_prefetch=2,
            grid=(1,),
            in_specs=[pl.BlockSpec(memory_space=pl.ANY)],
            out_specs=pl.BlockSpec((dp, here, d), lambda n, i, c: (0, 0, 0)),
            scratch_shapes=[pltpu.SemaphoreType.DMA((dp,))],
        ),
        compiler_params=pltpu.CompilerParams(vmem_limit_bytes=VMEM_LIMIT),
        cost_estimate=SHORT,
    )(info, count, rows)


def select_body(info, count, patches, arrived, out, sems):
    dp, here = arrived.shape[0], out.shape[1]
    copies, filled = [], []
    for m in range(OWNB):
        number = info[0] + dp * m
        source = source_of(count, number, dp)
        filled.append(patches[source, number - start_of(count, source, dp)])
        copies.append(pltpu.make_async_copy(arrived.at[source], out.at[m], sems.at[m]))
    run(copies)
    row = lax.broadcasted_iota(jnp.int32, out.shape[1:], 0) + info[1] * here
    for m in range(OWNB):
        out[m] = jnp.where(row < filled[m], out[m].astype(F32), 0.0).astype(out.dtype)


def select(arrived, info, count, patches):
    _, here, d = arrived.shape
    return pl.pallas_call(
        select_body,
        out_shape=jax.ShapeDtypeStruct((OWNB, here, d), BF16),
        grid_spec=pltpu.PrefetchScalarGridSpec(
            num_scalar_prefetch=3,
            grid=(1,),
            in_specs=[pl.BlockSpec(memory_space=pl.ANY)],
            out_specs=pl.BlockSpec((OWNB, here, d), lambda n, i, c, p: (0, 0, 0)),
            scratch_shapes=[pltpu.SemaphoreType.DMA((OWNB,))],
        ),
        compiler_params=pltpu.CompilerParams(vmem_limit_bytes=VMEM_LIMIT),
        cost_estimate=SHORT,
    )(info, count, patches, arrived)


def block_of(size, most):
    for width in range(most, 0, -128):
        if size % width == 0:
            return width
    return size


def load_rows(own, sib, rows):
    half = own.shape[0]
    rows[:half] = own[...]
    rows[half:] = sib[...]


def put_partner_columns(info, rows, out, hidden, chips):
    core, chip = info[0] & 1, info[0] >> 1
    width = rows.shape[1] // chips
    away = 1 - pool_bit(chip, core)
    for j in range(chips // 2):
        at = pl.multiple_of(chip_with(j, away, core) * width, 128)
        out[:, hidden + j * width:hidden + (j + 1) * width] = rows[:, pl.ds(at, width)]


def up_body(info, own, sib, w, out, slope, rows, *, hidden, chips):
    n = pl.program_id(0)

    @pl.when(n == 0)
    def _():
        load_rows(own, sib, rows)
        put_partner_columns(info, rows, out, hidden, chips)

    pre_act = jnp.dot(rows[...], w[...], preferred_element_type=F32)
    cdf = 0.5 * (1.0 + lax.erf(pre_act * 0.7071067811865476))
    density = jnp.exp(-0.5 * pre_act * pre_act) * 0.3989422804014327
    width = w.shape[1]
    out[:, pl.ds(pl.multiple_of(n * width, 128), width)] = (pre_act * cdf).astype(out.dtype)
    slope[...] = (cdf + pre_act * density).astype(slope.dtype)


def down_body(info, own, sib, w, slope, out, rows, *, hidden, chips):
    n = pl.program_id(0)

    @pl.when(n == 0)
    def _():
        load_rows(own, sib, rows)
        if out.shape[1] > hidden:
            put_partner_columns(info, rows, out, hidden, chips)

    act_grad = jnp.dot(rows[...], w[...], preferred_element_type=F32)
    width = w.shape[1]
    out[:, pl.ds(pl.multiple_of(n * width, 128), width)] = (act_grad * slope[...]).astype(out.dtype)


def columns_body(info, own, sib, out, rows, *, chips):
    load_rows(own, sib, rows)
    put_partner_columns(info, rows, out, 0, chips)


def partner_columns(own, sib, info, chips):
    half, d = own.shape
    spec = pl.BlockSpec((half, d), lambda n, i: (0, 0))
    return pl.pallas_call(
        functools.partial(columns_body, chips=chips),
        out_shape=jax.ShapeDtypeStruct((2 * half, d // 2), BF16),
        grid_spec=pltpu.PrefetchScalarGridSpec(
            num_scalar_prefetch=1,
            grid=(1,),
            in_specs=[spec, spec],
            out_specs=pl.BlockSpec((2 * half, d // 2), lambda n, i: (0, 0)),
            scratch_shapes=[pltpu.VMEM((2 * half, d), BF16)],
        ),
        compiler_params=pltpu.CompilerParams(vmem_limit_bytes=VMEM_LIMIT),
        cost_estimate=SHORT,
    )(info, own, sib)


def forward(own, sib, w, info, chips, slope=None, with_columns=True):
    half, d = own.shape
    hidden = w.shape[1] // 2
    width = block_of(hidden, 768)
    steps = hidden // width
    total = hidden + (d // 2 if with_columns else 0)
    out_shape = jax.ShapeDtypeStruct((2 * half, total), BF16)
    out_specs = pl.BlockSpec((2 * half, total), lambda n, i: (0, 0))
    slope_spec = pl.BlockSpec((2 * half, width), lambda n, i: (0, n))
    rows_spec = pl.BlockSpec((half, d), lambda n, i: (0, 0))
    w_spec = pl.BlockSpec((d, width), lambda n, i: (0, (i[0] & 1) * steps + n))
    in_specs = [rows_spec, rows_spec, w_spec]
    operands = [own, sib, w]
    if slope is None:
        body = up_body
        out_shape = (out_shape, jax.ShapeDtypeStruct((2 * half, hidden), BF16))
        out_specs = (out_specs, slope_spec)
    else:
        body = down_body
        in_specs.append(slope_spec)
        operands.append(slope)
    return pl.pallas_call(
        functools.partial(body, hidden=hidden, chips=chips),
        out_shape=out_shape,
        grid_spec=pltpu.PrefetchScalarGridSpec(
            num_scalar_prefetch=1,
            grid=(steps,),
            in_specs=in_specs,
            out_specs=out_specs,
            scratch_shapes=[pltpu.VMEM((2 * half, d), BF16)],
        ),
        compiler_params=pltpu.CompilerParams(vmem_limit_bytes=VMEM_LIMIT),
        cost_estimate=SHORT,
    )(info, *operands)


def input_body(info, pre, w, own, sib):
    value = lax.dot_general(pre[...], w[...], (((1,), (1,)), ((), ())), preferred_element_type=F32)
    half = own.shape[0]
    own[...] = value[:half].astype(own.dtype)
    sib[...] = value[half:].astype(sib.dtype)


def input_part(pre, w, info):
    rows = pre.shape[0]
    d, hidden = w.shape[0], w.shape[1] // 2
    width = block_of(d, 1536)
    shape = jax.ShapeDtypeStruct((rows // 2, d), BF16)
    spec = pl.BlockSpec((rows // 2, width), lambda n, i: (0, n))
    return pl.pallas_call(
        input_body,
        out_shape=(shape, shape),
        grid_spec=pltpu.PrefetchScalarGridSpec(
            num_scalar_prefetch=1,
            grid=(d // width,),
            in_specs=[
                pl.BlockSpec((rows, hidden), lambda n, i: (0, 0)),
                pl.BlockSpec((width, hidden), lambda n, i: (n, i[0] & 1)),
            ],
            out_specs=(spec, spec),
        ),
        compiler_params=pltpu.CompilerParams(vmem_limit_bytes=VMEM_LIMIT),
        cost_estimate=SHORT,
    )(info, pre, w)


def weight_body(at, *refs, begins, width, block):
    slots = len(begins)
    ins, outs, (left, right, total, left_sems, right_sems) = refs[:5 * slots], refs[5 * slots:-5], refs[-5:]
    half, hidden = ins[0].shape[0], right.shape[1]
    copies = []
    for s in range(slots):
        own, sib, there, mine, theirs = ins[5 * s:5 * s + 5]
        first = 4 * s * half
        for k, (rows, column, to, size) in enumerate((
            (own, at[0] * width, first, half),
            (sib, at[0] * width, first + half, half),
            (there, begins[s] + at[1] * width, first + 2 * half, 2 * half),
        )):
            source = rows.at[:, pl.ds(pl.multiple_of(column, 128), width)]
            copies.append(pltpu.make_async_copy(source, left.at[pl.ds(to, size)], left_sems.at[3 * s + k]))
        for k, hidden_side in enumerate((mine, theirs)):
            source = hidden_side.at[:, pl.ds(0, hidden)]
            to = right.at[pl.ds(first + 2 * k * half, 2 * half)]
            copies.append(pltpu.make_async_copy(source, to, right_sems.at[2 * s + k]))
    for copy in copies:
        copy.start()
    middle = slots // 2
    dims = (((0,), (0,)), ((), ()))
    early = 4 * middle * half
    span = width // 2
    is_first = at[2] == 0

    def by_columns(body):
        def step(n, carry):
            body(pl.ds(pl.multiple_of(n * block, 128), block))
            return carry

        lax.fori_loop(0, hidden // block, step, 0)

    def first_rows(cut):
        total[:, cut] = lax.dot_general(left[:early], right[:early, cut], dims, preferred_element_type=F32)

    def last_rows(cut):
        value = total[:, cut] + lax.dot_general(left[early:], right[early:, cut], dims, preferred_element_type=F32)
        if len(outs) == 1:
            outs[0][:, cut] = value.astype(outs[0].dtype)
        else:
            low, high = value[:span], value[span:]
            outs[0][:, cut] = jnp.where(is_first, low, high).astype(outs[0].dtype)
            outs[1][:, cut] = jnp.where(is_first, high, low).astype(outs[1].dtype)

    for copy in copies[:5 * middle]:
        copy.wait()
    by_columns(first_rows)
    for copy in copies[5 * middle:]:
        copy.wait()
    by_columns(last_rows)


def weight_part(rows, there_rows, rights, own_at, there_at, core, width, hidden, split):
    slots, size = len(rows), 2 * rows[0][0].shape[0]
    at = jnp.stack([own_at, there_at, core]).astype(jnp.int32)
    block = block_of(hidden, 512)
    operands = []
    for (own, sib), (there, _), (mine, theirs) in zip(rows, there_rows, rights):
        operands += [own, sib, there, mine, theirs]
    pieces = 2 if split else 1
    shape = jax.ShapeDtypeStruct((width // pieces, hidden), BF16)
    spec = pl.BlockSpec((width // pieces, hidden), lambda n, a: (0, 0))
    return pl.pallas_call(
        functools.partial(weight_body, begins=[begin for _, begin in there_rows], width=width, block=block),
        out_shape=(shape,) * pieces,
        grid_spec=pltpu.PrefetchScalarGridSpec(
            num_scalar_prefetch=1,
            grid=(1,),
            in_specs=[pl.BlockSpec(memory_space=pl.ANY)] * len(operands),
            out_specs=(spec,) * pieces,
            scratch_shapes=[
                pltpu.VMEM((2 * slots * size, width), BF16),
                pltpu.VMEM((2 * slots * size, hidden), BF16),
                pltpu.VMEM((width, hidden), F32),
                pltpu.SemaphoreType.DMA((3 * slots,)),
                pltpu.SemaphoreType.DMA((2 * slots,)),
            ],
        ),
        compiler_params=pltpu.CompilerParams(vmem_limit_bytes=VMEM_LIMIT),
        cost_estimate=SHORT,
    )(at, *operands)


def add(*values):
    return sum(v.astype(F32) for v in values).astype(BF16)


def local(x_rows, g_rows, w_up, w_down_t, block_count, patches):
    dp, tensor = lax.axis_size("dp"), lax.axis_size("tensor")
    chips = dp // 2
    me, plane = lax.axis_index("dp"), lax.axis_index("tensor")
    chip, core = me >> 1, me & 1
    info = jnp.stack([me, plane]).astype(jnp.int32)
    here, d = x_rows.shape[1:]
    hidden = w_up.shape[1] // 2
    ring = [(i, (i + 1) % tensor) for i in range(tensor)]
    to_sibling = [(i, i ^ 1) for i in range(dp)]
    to_pool = chip_perm(dp, lambda c: 1 << c)
    last = []

    def after(*values):
        out = lax.optimization_barrier((*values, *last))[:len(values)]
        return out if len(out) > 1 else out[0]

    def done(value):
        last[:] = [value]
        return value

    def onward(piece):
        return lax.ppermute(piece, "tensor", ring)

    def sibling(piece):
        return lax.ppermute(piece, "dp", to_sibling)

    def pooled(piece):
        return lax.ppermute(piece, "dp", to_pool)

    def exchange(rows):
        return lax.all_to_all(rows, "dp", split_axis=0, concat_axis=0, tiled=True)

    def chosen(arrived):
        return done(select(after(arrived), info, block_count, patches)).reshape(OWNB * here, d)

    def arrive(own, sib, ahead, further=True):
        piece = after(ahead)
        own.append(piece)
        sib.append(sibling(piece))
        return onward(piece) if further else None

    x_own, x_sib, x_there = [], [], []
    g_own, g_sib, g_there = [], [], []
    act, slope, pre, shares, pools = [], [], [], [], {}

    def settle(*names):
        last.extend(pools[name] for name in names if name in pools)

    def up(s):
        mine, slope_s = forward(*after(x_own[s], x_sib[s]), w_up, info, chips)
        theirs = pools["x", s] = pooled(done(mine))
        x_there.append((theirs, hidden))
        slope.append(slope_s)
        act.append((mine, theirs))

    def down(s, with_columns=True):
        mine = forward(*after(g_own[s], g_sib[s]), w_down_t, info, chips, slope[s], with_columns)
        theirs = pools["g", s] = pooled(done(mine))
        if with_columns:
            g_there.append((theirs, hidden))
        pre.append((mine, theirs))

    def share(s):
        own, sib = input_part(after(pre[s][0]), w_up, info)
        pools["share", s] = sibling(done(sib))
        shares.append((own, pools["share", s]))

    send_x = done(pack(x_rows, info, block_count, dp))
    arrived_x = exchange(send_x)
    send_g = done(pack(after(g_rows), info, block_count, dp))
    arrived_g = exchange(lax.optimization_barrier((send_g, arrived_x))[0])
    x_own.append(chosen(arrived_x))
    x_sib.append(sibling(x_own[0]))
    x_ahead = onward(x_own[0])
    up(0)
    end = tensor - 1
    for s in range(1, tensor):
        x_ahead = arrive(x_own, x_sib, x_ahead, s < end)
        if s == end:
            g_ahead = onward(after(g_own[0]))
        settle(("x", s - 2))
        up(s)
        if s == 1:
            g_own.append(chosen(arrived_g))
            g_sib.append(sibling(g_own[0]))
        if s == 2:
            settle(("x", 1))
            down(0)
    settle(("x", end - 1))
    share(0)
    for s in range(1, end):
        g_ahead = arrive(g_own, g_sib, g_ahead)
        settle(("share", s - 1), ("x", end) if s > 1 else None, ("g", s - 2))
        down(s)
        settle(("g", 0))
        share(s)

    settle(("g", end - 2))
    first_share = done(add(*after(*shares[1])))
    arrive(g_own, g_sib, g_ahead, False)
    running = onward(lax.optimization_barrier((first_share, g_own[end]))[0])
    columns = done(partner_columns(*after(g_own[end], g_sib[end]), info, chips))
    pools["columns"] = pooled(columns)
    g_there.append((pools["columns"], 0))
    settle(("share", end - 1))
    down(end, False)
    settle(("g", end - 1))
    share(end)

    span = d // dp
    near, mine_j = pool_bit(chip, core), other_bits(chip, core)

    def part(r, rows, there, rights, split):
        j = mine_j ^ r
        rows = [after(*rows[0]), *rows[1:]]
        parts = weight_part(
            rows, there, rights, chip_with(j, near, core), j, core, 2 * span, hidden, split
        )
        done(parts[0])
        return list(parts)

    def halves(r, rows, there, rights, split):
        if span % 128:
            return part(r, rows, there, rights, split)
        j = mine_j ^ r
        at = chip_with(j, near, core)
        parts = []
        for which in (core, 1 - core):
            rows = [after(*rows[0]), *rows[1:]]
            parts += weight_part(rows, there, rights, 2 * at + which, 2 * j + which, core, span, hidden, False)
            done(parts[-1])
        return parts

    bits = (chips // 2).bit_length() - 1

    def pass_on(parts):
        for k in reversed(range(1, bits)):
            perm = chip_perm(dp, lambda c: 2 << k)
            for r in range(1 << k, 2 << k):
                sent = [lax.ppermute(p, "dp", perm) for p in parts[r]]
                kept = parts.get(r ^ (1 << k))
                parts[r ^ (1 << k)] = [add(*both) for both in zip(kept, sent)] if kept else sent
        flip = lambda c: 2 >> c
        return [lax.ppermute(p, "dp", chip_perm(dp, flip, h == 1)) for h, p in enumerate(parts[1])]

    def core_rows(value, which):
        return lax.dynamic_slice_in_dim(value, which * span, span, 0)

    def finished(kept, parts, sent):
        if 0 in parts:
            kept = [add(*both) for both in zip(kept, parts[0])]
        if len(kept) == 2:
            mine = add(after(kept[0]), sent[0])
            other = add(sibling(kept[1]), sent[1])
        else:
            other = sibling(add(core_rows(kept[0], 1 - core), core_rows(sent[0], 1 - core)))
            mine = add(core_rows(after(kept[0]), core), core_rows(sent[0], core))
        return done(jnp.where(
            core == 0, jnp.concatenate([mine, other], axis=1), jnp.concatenate([other, mine], axis=1)
        ))

    down_sum = (list(zip(g_own, g_sib)), g_there, act, True)
    up_sum = (list(zip(x_own, x_sib)), x_there, pre, True)
    away = list(reversed(range(1, chips // 2)))
    settle("columns")
    last.append(running)
    down_parts = {r: halves(r, *down_sum) for r in away}
    down_sent = pass_on(down_parts)
    for s in range(2, end):
        running = onward(done(add(*after(*shares[s]), running)))
    settle(("g", end))
    up_parts = {r: part(r, *up_sum) for r in away}
    up_sent = pass_on(up_parts)
    down_kept = part(0, *down_sum)
    last.append(down_sent[0])
    running = onward(done(add(*after(*shares[end]), running)))
    last.append(down_sent[1])
    up_kept = part(0, *up_sum)
    down_grad = finished(down_kept, down_parts, down_sent)
    up_grad = finished(up_kept, up_parts, up_sent)
    input_grad = done(add(*after(*shares[0]), running)).reshape(OWNB, here, d)
    return input_grad, up_grad, down_grad


def solution(mesh):
    placed = (
        P("dp", "tensor", None),
        P("dp", "tensor", None),
        P(None, "tensor"),
        P(None, "tensor"),
        P(),
        P(),
    )
    return jax.shard_map(
        local,
        mesh=mesh,
        in_specs=placed,
        out_specs=(P("dp", "tensor", None), P("dp", "tensor"), P("dp", "tensor")),
        check_vma=False,
    )
```

```python
import functools

import jax
import jax.numpy as jnp
from jax import lax
from jax.experimental import pallas as pl
from jax.experimental.pallas import tpu as pltpu
from jax.sharding import PartitionSpec as P

OWNB = 4
BF16 = jnp.bfloat16
F32 = jnp.float32
VMEM_LIMIT = 64 * 1024 * 1024
SHORT = pl.CostEstimate(flops=1, bytes_accessed=1, transcendentals=0)


def chip_with(j, v, core):
    return jnp.where(core == 0, 2 * j + v, ((j >> 1) << 2) + 2 * v + (j & 1))


def pool_bit(chip, core):
    return jnp.where(core == 0, chip & 1, (chip >> 1) & 1)


def other_bits(chip, core):
    return jnp.where(core == 0, chip >> 1, ((chip >> 2) << 1) + (chip & 1))


def chip_perm(dp, flip, cross=False):
    return [(i, 2 * ((i >> 1) ^ flip(i & 1)) + ((i & 1) ^ int(cross))) for i in range(dp)]


def start_of(count, source, dp):
    total = jnp.int32(0)
    for j in range(dp):
        total = total + jnp.where(source > j, count[j], 0)
    return total


def source_of(count, number, dp):
    end, source = jnp.int32(0), jnp.int32(0)
    for j in range(dp):
        end = end + count[j]
        source = source + jnp.where(end <= number, 1, 0)
    return source


def run(copies):
    for copy in copies:
        copy.start()
    for copy in copies:
        copy.wait()


def pack_body(info, count, rows, out, sems):
    dp, blocks = out.shape[0], rows.shape[0]
    start = start_of(count, info[0], dp)
    copies = []
    for k in range(dp):
        block = jnp.minimum(lax.rem(k + OWNB * dp - start, dp), blocks - 1)
        copies.append(pltpu.make_async_copy(rows.at[block], out.at[k], sems.at[k]))
    run(copies)


def pack(rows, info, count, dp):
    _, here, d = rows.shape
    return pl.pallas_call(
        pack_body,
        out_shape=jax.ShapeDtypeStruct((dp, here, d), BF16),
        grid_spec=pltpu.PrefetchScalarGridSpec(
            num_scalar_prefetch=2,
            grid=(1,),
            in_specs=[pl.BlockSpec(memory_space=pl.ANY)],
            out_specs=pl.BlockSpec((dp, here, d), lambda n, i, c: (0, 0, 0)),
            scratch_shapes=[pltpu.SemaphoreType.DMA((dp,))],
        ),
        compiler_params=pltpu.CompilerParams(vmem_limit_bytes=VMEM_LIMIT),
        cost_estimate=SHORT,
    )(info, count, rows)


def select_body(info, count, patches, arrived, out, sems):
    dp, here = arrived.shape[0], out.shape[1]
    copies, filled = [], []
    for m in range(OWNB):
        number = info[0] + dp * m
        source = source_of(count, number, dp)
        filled.append(patches[source, number - start_of(count, source, dp)])
        copies.append(pltpu.make_async_copy(arrived.at[source], out.at[m], sems.at[m]))
    run(copies)
    row = lax.broadcasted_iota(jnp.int32, out.shape[1:], 0) + info[1] * here
    for m in range(OWNB):
        out[m] = jnp.where(row < filled[m], out[m].astype(F32), 0.0).astype(out.dtype)


def select(arrived, info, count, patches):
    _, here, d = arrived.shape
    return pl.pallas_call(
        select_body,
        out_shape=jax.ShapeDtypeStruct((OWNB, here, d), BF16),
        grid_spec=pltpu.PrefetchScalarGridSpec(
            num_scalar_prefetch=3,
            grid=(1,),
            in_specs=[pl.BlockSpec(memory_space=pl.ANY)],
            out_specs=pl.BlockSpec((OWNB, here, d), lambda n, i, c, p: (0, 0, 0)),
            scratch_shapes=[pltpu.SemaphoreType.DMA((OWNB,))],
        ),
        compiler_params=pltpu.CompilerParams(vmem_limit_bytes=VMEM_LIMIT),
        cost_estimate=SHORT,
    )(info, count, patches, arrived)


def block_of(size, most):
    for width in range(most, 0, -128):
        if size % width == 0:
            return width
    return size


def load_rows(own, sib, rows):
    half = own.shape[0]
    rows[:half] = own[...]
    rows[half:] = sib[...]


def put_partner_columns(info, rows, out, hidden, chips):
    core, chip = info[0] & 1, info[0] >> 1
    width = rows.shape[1] // chips
    away = 1 - pool_bit(chip, core)
    for j in range(chips // 2):
        at = pl.multiple_of(chip_with(j, away, core) * width, 128)
        out[:, hidden + j * width:hidden + (j + 1) * width] = rows[:, pl.ds(at, width)]


def up_body(info, own, sib, w, out, slope, rows, *, hidden, chips):
    n = pl.program_id(0)

    @pl.when(n == 0)
    def _():
        load_rows(own, sib, rows)
        put_partner_columns(info, rows, out, hidden, chips)

    pre_act = jnp.dot(rows[...], w[...], preferred_element_type=F32)
    cdf = 0.5 * (1.0 + lax.erf(pre_act * 0.7071067811865476))
    density = jnp.exp(-0.5 * pre_act * pre_act) * 0.3989422804014327
    width = w.shape[1]
    out[:, pl.ds(pl.multiple_of(n * width, 128), width)] = (pre_act * cdf).astype(out.dtype)
    slope[...] = (cdf + pre_act * density).astype(slope.dtype)


def down_body(info, own, sib, w, slope, out, rows, *, hidden, chips):
    n = pl.program_id(0)

    @pl.when(n == 0)
    def _():
        load_rows(own, sib, rows)
        if out.shape[1] > hidden:
            put_partner_columns(info, rows, out, hidden, chips)

    act_grad = jnp.dot(rows[...], w[...], preferred_element_type=F32)
    width = w.shape[1]
    out[:, pl.ds(pl.multiple_of(n * width, 128), width)] = (act_grad * slope[...]).astype(out.dtype)


def columns_body(info, own, sib, out, rows, *, chips):
    load_rows(own, sib, rows)
    put_partner_columns(info, rows, out, 0, chips)


def partner_columns(own, sib, info, chips):
    half, d = own.shape
    spec = pl.BlockSpec((half, d), lambda n, i: (0, 0))
    return pl.pallas_call(
        functools.partial(columns_body, chips=chips),
        out_shape=jax.ShapeDtypeStruct((2 * half, d // 2), BF16),
        grid_spec=pltpu.PrefetchScalarGridSpec(
            num_scalar_prefetch=1,
            grid=(1,),
            in_specs=[spec, spec],
            out_specs=pl.BlockSpec((2 * half, d // 2), lambda n, i: (0, 0)),
            scratch_shapes=[pltpu.VMEM((2 * half, d), BF16)],
        ),
        compiler_params=pltpu.CompilerParams(vmem_limit_bytes=VMEM_LIMIT),
        cost_estimate=SHORT,
    )(info, own, sib)


def forward(own, sib, w, info, chips, slope=None, with_columns=True):
    half, d = own.shape
    hidden = w.shape[1] // 2
    width = block_of(hidden, 768)
    steps = hidden // width
    total = hidden + (d // 2 if with_columns else 0)
    out_shape = jax.ShapeDtypeStruct((2 * half, total), BF16)
    out_specs = pl.BlockSpec((2 * half, total), lambda n, i: (0, 0))
    slope_spec = pl.BlockSpec((2 * half, width), lambda n, i: (0, n))
    rows_spec = pl.BlockSpec((half, d), lambda n, i: (0, 0))
    w_spec = pl.BlockSpec((d, width), lambda n, i: (0, (i[0] & 1) * steps + n))
    in_specs = [rows_spec, rows_spec, w_spec]
    operands = [own, sib, w]
    if slope is None:
        body = up_body
        out_shape = (out_shape, jax.ShapeDtypeStruct((2 * half, hidden), BF16))
        out_specs = (out_specs, slope_spec)
    else:
        body = down_body
        in_specs.append(slope_spec)
        operands.append(slope)
    return pl.pallas_call(
        functools.partial(body, hidden=hidden, chips=chips),
        out_shape=out_shape,
        grid_spec=pltpu.PrefetchScalarGridSpec(
            num_scalar_prefetch=1,
            grid=(steps,),
            in_specs=in_specs,
            out_specs=out_specs,
            scratch_shapes=[pltpu.VMEM((2 * half, d), BF16)],
        ),
        compiler_params=pltpu.CompilerParams(vmem_limit_bytes=VMEM_LIMIT),
        cost_estimate=SHORT,
    )(info, *operands)


def input_body(info, pre, w, own, sib):
    value = lax.dot_general(pre[...], w[...], (((1,), (1,)), ((), ())), preferred_element_type=F32)
    half = own.shape[0]
    own[...] = value[:half].astype(own.dtype)
    sib[...] = value[half:].astype(sib.dtype)


def input_part(pre, w, info):
    rows = pre.shape[0]
    d, hidden = w.shape[0], w.shape[1] // 2
    width = block_of(d, 1536)
    shape = jax.ShapeDtypeStruct((rows // 2, d), BF16)
    spec = pl.BlockSpec((rows // 2, width), lambda n, i: (0, n))
    return pl.pallas_call(
        input_body,
        out_shape=(shape, shape),
        grid_spec=pltpu.PrefetchScalarGridSpec(
            num_scalar_prefetch=1,
            grid=(d // width,),
            in_specs=[
                pl.BlockSpec((rows, hidden), lambda n, i: (0, 0)),
                pl.BlockSpec((width, hidden), lambda n, i: (n, i[0] & 1)),
            ],
            out_specs=(spec, spec),
        ),
        compiler_params=pltpu.CompilerParams(vmem_limit_bytes=VMEM_LIMIT),
        cost_estimate=SHORT,
    )(info, pre, w)


def weight_body(at, *refs, begins, width, block):
    slots = len(begins)
    ins, outs, (left, right, total, left_sems, right_sems) = refs[:5 * slots], refs[5 * slots:-5], refs[-5:]
    half, hidden = ins[0].shape[0], right.shape[1]
    copies = []
    for s in range(slots):
        own, sib, there, mine, theirs = ins[5 * s:5 * s + 5]
        first = 4 * s * half
        for k, (rows, column, to, size) in enumerate((
            (own, at[0] * width, first, half),
            (sib, at[0] * width, first + half, half),
            (there, begins[s] + at[1] * width, first + 2 * half, 2 * half),
        )):
            source = rows.at[:, pl.ds(pl.multiple_of(column, 128), width)]
            copies.append(pltpu.make_async_copy(source, left.at[pl.ds(to, size)], left_sems.at[3 * s + k]))
        for k, hidden_side in enumerate((mine, theirs)):
            source = hidden_side.at[:, pl.ds(0, hidden)]
            to = right.at[pl.ds(first + 2 * k * half, 2 * half)]
            copies.append(pltpu.make_async_copy(source, to, right_sems.at[2 * s + k]))
    for copy in copies:
        copy.start()
    middle = slots // 2
    dims = (((0,), (0,)), ((), ()))
    early = 4 * middle * half
    span = width // 2
    is_first = at[2] == 0

    def by_columns(body, unroll):
        def step(n, carry):
            body(pl.ds(pl.multiple_of(n * block, 128), block))
            return carry

        lax.fori_loop(0, hidden // block, step, 0, unroll=unroll)

    def first_rows(cut):
        total[:, cut] = lax.dot_general(left[:early], right[:early, cut], dims, preferred_element_type=F32)

    def last_rows(cut):
        value = total[:, cut] + lax.dot_general(left[early:], right[early:, cut], dims, preferred_element_type=F32)
        if len(outs) == 1:
            outs[0][:, cut] = value.astype(outs[0].dtype)
        else:
            low, high = value[:span], value[span:]
            outs[0][:, cut] = jnp.where(is_first, low, high).astype(outs[0].dtype)
            outs[1][:, cut] = jnp.where(is_first, high, low).astype(outs[1].dtype)

    for copy in copies[:5 * middle]:
        copy.wait()
    by_columns(first_rows, True)
    for copy in copies[5 * middle:]:
        copy.wait()
    by_columns(last_rows, False)


def weight_part(rows, there_rows, rights, own_at, there_at, core, width, hidden, split):
    slots, size = len(rows), 2 * rows[0][0].shape[0]
    at = jnp.stack([own_at, there_at, core]).astype(jnp.int32)
    block = block_of(hidden, 512)
    operands = []
    for (own, sib), (there, _), (mine, theirs) in zip(rows, there_rows, rights):
        operands += [own, sib, there, mine, theirs]
    pieces = 2 if split else 1
    shape = jax.ShapeDtypeStruct((width // pieces, hidden), BF16)
    spec = pl.BlockSpec((width // pieces, hidden), lambda n, a: (0, 0))
    return pl.pallas_call(
        functools.partial(weight_body, begins=[begin for _, begin in there_rows], width=width, block=block),
        out_shape=(shape,) * pieces,
        grid_spec=pltpu.PrefetchScalarGridSpec(
            num_scalar_prefetch=1,
            grid=(1,),
            in_specs=[pl.BlockSpec(memory_space=pl.ANY)] * len(operands),
            out_specs=(spec,) * pieces,
            scratch_shapes=[
                pltpu.VMEM((2 * slots * size, width), BF16),
                pltpu.VMEM((2 * slots * size, hidden), BF16),
                pltpu.VMEM((width, hidden), F32),
                pltpu.SemaphoreType.DMA((3 * slots,)),
                pltpu.SemaphoreType.DMA((2 * slots,)),
            ],
        ),
        compiler_params=pltpu.CompilerParams(vmem_limit_bytes=VMEM_LIMIT),
        cost_estimate=SHORT,
    )(at, *operands)


def add(*values):
    return sum(v.astype(F32) for v in values).astype(BF16)


def local(x_rows, g_rows, w_up, w_down_t, block_count, patches):
    dp, tensor = lax.axis_size("dp"), lax.axis_size("tensor")
    chips = dp // 2
    me, plane = lax.axis_index("dp"), lax.axis_index("tensor")
    chip, core = me >> 1, me & 1
    info = jnp.stack([me, plane]).astype(jnp.int32)
    here, d = x_rows.shape[1:]
    hidden = w_up.shape[1] // 2
    ring = [(i, (i + 1) % tensor) for i in range(tensor)]
    to_sibling = [(i, i ^ 1) for i in range(dp)]
    to_pool = chip_perm(dp, lambda c: 1 << c)
    last = []

    def after(*values):
        out = lax.optimization_barrier((*values, *last))[:len(values)]
        return out if len(out) > 1 else out[0]

    def done(value):
        last[:] = [value]
        return value

    def onward(piece):
        return lax.ppermute(piece, "tensor", ring)

    def sibling(piece):
        return lax.ppermute(piece, "dp", to_sibling)

    def pooled(piece):
        return lax.ppermute(piece, "dp", to_pool)

    def exchange(rows):
        return lax.all_to_all(rows, "dp", split_axis=0, concat_axis=0, tiled=True)

    def chosen(arrived):
        return done(select(after(arrived), info, block_count, patches)).reshape(OWNB * here, d)

    def arrive(own, sib, ahead, further=True):
        piece = after(ahead)
        own.append(piece)
        sib.append(sibling(piece))
        return onward(piece) if further else None

    x_own, x_sib, x_there = [], [], []
    g_own, g_sib, g_there = [], [], []
    act, slope, pre, shares, pools = [], [], [], [], {}

    def settle(*names):
        last.extend(pools[name] for name in names if name in pools)

    def up(s):
        mine, slope_s = forward(*after(x_own[s], x_sib[s]), w_up, info, chips)
        theirs = pools["x", s] = pooled(done(mine))
        x_there.append((theirs, hidden))
        slope.append(slope_s)
        act.append((mine, theirs))

    def down(s, with_columns=True):
        mine = forward(*after(g_own[s], g_sib[s]), w_down_t, info, chips, slope[s], with_columns)
        theirs = pools["g", s] = pooled(done(mine))
        if with_columns:
            g_there.append((theirs, hidden))
        pre.append((mine, theirs))

    def share(s):
        own, sib = input_part(after(pre[s][0]), w_up, info)
        pools["share", s] = sibling(done(sib))
        shares.append((own, pools["share", s]))

    send_x = done(pack(x_rows, info, block_count, dp))
    arrived_x = exchange(send_x)
    send_g = done(pack(after(g_rows), info, block_count, dp))
    arrived_g = exchange(lax.optimization_barrier((send_g, arrived_x))[0])
    x_own.append(chosen(arrived_x))
    x_sib.append(sibling(x_own[0]))
    x_ahead = onward(x_own[0])
    up(0)
    end = tensor - 1
    for s in range(1, tensor):
        x_ahead = arrive(x_own, x_sib, x_ahead, s < end)
        if s == end:
            g_ahead = onward(after(g_own[0]))
        settle(("x", s - 2))
        up(s)
        if s == 1:
            g_own.append(chosen(arrived_g))
            g_sib.append(sibling(g_own[0]))
        if s == 2:
            settle(("x", 1))
            down(0)
    settle(("x", end - 1))
    share(0)
    for s in range(1, end):
        g_ahead = arrive(g_own, g_sib, g_ahead)
        settle(("share", s - 1), ("x", end) if s > 1 else None, ("g", s - 2))
        down(s)
        settle(("g", 0))
        share(s)

    settle(("g", end - 2))
    first_share = done(add(*after(*shares[1])))
    arrive(g_own, g_sib, g_ahead, False)
    running = onward(lax.optimization_barrier((first_share, g_own[end]))[0])
    columns = done(partner_columns(*after(g_own[end], g_sib[end]), info, chips))
    pools["columns"] = pooled(columns)
    g_there.append((pools["columns"], 0))
    settle(("share", end - 1))
    down(end, False)
    settle(("g", end - 1))
    share(end)

    span = d // dp
    near, mine_j = pool_bit(chip, core), other_bits(chip, core)

    def part(r, rows, there, rights, split):
        j = mine_j ^ r
        rows = [after(*rows[0]), *rows[1:]]
        parts = weight_part(
            rows, there, rights, chip_with(j, near, core), j, core, 2 * span, hidden, split
        )
        done(parts[0])
        return list(parts)

    bits = (chips // 2).bit_length() - 1

    def pass_on(parts):
        for k in reversed(range(1, bits)):
            perm = chip_perm(dp, lambda c: 2 << k)
            for r in range(1 << k, 2 << k):
                sent = [lax.ppermute(p, "dp", perm) for p in parts[r]]
                kept = parts.get(r ^ (1 << k))
                parts[r ^ (1 << k)] = [add(*both) for both in zip(kept, sent)] if kept else sent
        flip = lambda c: 2 >> c
        return [lax.ppermute(p, "dp", chip_perm(dp, flip, h == 1)) for h, p in enumerate(parts[1])]

    def begun(kept, parts, sent):
        if 0 in parts:
            kept = [add(*both) for both in zip(kept, parts[0])]
        return done(add(after(kept[0]), sent[0])), sibling(kept[1])

    def finished(mine, sib, sent):
        other = add(after(sib), sent[1])
        return done(jnp.where(
            core == 0, jnp.concatenate([mine, other], axis=1), jnp.concatenate([other, mine], axis=1)
        ))

    down_sum = (list(zip(g_own, g_sib)), g_there, act, True)
    up_sum = (list(zip(x_own, x_sib)), x_there, pre, True)
    away = list(reversed(range(1, chips // 2)))
    settle("columns")
    last.append(running)
    down_parts = {r: part(r, *down_sum) for r in away}
    down_sent = pass_on(down_parts)
    for s in range(2, end):
        running = onward(done(add(*after(*shares[s]), running)))
    settle(("g", end))
    up_parts = {r: part(r, *up_sum) for r in away}
    up_sent = pass_on(up_parts)
    down_kept = part(0, *down_sum)
    running = onward(done(add(*after(*shares[end]), running)))
    last.extend(down_sent)
    up_kept = part(0, *up_sum)
    down_grad = finished(*begun(down_kept, down_parts, down_sent), down_sent)
    up_begun = begun(up_kept, up_parts, up_sent)
    input_grad = done(add(*after(*shares[0]), running)).reshape(OWNB, here, d)
    up_grad = finished(*up_begun, up_sent)
    return input_grad, up_grad, down_grad


def solution(mesh):
    placed = (
        P("dp", "tensor", None),
        P("dp", "tensor", None),
        P(None, "tensor"),
        P(None, "tensor"),
        P(),
        P(),
    )
    return jax.shard_map(
        local,
        mesh=mesh,
        in_specs=placed,
        out_specs=(P("dp", "tensor", None), P("dp", "tensor"), P("dp", "tensor")),
        check_vma=False,
    )
```
